256 devices in a mesh: gx: 8 (over x, core), gy: 8 (over z), gz: 4 (over y).
Axes of the slice: x: 4, y: 4, z: 8, core: 2. Of those that a mesh axis runs over, the one named last changes fastest.
Arguments:
- density_level: int32 [32, 128, 512], P('gx', 'gy', 'gz'), may hold values from 0 to 255
- support_mask: int32 [32, 128, 512], P('gx', 'gy', 'gz'), may hold values 0 or 1
- load_mask: int32 [32, 128, 512], P('gx', 'gy', 'gz'), may hold values 0 or 1
- load_vector: float32 [3, 32, 128, 512], P(None, 'gx', 'gy', 'gz'), may hold values from -40 to 40
Outputs:
- displacement: float32 [3, 32, 128, 512], P(None, 'gx', 'gy', 'gz')
The draws below stay inside these ranges and needn't reach their ends.
All inputs are finite; a program needn't handle non-finite values. No bound on the sum of `support_mask` or of `load_mask` on one device may be relied on, other than what follows from the above.
Results may differ from the reference program's by a relative error of at most 0.0003.
Values sent between devices are 32-bit elements; how exact they have to be, the bound alone decides.
No kernel may reach another device: no remote copies, remote signals or barrier semaphores. Data moves between devices by JAX's collectives and lax.ppermute only.
A program may use at most 64 MiB of HBM per device.

```python
import jax
import jax.numpy as jnp
import numpy as np
from jax import lax

LEVELS = 3
DEGREE = 3
NX = 32
NY = 128
NZ = 512


def draw_load_vector(key, part):
    key = jax.random.fold_in(key, 11)
    coord_x = jnp.arange(NX, dtype=jnp.float32) / NX
    coord_y = jnp.arange(NY, dtype=jnp.float32) / NY
    coord_z = jnp.arange(NZ, dtype=jnp.float32) / NZ
    blend = (coord_x[:, None, None] + coord_y[None, :, None] + coord_z[None, None, :]) / 3.0
    envelope = jnp.exp(jnp.log(10.0) * blend)
    rough = jnp.clip(jax.random.normal(key, (3, NX, NY, NZ), jnp.float32), -4.0, 4.0)
    return envelope * rough


def with_ends(values, key, smallest, high):
    shape = values.shape
    place = [jax.random.randint(jax.random.fold_in(key, axis), (), 0, shape[axis]) for axis in range(len(shape))]
    values = values.at[tuple(place)].set(smallest)
    longest = shape.index(max(shape))
    place[longest] = (place[longest] + 1) % shape[longest]
    return values.at[tuple(place)].set(high)


def setup_inputs(seed: int = 0) -> dict:
    arg_keys = jax.random.split(jax.random.key(seed), 5)
    density_level = with_ends(jax.random.randint(arg_keys[0], (NX, NY, NZ), 0, 256), jax.random.fold_in(arg_keys[0], 1), 0, 255).astype(jnp.int32)
    support_mask = with_ends((jax.random.randint(arg_keys[1], (NX, NY, NZ), 0, 8) < 1).astype(jnp.int32), jax.random.fold_in(arg_keys[1], 1), 0, 1)
    load_mask = with_ends((jax.random.randint(arg_keys[2], (NX, NY, NZ), 0, 2) < 1).astype(jnp.int32), jax.random.fold_in(arg_keys[2], 1), 0, 1)
    load_vector = draw_load_vector(jax.random.fold_in(arg_keys[4], 71), 0)
    return {"density_level": density_level, "support_mask": support_mask, "load_mask": load_mask, "load_vector": load_vector}


young_floor = 1e-3
poisson = 0.3
headroom = 1.5
floor_share = 0.3
corner_list = [(a, b, e) for a in (0, 1) for b in (0, 1) for e in (0, 1)]


def element_matrix():
    lame_first = poisson / ((1.0 + poisson) * (1.0 - 2.0 * poisson))
    shear_mod = 1.0 / (2.0 * (1.0 + poisson))
    elastic = np.zeros((6, 6))
    elastic[:3, :3] = lame_first
    for i in range(3):
        elastic[i, i] = lame_first + 2.0 * shear_mod
        elastic[i + 3, i + 3] = shear_mod
    points = [(1.0 - 3.0 ** -0.5) / 2.0, (1.0 + 3.0 ** -0.5) / 2.0]
    stiffness = np.zeros((24, 24))
    for point_x in points:
        for point_y in points:
            for point_z in points:
                strain = np.zeros((6, 24))
                for n, (a, b, e) in enumerate(corner_list):
                    shape_x = point_x if a else 1.0 - point_x
                    shape_y = point_y if b else 1.0 - point_y
                    shape_z = point_z if e else 1.0 - point_z
                    slope_x = 1.0 if a else -1.0
                    slope_y = 1.0 if b else -1.0
                    slope_z = 1.0 if e else -1.0
                    grad_x = slope_x * shape_y * shape_z
                    grad_y = shape_x * slope_y * shape_z
                    grad_z = shape_x * shape_y * slope_z
                    strain[0, n] = grad_x
                    strain[1, 8 + n] = grad_y
                    strain[2, 16 + n] = grad_z
                    strain[3, n] = grad_y
                    strain[3, 8 + n] = grad_x
                    strain[4, 8 + n] = grad_z
                    strain[4, 16 + n] = grad_y
                    strain[5, n] = grad_z
                    strain[5, 16 + n] = grad_x
                stiffness = stiffness + 0.125 * strain.T @ elastic @ strain
    return stiffness


def diagonal_entries():
    stiffness = element_matrix()
    return np.array([stiffness[i, i] for i in range(24)])


def young_of(density_level):
    scaled = density_level.astype(jnp.float32) / 255.0
    return young_floor + (1.0 - young_floor) * scaled * scaled * scaled


def coarsen(young, free_mask):
    size_x, size_y, size_z = young.shape
    young_next = young.reshape(size_x // 2, 2, size_y // 2, 2, size_z // 2, 2).mean(axis=(1, 3, 5))
    return young_next, free_mask[::2, ::2, ::2]


def roll_level(young, free_mask, scale):
    matrix = jnp.asarray(element_matrix(), jnp.float32)
    diag_vals = diagonal_entries()
    young_s = young * scale
    diag_rows = []
    for component in range(3):
        summed = jnp.zeros(young.shape, jnp.float32)
        for n, (a, b, e) in enumerate(corner_list):
            summed = summed + jnp.roll(young_s * float(diag_vals[component * 8 + n]), (a, b, e), axis=(0, 1, 2))
        diag_rows.append(summed)
    diagonal = free_mask * jnp.stack(diag_rows) + (1.0 - free_mask)

    def apply_op(vector):
        masked = vector * free_mask
        corner_stack = jnp.stack([jnp.roll(masked[component], (-a, -b, -e), axis=(0, 1, 2)) for component in range(3) for (a, b, e) in corner_list])
        forces = jnp.dot(matrix, corner_stack.reshape(24, -1), precision=lax.Precision.HIGHEST, preferred_element_type=jnp.float32)
        forces = forces.reshape(corner_stack.shape) * young_s
        rows_out = []
        for component in range(3):
            summed = jnp.zeros(young.shape, jnp.float32)
            for n, (a, b, e) in enumerate(corner_list):
                summed = summed + jnp.roll(forces[component * 8 + n], (a, b, e), axis=(0, 1, 2))
            rows_out.append(summed)
        return free_mask * jnp.stack(rows_out) + (1.0 - free_mask) * vector

    return apply_op, diagonal


def restrict(values):
    for which_dim in (1, 2, 3):
        center = lax.slice_in_dim(values, 0, values.shape[which_dim], 2, which_dim)
        odd_part = lax.slice_in_dim(values, 1, values.shape[which_dim], 2, which_dim)
        values = center + 0.5 * (jnp.roll(odd_part, 1, axis=which_dim) + odd_part)
    return values


def prolong(values):
    for which_dim in (1, 2, 3):
        odd_part = 0.5 * (values + jnp.roll(values, -1, axis=which_dim))
        paired = jnp.stack([values, odd_part], axis=which_dim + 1)
        new_shape = list(values.shape)
        new_shape[which_dim] = 2 * values.shape[which_dim]
        values = paired.reshape(new_shape)
    return values


def rayleigh(operator, probe):
    apply_op, diagonal = operator
    scaled = probe / diagonal
    return jnp.sum(scaled * apply_op(scaled)) / jnp.sum(scaled * (diagonal * scaled))


def chebyshev(operator, estimate, right_side, start, want_residual):
    apply_op, diagonal = operator
    top_end = headroom * estimate
    bottom_end = floor_share * top_end
    centre = 0.5 * (top_end + bottom_end)
    half_width = 0.5 * (top_end - bottom_end)
    ratio_width = centre / half_width
    weight_old = 1.0 / ratio_width
    if start is None:
        residual = right_side
    else:
        residual = right_side - apply_op(start)
    step_dir = (residual / diagonal) / centre
    iterate = step_dir if start is None else start + step_dir
    for turn in range(DEGREE - 1):
        residual = residual - apply_op(step_dir)
        weight_new = 1.0 / (2.0 * ratio_width - weight_old)
        step_dir = weight_new * weight_old * step_dir + (2.0 * weight_new / half_width) * (residual / diagonal)
        iterate = iterate + step_dir
        weight_old = weight_new
    if want_residual:
        return iterate, residual - apply_op(step_dir)
    return iterate, None


def reference(density_level, support_mask, load_mask, load_vector):
    youngs = [young_of(density_level)]
    frees = [1.0 - support_mask.astype(jnp.float32)]
    for l in range(1, LEVELS):
        young_next, free_next = coarsen(youngs[-1], frees[-1])
        youngs.append(young_next)
        frees.append(free_next)
    operators = [roll_level(youngs[l], frees[l], 2.0 ** l) for l in range(LEVELS)]
    right_side = frees[0] * load_mask.astype(jnp.float32) * load_vector
    probe = right_side
    estimates = []
    for l in range(LEVELS):
        if l > 0:
            probe = frees[l] * restrict(probe)
        estimates.append(rayleigh(operators[l], probe))
    sides = [right_side]
    iterates = []
    for l in range(LEVELS - 1):
        iterate, residual = chebyshev(operators[l], estimates[l], sides[l], None, True)
        iterates.append(iterate)
        sides.append(frees[l + 1] * restrict(residual))
    coarse_x, unused = chebyshev(operators[-1], estimates[-1], sides[-1], None, False)
    for l in range(LEVELS - 2, -1, -1):
        start = iterates[l] + frees[l] * prolong(coarse_x)
        coarse_x, unused = chebyshev(operators[l], estimates[l], sides[l], start, False)
    return coarse_x
```

```python
import jax
import jax.numpy as jnp
import numpy as np
from jax import lax
from jax.experimental import pallas as pl
from jax.experimental.pallas import tpu as pltpu
from jax.sharding import PartitionSpec as P

f32 = jnp.float32
young_floor = 0.001
poisson = 0.3
headroom = 1.5
floor_share = 0.3
lam = poisson / ((1.0 + poisson) * (1.0 - 2.0 * poisson))
mu = 1.0 / (2.0 * (1.0 + poisson))
diag_entry = (lam + 2 * mu + 2 * mu) / 16 + (2 * (lam + 3 * mu) + 2 * mu) / 48 + (lam + 4 * mu) / 144
top_share = headroom
centre_share = 0.5 * headroom * (1.0 + floor_share)
half_share = 0.5 * headroom * (1.0 - floor_share)
VMEM_LIMIT = 56 * 1024 * 1024

NXE, NYE, NZE = 15, 32, 256
SS, SD, DS, DD = 0, 1, 2, 3


def shifted(values, amount, axis):
    return pltpu.roll(values, amount % values.shape[axis], axis=axis)


def modes(w):
    up = shifted(w, -1, 1)
    s = w + up
    d = up - w
    s_up = shifted(s, -1, 0)
    d_up = shifted(d, -1, 0)
    return s + s_up, d + d_up, s_up - s, d_up - d


def back_modes(g):
    zs = (g[SS] - g[DS]) + shifted(g[SS] + g[DS], 1, 0)
    zd = (g[SD] - g[DD]) + shifted(g[SD] + g[DD], 1, 0)
    return (zs - zd) + shifted(zs + zd, 1, 1)


def element_forces(t0, t1, e):
    u = {}
    for c in range(3):
        for m in range(4):
            u[c, "d", m] = t1[c][m] - t0[c][m]
            if m != SS:
                u[c, "s", m] = t1[c][m] + t0[c][m]
    f = {}
    e_a, e_b, e_c = e * (lam / 16), e * (2 * mu / 16), e * (mu / 16)
    e_d, e_e, e_f = e * (lam / 48), e * (3 * mu / 48), e * (mu / 48)
    e_g = e * ((lam + 4 * mu) / 144)
    normal = ((0, "d", SS), (1, "s", DS), (2, "s", SD))
    t = e_a * (u[normal[0]] + u[normal[1]] + u[normal[2]])
    for key in normal:
        f[key] = t + e_b * u[key]
    for one, two in (((0, "s", DS), (1, "d", SS)), ((1, "s", SD), (2, "s", DS)), ((0, "s", SD), (2, "d", SS))):
        f[one] = f[two] = e_c * (u[one] + u[two])
    for one, two in (((0, "d", DS), (2, "s", DD)), ((0, "d", SD), (1, "s", DD)), ((1, "d", DS), (2, "d", SD))):
        p = e_d * (u[one] + u[two])
        f[one] = p + e_e * u[one]
        f[two] = p + e_e * u[two]
    triple = ((0, "s", DD), (1, "d", SD), (2, "d", DS))
    q = u[triple[0]] + u[triple[1]] + u[triple[2]]
    for key in triple:
        f[key] = e_f * (u[key] + q)
    for c in range(3):
        f[c, "d", DD] = e_g * u[c, "d", DD]
    return u, f


def apply_planes(t_ref, c_ref, g_ref, lo, n, load_w, load_e, emit):
    rows, lanes = t_ref.shape[-2:]

    def store(par, i):
        w = load_w(i)
        for c in range(3):
            for m, val in enumerate(modes(w[c])):
                t_ref[par, 4 * c + m] = val

    store((lo - 1) & 1, lo - 1)
    c_ref[...] = jnp.zeros(c_ref.shape, f32)

    def step(i, carry):
        par = i & 1
        store(1 - par, i + 1)
        for r in range(0, rows, 8):
            for l in range(0, lanes, 128):
                at = (slice(r, r + 8), slice(l, l + 128))
                t0 = [[t_ref[(par, 4 * c + m) + at] for m in range(4)] for c in range(3)]
                t1 = [[t_ref[(1 - par, 4 * c + m) + at] for m in range(4)] for c in range(3)]
                u, f = element_forces(t0, t1, load_e(i, at))
                for c in range(3):
                    for m in range(4):
                        d = f[c, "d", m]
                        old = c_ref[(4 * c + m,) + at]
                        if m == SS:
                            g_ref[(4 * c + m,) + at] = old - d
                            c_ref[(4 * c + m,) + at] = d
                        else:
                            s = f[c, "s", m]
                            g_ref[(4 * c + m,) + at] = old + (s - d)
                            c_ref[(4 * c + m,) + at] = s + d

        @pl.when(i >= lo)
        def _():
            emit(i, [back_modes([g_ref[4 * c + m] for m in range(4)]) for c in range(3)])

        return carry

    lax.fori_loop(lo - 1, lo + n, step, 0)


def work_buffers(rows, lanes):
    return [
        pltpu.VMEM((2, 12, rows, lanes), f32),
        pltpu.VMEM((12, rows, lanes), f32),
        pltpu.VMEM((12, rows, lanes), f32),
    ]


def low_sum(a):
    a = a + shifted(a, 1, 1)
    return a + shifted(a, 1, 0)


def inverse_diagonal(e_sum, free, scale):
    return jnp.where(free > 0.5, 1.0 / (e_sum * (diag_entry * scale)), 1.0)


def matrix(shape, fun):
    r = lax.broadcasted_iota(jnp.int32, shape, 0)
    c = lax.broadcasted_iota(jnp.int32, shape, 1)
    return fun(r, c)


def dot(a, b):
    return jnp.dot(a, b, precision=lax.Precision.HIGHEST, preferred_element_type=f32)


def to_f(cond, val=1.0):
    return jnp.where(cond, f32(val), f32(0.0))


def restrict_rows(out, size, count=None):
    def fun(r, c):
        near = (c == 2 * r + 1) | (c == (2 * r - 1) % size)
        full = to_f(c == 2 * r) + to_f(near, 0.5)
        return full if count is None else jnp.where(r < count, full, 0.0)

    return matrix((out, size), fun)


def restrict_lanes(size, out, period, first=0, count=None):
    def fun(r, c):
        j = (c - first) % period
        near = (r == 2 * j + 1) | (r == (2 * j - 1) % size)
        full = to_f(r == 2 * j) + to_f(near, 0.5)
        return full if count is None else jnp.where((c >= first) & (c < first + count), full, 0.0)

    return matrix((size, out), fun)


def pick_rows(out, size, count=None):
    def fun(r, c):
        full = to_f(c == 2 * r)
        return full if count is None else jnp.where(r < count, full, 0.0)

    return matrix((out, size), fun)


def mean_rows(out, size, count=None):
    def fun(r, c):
        full = to_f((c == 2 * r) | (c == 2 * r + 1), 0.5)
        return full if count is None else jnp.where(r < count, full, 0.0)

    return matrix((out, size), fun)


def pick_lanes(size, out, period, first=0, count=None):
    def fun(r, c):
        full = to_f(r == 2 * ((c - first) % period))
        return full if count is None else jnp.where((c >= first) & (c < first + count), full, 0.0)

    return matrix((size, out), fun)


def mean_lanes(size, out, period, first=0, count=None):
    def fun(r, c):
        j = (c - first) % period
        full = to_f((r == 2 * j) | (r == 2 * j + 1), 0.5)
        return full if count is None else jnp.where((c >= first) & (c < first + count), full, 0.0)

    return matrix((size, out), fun)


def prolong_rows(out, size, first):
    def fun(r, c):
        base = r // 2 + first
        odd = r % 2
        return jnp.where(odd == 0, to_f(c == base), to_f((c == base) | (c == base + 1), 0.5))

    return matrix((out, size), fun)


def prolong_lanes(size, out, period):
    def fun(r, c):
        base = (c // 2) % period
        odd = c % 2
        return jnp.where(odd == 0, to_f(r == base), to_f((r == base) | (r == (base + 1) % period), 0.5))

    return matrix((size, out), fun)


def prepare_kernel(density, support, load, vector, own, low, high):
    scaled = density[...].astype(f32) / 255.0
    young = young_floor + (1.0 - young_floor) * scaled * scaled * scaled
    free = 1.0 - support[...].astype(f32)
    masked = free * load[...].astype(f32)
    rows = [young, free] + [masked * vector[c] for c in range(3)]
    for a, val in enumerate(rows):
        own[a] = val
        low[a] = val[0:1]
        high[a] = val[2:4]


def join_x_kernel(own, left, right, far_left, far_right, low, high):
    for out, rows in ((low, slice(0, 8)), (high, slice(8, 16))):
        for a in range(5):
            out[a, 0:2] = far_left[a, :, rows]
            out[a, 2:6] = left[a, :, rows]
            out[a, 6:10] = own[a, :, rows]
            out[a, 10:14] = right[a, :, rows]
            out[a, 14:15] = far_right[a, :, rows]


def lane_index(shape):
    return lax.broadcasted_iota(jnp.int32, shape, len(shape) - 1)


def pack_z_kernel(up, low, high, down, first, last):
    tiles = (up, low, high, down)
    lane = lane_index((8, 128))
    for a in range(5):
        for t in range(4):
            acc_first = jnp.zeros((8, 128), f32)
            acc_last = jnp.zeros((8, 128), f32)
            for g in range(NXE):
                val = tiles[t][a, g]
                inside = (lane >= 8 * g) & (lane < 8 * g + 8)
                acc_first = jnp.where(inside, shifted(val, 8 * g, 1), acc_first)
                acc_last = jnp.where(inside, shifted(val, 8 * g + 8, 1), acc_last)
            first[a, 8 * t : 8 * t + 8] = acc_first
            last[a, 8 * t : 8 * t + 8] = acc_last


def first_kernel(up, low, high, down, from_left, from_right, ext, dinv, w0, static, sums, c1, y1, f1, d1, tb, cb, gb):
    tiles = (up, low, high, down)
    lane = lane_index((8, 128))
    for a in range(5):
        for t in range(4):
            rows = slice(8 * t, 8 * t + 8)
            left = from_left[a, rows]
            right = from_right[a, rows]
            for g in range(NXE):
                ext[a, g, rows, 0:128] = tiles[t][a, g]
                halo = jnp.where(lane < 8, shifted(right, -8 * g, 1), 0.0)
                ext[a, g, rows, 128:256] = jnp.where(lane >= 120, shifted(left, 120 - 8 * g, 1), halo)

    def diag_step(i, old):
        new = low_sum(ext[0, i])
        dinv[i] = inverse_diagonal(new + old, ext[1, i], 1.0)
        return new

    lax.fori_loop(0, NXE, diag_step, jnp.zeros((NYE, NZE), f32))

    def load_w(i):
        scaled = dinv[i] * ext[1, i]
        return [ext[2 + c, i] * scaled for c in range(3)]

    def emit(i, g):
        free = ext[1, i]
        for c in range(3):
            w0[c, i] = jnp.where(free > 0.5, g[c], ext[2 + c, i] * dinv[i])

    apply_planes(tb, cb, gb, 2, 12, load_w, lambda i, at: ext[(0, i) + at], emit)

    own_rows, own_lanes = slice(8, 24), slice(0, 128)
    num = jnp.zeros((16, 128), f32)
    den = jnp.zeros((16, 128), f32)
    for i in range(6, 10):
        for c in range(3):
            b = ext[2 + c, i, own_rows, own_lanes]
            z = b * dinv[i, own_rows, own_lanes]
            num = num + z * w0[c, i, own_rows, own_lanes]
            den = den + z * b
    totals = [jnp.sum(num), jnp.sum(den)]

    ry, rz = restrict_rows(16, 32), restrict_lanes(256, 128, 128)
    py, pz = pick_rows(16, 32), pick_lanes(256, 128, 128)
    my, mz = mean_rows(16, 32), mean_lanes(256, 128, 128)
    for k in range(5):
        i = 2 * k + 4
        f1[k] = dot(dot(py, ext[1, i]), pz)
        for c in range(3):
            fine = ext[2 + c, i] + 0.5 * (ext[2 + c, i - 1] + ext[2 + c, i + 1])
            c1[c, k] = dot(dot(ry, fine), rz) * f1[k]
    for k in range(6):
        fine = 0.5 * (ext[0, 2 * k + 2] + ext[0, 2 * k + 3])
        y1[k] = dot(dot(my, fine), mz)

    def level_sums(nodes, planes, elements, frees, own, scale):
        rows_own, lanes_own, count = own
        shape = frees[0].shape
        r = lax.broadcasted_iota(jnp.int32, shape, 0)
        l = lax.broadcasted_iota(jnp.int32, shape, 1)
        mine = (r >= rows_own[0]) & (r < rows_own[1]) & (l < lanes_own)
        num = jnp.zeros(shape, f32)
        den = jnp.zeros(shape, f32)
        t_planes = []
        for k in range(count + 1):
            inv = inverse_diagonal(low_sum(elements[k]) + low_sum(elements[k + 1]), frees[k], scale)
            z = [nodes[k][c] * inv for c in range(3)]
            t_planes.append([modes(z[c] * frees[k]) for c in range(3)])
            if k < count:
                for c in range(3):
                    num = num + jnp.where(frees[k] > 0.5, 0.0, z[c] * z[c])
                    den = den + z[c] * nodes[k][c]
        for k in range(count):
            u, f = element_forces(t_planes[k], t_planes[k + 1], elements[k + 1] * scale)
            for key in f:
                num = num + u[key] * f[key]
        return [jnp.sum(jnp.where(mine, num, 0.0)), jnp.sum(jnp.where(mine, den, 0.0))]

    totals += level_sums(
        [[c1[c, k] for c in range(3)] for k in range(1, 4)],
        None,
        [y1[k] for k in range(1, 5)],
        [f1[k] for k in range(1, 4)],
        ((4, 12), 64, 2),
        2.0,
    )
    ry2, rz2 = restrict_rows(8, 16), restrict_lanes(128, 128, 64)
    py2, pz2 = pick_rows(8, 16), pick_lanes(128, 128, 64)
    my2, mz2 = mean_rows(8, 16), mean_lanes(128, 128, 64)
    f2 = [dot(dot(py2, f1[k]), pz2) for k in (1, 3)]
    c2 = []
    for n, k in enumerate((1, 3)):
        c2.append([dot(dot(ry2, c1[c, k] + 0.5 * (c1[c, k - 1] + c1[c, k + 1])), rz2) * f2[n] for c in range(3)])
    y2 = [dot(dot(my2, 0.5 * (y1[k] + y1[k + 1])), mz2) for k in (0, 2, 4)]
    totals += level_sums(c2, None, y2, f2, ((2, 6), 32, 1), 4.0)

    row = lax.broadcasted_iota(jnp.int32, (8, 128), 0)
    out = jnp.zeros((8, 128), f32)
    for k, total in enumerate(totals):
        out = jnp.where(row == k, total, out)
    sums[...] = out

    lane = lane_index((8, 128))
    static[0] = jnp.where(lane < 64, y1[2, 4:12], shifted(y1[3, 4:12], 64, 1))
    static[1] = jnp.where(lane < 64, f1[1, 4:12], shifted(f1[2, 4:12], 64, 1))


def second_kernel(ext, dinv, w0, w1, w2, full, tb, cb, gb):
    def run(src, lo, n, dst):
        def load_w(i):
            scaled = dinv[i] * ext[1, i]
            return [src(c, i) * scaled for c in range(3)]

        def emit(i, g):
            free = ext[1, i]
            for c in range(3):
                dst(c, i, jnp.where(free > 0.5, g[c], src(c, i) * dinv[i]))

        apply_planes(tb, cb, gb, lo, n, load_w, lambda i, at: ext[(0, i) + at], emit)

    def put_full(c, i, val):
        full[c, i] = val

    def put_last(c, i, val):
        w2[c, i - 4] = val

    run(lambda c, i: w0[c, i], 3, 10, put_full)
    run(lambda c, i: full[c, i], 4, 8, put_last)
    for c in range(3):
        for k in range(8):
            w1[c, k] = full[c, k + 4]


def estimate_of(sums, level):
    return jnp.max(sums[2 * level : 2 * level + 1, :] / sums[2 * level + 1 : 2 * level + 2, :])


def polynomial():
    theta, delta = centre_share, half_share
    sigma = theta / delta
    rho0 = 1.0 / sigma
    rho1 = 1.0 / (2.0 * sigma - rho0)
    rho2 = 1.0 / (2.0 * sigma - rho1)
    a10 = rho1 * rho0 / theta + 2.0 * rho1 / delta
    a11 = -2.0 * rho1 / (delta * theta)
    a20 = rho2 * rho1 * a10 + 2.0 * rho2 / delta
    a21 = rho2 * rho1 * a11 - (2.0 * rho2 / delta) * (1.0 / theta + a10)
    a22 = -(2.0 * rho2 / delta) * a11
    return 1.0 / theta + a10 + a20, a11 + a21, a22


def turns():
    sigma = centre_share / half_share
    rho = 1.0 / sigma
    out = []
    for _ in range(2):
        new = 1.0 / (2.0 * sigma - rho)
        out.append((new * rho, 2.0 * new / half_share))
        rho = new
    return out


def third_kernel(sums, ext, dinv, w0, w1, w2, static, res, pre, pack):
    inv = 1.0 / estimate_of(sums, 0)
    k0, k1, k2 = polynomial()
    b0 = k0 * inv
    b1 = k1 * inv * inv
    b2 = k2 * inv * inv * inv

    def step(k, carry):
        for c in range(3):
            res[c, k] = ext[2 + c, k + 4] - (b0 * w0[c, k + 4] + b1 * w1[c, k] + b2 * w2[c, k])
        return carry

    lax.fori_loop(0, 8, step, 0)
    rows, lanes = slice(8, 24), slice(0, 128)
    for k in range(4):
        for c in range(3):
            part = b0 * ext[2 + c, k + 6, rows, lanes] + b1 * w0[c, k + 6, rows, lanes] + b2 * w1[c, k + 2, rows, lanes]
            pre[c, k] = dinv[k + 6, rows, lanes] * part
    ry = matrix((8, 32), lambda r, c: to_f(c == 2 * r + 8) + to_f((c == 2 * r + 9) | (c == 2 * r + 7), 0.5))
    rz0 = restrict_lanes(256, 128, 128, 0, 64)
    rz1 = restrict_lanes(256, 128, 128, 64, 64)
    pack[0] = static[0]
    pack[1] = static[1]
    for c in range(3):
        one = res[c, 2] + 0.5 * (res[c, 1] + res[c, 3])
        two = res[c, 4] + 0.5 * (res[c, 3] + res[c, 5])
        pack[2 + c] = (dot(dot(ry, one), rz0) + dot(dot(ry, two), rz1)) * static[1]


def pack_coarse_kernel(t0, t1, t2, t3, t4, first, last):
    lane = lane_index((8, 128))
    for t, tile in enumerate((t0, t1, t2, t3, t4)):
        for a in range(5):
            for half in range(2):
                acc_first = jnp.zeros((8, 128), f32)
                acc_last = jnp.zeros((8, 128), f32)
                for s in range(8):
                    val = tile[4 * half + s // 2, a]
                    start = 64 * (s % 2)
                    inside = (lane >= 16 * s) & (lane < 16 * s + 16)
                    acc_first = jnp.where(inside, shifted(val, 16 * s - start, 1), acc_first)
                    acc_last = jnp.where(inside, shifted(val, 16 * s - start - 48, 1), acc_last)
                first[t, a, half] = acc_first
                last[t, a, half] = acc_last


def coarse_kernel(
    sums, core, t0, t1, t2, t3, t4, from_left, from_right, out, ext, dinv, d_a, d_b, x1, e1, y2, f2, i2, r2, d2a, d2b, x2, tb, cb, gb, tb2, cb2, gb2
):
    lane = lane_index((8, 128))
    for t, tile in enumerate((t0, t1, t2, t3, t4)):
        rows = slice(8 * t, 8 * t + 8)
        for a in range(5):
            for i in range(16):
                val = tile[i // 2, a]
                if i % 2:
                    val = shifted(val, 64, 1)
                s = i % 8
                right = from_right[t, a, i // 8]
                left = from_left[t, a, i // 8]
                val = jnp.where(lane < 64, val, 0.0)
                val = jnp.where((lane >= 64) & (lane < 80), shifted(right, 64 - 16 * s, 1), val)
                ext[a, i, rows] = jnp.where(lane >= 112, shifted(left, 112 - 16 * s, 1), val)

    inv1 = 1.0 / estimate_of(sums, 1)
    inv2 = 1.0 / estimate_of(sums, 2)
    start = 1.0 / centre_share
    later = turns()

    def diag_step(i, old):
        new = low_sum(ext[0, i])
        dinv[i] = inverse_diagonal(new + old, ext[1, i], 2.0)
        return new

    lax.fori_loop(0, 16, diag_step, low_sum(ext[0, 15]))

    def smooth(res, inv, n, scale, free_of, e_of, d_inv, bufs, first, second, x, rows, last):
        steps = [(first, second) + later[0], (second, first) + later[1]]
        if last:
            steps.append((first, None, 0.0, 0.0))
        for src, dst, keep, gain in steps:

            def load_w(i, src=src):
                i = i & (n - 1)
                free = free_of(i)
                return [src[c, i] * free for c in range(3)]

            def emit(i, g, src=src, dst=dst, keep=keep, gain=gain):
                free = free_of(i)
                for c in range(3):
                    d = src[c, i]
                    left = res(c, i) - jnp.where(free > 0.5, g[c], d)
                    res(c, i, left)
                    if dst is not None:
                        new = keep * d + (gain * inv) * (d_inv(i) * left)
                        dst[c, i] = new
                        x[c, i] = x[c, i] + new

            apply_planes(*bufs, 0, n, load_w, lambda i, at: e_of(i & (n - 1), at) * scale, emit)

    def res1(c, i, val=None):
        if val is None:
            return ext[2 + c, i]
        ext[2 + c, i] = val

    def begin1(i, carry):
        for c in range(3):
            d = (start * inv1) * (dinv[i] * ext[2 + c, i])
            d_a[c, i] = d
            x1[c, i] = d
        return carry

    lax.fori_loop(0, 16, begin1, 0)
    smooth(
        res1, inv1, 16, 2.0, lambda i: ext[1, i], lambda i, at: ext[(0, i) + at], lambda i: dinv[i],
        (tb, cb, gb), d_a, d_b, x1, 40, True,
    )

    ry, rz = restrict_rows(24, 40, 20), restrict_lanes(128, 128, 64)
    py, pz = pick_rows(24, 40, 20), pick_lanes(128, 128, 64)
    my, mz = mean_rows(24, 40, 20), mean_lanes(128, 128, 64)

    def down(k, carry):
        i = 2 * k
        below = (i + 15) & 15
        free = dot(dot(py, ext[1, i]), pz)
        f2[k] = free
        y2[k] = dot(dot(my, 0.5 * (ext[0, i] + ext[0, i + 1])), mz)
        for c in range(3):
            fine = ext[2 + c, i] + 0.5 * (ext[2 + c, below] + ext[2 + c, i + 1])
            r2[c, k] = dot(dot(ry, fine), rz) * free
        return carry

    lax.fori_loop(0, 8, down, 0)

    def begin2(k, carry):
        inverse = inverse_diagonal(low_sum(y2[k]) + low_sum(y2[(k + 7) & 7]), f2[k], 4.0)
        i2[k] = inverse
        for c in range(3):
            d = (start * inv2) * (inverse * r2[c, k])
            d2a[c, k] = d
            x2[c, k] = d
        return carry

    lax.fori_loop(0, 8, begin2, 0)

    def res2(c, i, val=None):
        if val is None:
            return r2[c, i]
        r2[c, i] = val

    smooth(
        res2, inv2, 8, 4.0, lambda i: f2[i], lambda i, at: y2[(i,) + at], lambda i: i2[i],
        (tb2, cb2, gb2), d2a, d2b, x2, 24, False,
    )

    up = slice(8, 32)
    qy, qz = prolong_rows(24, 24, 4), prolong_lanes(128, 128, 64)

    def raise_step(k, carry):
        for c in range(3):
            here = x2[c, k]
            even = dot(dot(qy, here), qz)
            odd = dot(dot(qy, 0.5 * (here + x2[c, (k + 1) & 7])), qz)
            e1[c, 2 * k] = even * ext[1, 2 * k, up]
            e1[c, 2 * k + 1] = odd * ext[1, 2 * k + 1, up]
        return carry

    lax.fori_loop(0, 8, raise_step, 0)

    def load_e(i):
        i = i & 15
        free = ext[1, i, up]
        return [e1[c, i] * free for c in range(3)]

    def emit_e(i, g):
        free = ext[1, i, up]
        for c in range(3):
            left = ext[2 + c, i, up] - jnp.where(free > 0.5, g[c], e1[c, i])
            ext[2 + c, i, up] = left
            d = (start * inv1) * (dinv[i, up] * left)
            d_a[c, i, up] = d
            x1[c, i, up] = x1[c, i, up] + e1[c, i] + d

    def young_up(i, at):
        rows = slice(at[0].start + 8, at[0].stop + 8)
        return ext[0, i & 15, rows, at[1]] * 2.0

    apply_planes(tb2, cb2, gb2, 0, 16, load_e, young_up, emit_e)
    for src, dst, keep, gain in [(d_a, d_b) + later[0], (d_b, d_a) + later[1]]:

        def load_d(i, src=src):
            i = i & 15
            free = ext[1, i, up]
            return [src[c, i, up] * free for c in range(3)]

        def emit_d(i, g, src=src, dst=dst, keep=keep, gain=gain):
            free = ext[1, i, up]
            for c in range(3):
                d = src[c, i, up]
                left = ext[2 + c, i, up] - jnp.where(free > 0.5, g[c], d)
                ext[2 + c, i, up] = left
                new = keep * d + (gain * inv1) * (dinv[i, up] * left)
                dst[c, i, up] = new
                x1[c, i, up] = x1[c, i, up] + new

        apply_planes(tb2, cb2, gb2, 0, 16, load_d, young_up, emit_d)

    place = 2 * core[0]
    for k in range(6):
        for c in range(3):
            out[c, k] = x1[c, (place + (14 + k)) & 15, up]


def last_kernel(sums, ext, dinv, res_in, pre, x1, out, e0, res, d_a, d_b, tb, cb, gb):
    inv = 1.0 / estimate_of(sums, 0)
    start = 1.0 / centre_share
    later = turns()
    qy, qz = prolong_rows(32, 24, 4), prolong_lanes(128, 256, 128)
    half = [[dot(dot(qy, x1[c, k]), qz) for k in range(6)] for c in range(3)]
    for k in range(6):
        for c in range(3):
            e0[c, 2 * k] = half[c][k] * ext[1, 2 * k + 2]
            if k < 5:
                e0[c, 2 * k + 1] = 0.5 * (half[c][k] + half[c][k + 1]) * ext[1, 2 * k + 3]
    rows, lanes = slice(8, 24), slice(0, 128)

    def load_e(i):
        return [e0[c, i - 2] * ext[1, i] for c in range(3)]

    def emit_e(i, g):
        free = ext[1, i]
        for c in range(3):
            left = res_in[c, i - 4] - jnp.where(free > 0.5, g[c], e0[c, i - 2])
            res[c, i - 4] = left
            d_a[c, i - 4] = (start * inv) * (dinv[i] * left)

    young = lambda i, at: ext[(0, i) + at]
    apply_planes(tb, cb, gb, 4, 8, load_e, young, emit_e)

    def load_a(i):
        return [d_a[c, i - 4] * ext[1, i] for c in range(3)]

    def emit_a(i, g):
        free = ext[1, i]
        keep, gain = later[0]
        for c in range(3):
            d = d_a[c, i - 4]
            left = res[c, i - 4] - jnp.where(free > 0.5, g[c], d)
            res[c, i - 4] = left
            d_b[c, i - 4] = keep * d + (gain * inv) * (dinv[i] * left)

    apply_planes(tb, cb, gb, 5, 6, load_a, young, emit_a)

    def load_b(i):
        return [d_b[c, i - 4] * ext[1, i] for c in range(3)]

    def emit_b(i, g):
        free = ext[1, i]
        keep, gain = later[1]
        for c in range(3):
            d = d_b[c, i - 4]
            left = res[c, i - 4] - jnp.where(free > 0.5, g[c], d)
            new = keep * d + (gain * inv) * (dinv[i] * left)
            total = e0[c, i - 2] + d_a[c, i - 4] + d + new
            out[c, i - 6] = pre[c, i - 6] + total[rows, lanes]

    apply_planes(tb, cb, gb, 6, 4, load_b, young, emit_b)


def call(kernel, outs, scratch=(), smem=None, flops=0):
    def run(*args):
        specs = [pl.BlockSpec(memory_space=pltpu.SMEM if n == smem else pltpu.VMEM) for n in range(len(args))]
        return pl.pallas_call(
            kernel,
            in_specs=specs,
            out_specs=[pl.BlockSpec(memory_space=pltpu.VMEM) for _ in outs],
            out_shape=[jax.ShapeDtypeStruct(shape, f32) for shape in outs],
            scratch_shapes=list(scratch),
            compiler_params=pltpu.CompilerParams(vmem_limit_bytes=VMEM_LIMIT),
            cost_estimate=pl.CostEstimate(flops=flops, bytes_accessed=1 << 20, transcendentals=0),
        )(*args)

    return run


def send(value, axis, shift):
    count = lax.axis_size(axis)
    return lax.ppermute(value, axis, [(i, (i + shift) % count) for i in range(count)])


def swap_core(value):
    return lax.ppermute(value, "gx", [(i, i ^ 1) for i in range(lax.axis_size("gx"))])


def total_of(sums):
    sums = sums + swap_core(sums)
    sums = sums + send(sums, "gx", 2) + send(sums, "gx", -2) + send(sums, "gx", 4)
    sums = sums + send(sums, "gz", 1) + send(sums, "gz", -1) + send(sums, "gz", 2)
    sums = sums + send(sums, "gy", 4)
    return sums + send(sums, "gy", 1) + send(sums, "gy", -1) + send(sums, "gy", 2)


def local(density_level, support_mask, load_mask, load_vector):
    own, low, high = call(prepare_kernel, [(5, 4, 16, 128), (5, 1, 16, 128), (5, 2, 16, 128)])(
        density_level, support_mask, load_mask, load_vector
    )
    left, right = send(own, "gx", 1), send(own, "gx", -1)
    far_left, far_right = send(high, "gx", 2), send(low, "gx", -2)
    low, high = call(join_x_kernel, [(5, NXE, 8, 128)] * 2)(own, left, right, far_left, far_right)
    up, down = send(high, "gy", 1), send(low, "gy", -1)
    first, last = call(pack_z_kernel, [(5, 32, 128)] * 2)(up, low, high, down)
    from_left, from_right = send(last, "gz", 1), send(first, "gz", -1)
    fine = (NYE, NZE)
    ext, dinv, w0, static, sums = call(
        first_kernel,
        [(5, NXE) + fine, (NXE,) + fine, (3, NXE) + fine, (2, 8, 128), (8, 128)],
        [
            pltpu.VMEM((3, 5, 16, 128), f32),
            pltpu.VMEM((6, 16, 128), f32),
            pltpu.VMEM((5, 16, 128), f32),
            pltpu.VMEM((8, 128), f32),
        ]
        + work_buffers(*fine),
    )(up, low, high, down, from_left, from_right)
    w1, w2 = call(
        second_kernel, [(3, 8) + fine] * 2, [pltpu.VMEM((3, NXE) + fine, f32)] + work_buffers(*fine), flops=1 << 26
    )(ext, dinv, w0)
    sums = total_of(sums)
    res, pre, pack = call(third_kernel, [(3, 8) + fine, (3, 4, 16, 128), (5, 8, 128)])(
        sums, ext, dinv, w0, w1, w2, static
    )
    core = lax.axis_index("gx") & 1
    other = swap_core(pack)
    pair = jnp.stack([jnp.where(core == 0, pack, other), jnp.where(core == 0, other, pack)])
    chips = jnp.concatenate([pair, send(pair, "gx", -2), send(pair, "gx", 4), send(pair, "gx", 2)], axis=0)
    tiles = [send(chips, "gy", 2), send(chips, "gy", 1), chips, send(chips, "gy", -1), send(chips, "gy", -2)]
    first, last = call(pack_coarse_kernel, [(5, 5, 2, 8, 128)] * 2)(*tiles)
    from_left, from_right = send(last, "gz", 1), send(first, "gz", -1)
    big, mid = (16, 40, 128), (8, 24, 128)
    x1 = call(
        coarse_kernel,
        [(3, 6, 24, 128)],
        [
            pltpu.VMEM((5,) + big, f32),
            pltpu.VMEM(big, f32),
            pltpu.VMEM((3,) + big, f32),
            pltpu.VMEM((3,) + big, f32),
            pltpu.VMEM((3,) + big, f32),
            pltpu.VMEM((3, 16, 24, 128), f32),
            pltpu.VMEM(mid, f32),
            pltpu.VMEM(mid, f32),
            pltpu.VMEM(mid, f32),
            pltpu.VMEM((3,) + mid, f32),
            pltpu.VMEM((3,) + mid, f32),
            pltpu.VMEM((3,) + mid, f32),
            pltpu.VMEM((3,) + mid, f32),
        ]
        + work_buffers(40, 128)
        + work_buffers(24, 128),
        smem=1,
    )(sums, core.reshape(1).astype(jnp.int32), *tiles, from_left, from_right)[0]
    return call(
        last_kernel,
        [(3, 4, 16, 128)],
        [
            pltpu.VMEM((3, 12) + fine, f32),
            pltpu.VMEM((3, 8) + fine, f32),
            pltpu.VMEM((3, 8) + fine, f32),
            pltpu.VMEM((3, 8) + fine, f32),
        ]
        + work_buffers(*fine),
    )(sums, ext, dinv, res, pre, x1)[0]


def solution(mesh):
    block = P("gx", "gy", "gz")
    return jax.shard_map(
        local,
        mesh=mesh,
        in_specs=(block, block, block, P(None, "gx", "gy", "gz")),
        out_specs=P(None, "gx", "gy", "gz"),
        check_vma=False,
    )
```

```python
import jax
import jax.numpy as jnp
from jax import lax
from jax.experimental import pallas as pl
from jax.experimental.pallas import tpu as pltpu
from jax.sharding import PartitionSpec as P

f32 = jnp.float32
young_floor = 0.001
poisson = 0.3
headroom = 1.5
floor_share = 0.3
lam = poisson / ((1.0 + poisson) * (1.0 - 2.0 * poisson))
mu = 1.0 / (2.0 * (1.0 + poisson))
diag_entry = (lam + 2 * mu + 2 * mu) / 16 + (2 * (lam + 3 * mu) + 2 * mu) / 48 + (lam + 4 * mu) / 144
centre_share = 0.5 * headroom * (1.0 + floor_share)
half_share = 0.5 * headroom * (1.0 - floor_share)
VMEM_LIMIT = 56 * 1024 * 1024

NXE = 15
SS, SD, DS, DD = 0, 1, 2, 3
REG = (8, 128)


def roll(v, amount, axis):
    return pltpu.roll(v, amount % v.shape[axis], axis=axis)


def lanes_of(shape=REG):
    return lax.broadcasted_iota(jnp.int32, shape, 1)


def z_next(p):
    return [p[1], roll(p[0], -1, 1)] if len(p) == 2 else [roll(p[0], -1, 1)]


def z_prev(p):
    return [roll(p[1], 1, 1), p[0]] if len(p) == 2 else [roll(p[0], 1, 1)]


def y_next(plane):
    return plane[1:] + [[roll(v, -1, 0) for v in plane[0]]]


def y_prev(plane):
    return [[roll(v, 1, 0) for v in plane[-1]]] + plane[:-1]


def added(one, two):
    return [[a + b for a, b in zip(p, q)] for p, q in zip(one, two)]


def get_plane(ref, *at):
    groups, parts = ref.shape[-4:-2]
    return [[ref[at + (y, z)] for z in range(parts)] for y in range(groups)]


def element_forces(t0, t1, e):
    u = {}
    for c in range(3):
        for m in range(4):
            u[c, "d", m] = t1[c][m] - t0[c][m]
            if m != SS:
                u[c, "s", m] = t1[c][m] + t0[c][m]
    f = {}
    e_a, e_b, e_c = e * (lam / 16), e * (2 * mu / 16), e * (mu / 16)
    e_d, e_e, e_f = e * (lam / 48), e * (3 * mu / 48), e * (mu / 48)
    e_g = e * ((lam + 4 * mu) / 144)
    normal = ((0, "d", SS), (1, "s", DS), (2, "s", SD))
    t = e_a * (u[normal[0]] + u[normal[1]] + u[normal[2]])
    for key in normal:
        f[key] = t + e_b * u[key]
    for one, two in (((0, "s", DS), (1, "d", SS)), ((1, "s", SD), (2, "s", DS)), ((0, "s", SD), (2, "d", SS))):
        f[one] = f[two] = e_c * (u[one] + u[two])
    for one, two in (((0, "d", DS), (2, "s", DD)), ((0, "d", SD), (1, "s", DD)), ((1, "d", DS), (2, "d", SD))):
        p = e_d * (u[one] + u[two])
        f[one] = p + e_e * u[one]
        f[two] = p + e_e * u[two]
    triple = ((0, "s", DD), (1, "d", SD), (2, "d", DS))
    q = u[triple[0]] + u[triple[1]] + u[triple[2]]
    for key in triple:
        f[key] = e_f * (u[key] + q)
    for c in range(3):
        f[c, "d", DD] = e_g * u[c, "d", DD]
    return u, f


def z_modes(w):
    out = []
    for p in w:
        out.append([(a + b, b - a) for a, b in zip(p, z_next(p))])
    return out


def y_modes(cur, nxt):
    return [[(s + su, d + du, su - s, du - d) for (s, d), (su, du) in zip(p, q)] for p, q in zip(cur, nxt)]


def rows_above(first):
    return [[tuple(roll(v, -1, 0) for v in pair) for pair in p] for p in first]


def forward_plane(t, groups, load_w):
    first = cur = z_modes(load_w(0))
    for y in range(groups):
        nxt = z_modes(load_w(y + 1)) if y < groups - 1 else rows_above(first)
        for c, p in enumerate(y_modes(cur, nxt)):
            for z, vals in enumerate(p):
                for m, val in enumerate(vals):
                    t[4 * c + m, y, z] = val
        cur = nxt


def finish_rows(low, high):
    res = []
    for one, two in zip(low, high):
        s = [a[0] + b[0] for a, b in zip(one, two)]
        d = [a[1] + b[1] for a, b in zip(one, two)]
        down = [a - b for a, b in zip(s, d)]
        up = z_prev([a + b for a, b in zip(s, d)])
        res.append([a + b for a, b in zip(down, up)])
    return res


def element_plane(t0_ref, t1_ref, c_ref, groups, parts, load_w, load_e, emit, fresh):
    first = cur = z_modes(load_w(0))
    prev = start = None
    for y in range(groups):
        nxt = z_modes(load_w(y + 1)) if y < groups - 1 else rows_above(first)
        t1 = y_modes(cur, nxt)
        low = [[None] * parts for _ in range(3)]
        high = [[None] * parts for _ in range(3)]
        for z in range(parts):
            t0 = [[t0_ref[4 * c + m, y, z] for m in range(4)] for c in range(3)]
            for c in range(3):
                for m in range(4):
                    t1_ref[4 * c + m, y, z] = t1[c][z][m]
            u, f = element_forces(t0, [t1[c][z] for c in range(3)], load_e(y, z))
            for c in range(3):
                g = []
                for m in range(4):
                    d = f[c, "d", m]
                    if not fresh:
                        old = c_ref[4 * c + m, y, z]
                        g.append(old - d if m == SS else old + (f[c, "s", m] - d))
                    c_ref[4 * c + m, y, z] = d if m == SS else f[c, "s", m] + d
                if not fresh:
                    low[c][z] = (g[SS] - g[DS], g[SD] - g[DD])
                    high[c][z] = (g[SS] + g[DS], g[SD] + g[DD])
        if not fresh:
            if y == 0:
                start = low
            else:
                emit(y, finish_rows(low, prev))
            prev = high
        cur = nxt
    if not fresh:
        last = [[tuple(roll(v, 1, 0) for v in pair) for pair in p] for p in prev]
        emit(0, finish_rows(start, last))


def apply_planes(bufs, lo, n, load_w, load_e, emit):
    t_ref, c_ref = bufs
    groups, parts = c_ref.shape[1:3]

    def one(i, a, fresh=False):
        element_plane(
            t_ref.at[a],
            t_ref.at[1 - a],
            c_ref,
            groups,
            parts,
            lambda y: load_w(i + 1, y),
            lambda y, z: load_e(i, y, z),
            lambda y, res: emit(i, y, res),
            fresh,
        )

    forward_plane(t_ref.at[0], groups, lambda y: load_w(lo - 1, y))
    one(lo - 1, 0, True)

    def step(j, carry):
        one(lo + 2 * j, 1)
        one(lo + 2 * j + 1, 0)
        return carry

    lax.fori_loop(0, n // 2, step, 0)


def work_buffers(groups, parts):
    return [pltpu.VMEM((2, 12, groups, parts) + REG, f32), pltpu.VMEM((12, groups, parts) + REG, f32)]


def low_sum(plane):
    plane = [[a + b for a, b in zip(p, z_prev(p))] for p in plane]
    return added(plane, y_prev(plane))


def inverse_diagonal(e_sum, free, scale):
    return jnp.where(free > 0.5, 1.0 / (e_sum * (diag_entry * scale)), 1.0)


def matrix(fun):
    shape = (128, 128)
    r = lax.broadcasted_iota(jnp.int32, shape, 0)
    c = lax.broadcasted_iota(jnp.int32, shape, 1)
    return fun(r, c)


def dot(a, b):
    return jnp.dot(a, b, precision=lax.Precision.HIGHEST, preferred_element_type=f32)


def to_f(cond, val=1.0):
    return jnp.where(cond, f32(val), f32(0.0))


def split_matrix(width):
    def fun(r, c):
        z = r % width
        return to_f(c == r - z + (z % 2) * (width // 2) + z // 2)

    return matrix(fun)


def join_matrix():
    return matrix(lambda r, c: to_f(c == (r % 64) * 2 + r // 64))


def prepare_kernel(density, support, load, vector, own, low, high):
    scaled = density[...].astype(f32) / 255.0
    young = young_floor + (1.0 - young_floor) * scaled * scaled * scaled
    free = 1.0 - support[...].astype(f32)
    masked = free * load[...].astype(f32)
    split = split_matrix(128)
    rows = [young, free] + [masked * vector[c] for c in range(3)]
    for a, val in enumerate(rows):
        val = dot(val.reshape(64, 128), split).reshape(4, 16, 128)
        own[a] = val
        low[a] = val[0:1]
        high[a] = val[2:4]


def join_x_kernel(own, left, right, far_left, far_right, low, high):
    for out, rows in ((low, slice(0, 8)), (high, slice(8, 16))):
        for a in range(5):
            out[a, 0:2] = far_left[a, :, rows]
            out[a, 2:6] = left[a, :, rows]
            out[a, 6:10] = own[a, :, rows]
            out[a, 10:14] = right[a, :, rows]
            out[a, 14:15] = far_right[a, :, rows]


def pack_z_kernel(up, low, high, down, first, last):
    tiles = (up, low, high, down)
    lane = lanes_of() % 64
    for a in range(5):
        for t in range(4):
            acc_first = jnp.zeros(REG, f32)
            acc_last = jnp.zeros(REG, f32)
            for g in range(NXE):
                val = tiles[t][a, g]
                inside = (lane >= 4 * g) & (lane < 4 * g + 4)
                acc_first = jnp.where(inside, roll(val, 4 * g, 1), acc_first)
                acc_last = jnp.where(inside, roll(val, 4 * g - 60, 1), acc_last)
            first[a, 8 * t : 8 * t + 8] = acc_first
            last[a, 8 * t : 8 * t + 8] = acc_last


def first_kernel(up, low, high, down, from_left, from_right, stat, load, dinv, w0, static, sums, nat, rows16, tb, cb):
    lane = lanes_of()
    for a in range(5):
        for g in range(NXE):
            for t, tile in enumerate((up, low, high, down)):
                nat[a, g, 8 * t : 8 * t + 8] = tile[a, g]
    for a in range(5):
        for y in range(4):
            rows = pl.ds(y, 8, stride=4)
            left = from_left[a, rows]
            right = from_right[a, rows]
            for g in range(NXE):
                own = nat[a, g, rows]
                even = jnp.where(lane < 64, own, 0.0)
                even = jnp.where((lane >= 64) & (lane < 68), roll(right, 64 - 4 * g, 1), even)
                even = jnp.where(lane >= 124, roll(left, 124 - 4 * g, 1), even)
                odd = jnp.where(lane < 64, roll(own, 64, 1), 0.0)
                odd = jnp.where((lane >= 64) & (lane < 68), roll(right, -4 * g, 1), odd)
                odd = jnp.where(lane >= 124, roll(left, 60 - 4 * g, 1), odd)
                for z, val in enumerate((even, odd)):
                    if a < 2:
                        stat[a, g, y, z] = val
                    else:
                        load[a - 2, g, y, z] = val

    def diag_step(i, carry):
        total = added(low_sum(get_plane(stat, 0, i)), low_sum(get_plane(stat, 0, jnp.maximum(i - 1, 0))))
        for y in range(4):
            for z in range(2):
                dinv[i, y, z] = inverse_diagonal(total[y][z], stat[1, i, y, z], 1.0)
        return carry

    lax.fori_loop(0, NXE, diag_step, 0)

    def load_w(i, y):
        scaled = [dinv[i, y, z] * stat[1, i, y, z] for z in range(2)]
        return [[load[c, i, y, z] * scaled[z] for z in range(2)] for c in range(3)]

    def emit(i, y, g):
        for z in range(2):
            free = stat[1, i, y, z]
            inv = dinv[i, y, z]
            for c in range(3):
                w0[c, i, y, z] = jnp.where(free > 0.5, g[c][z], load[c, i, y, z] * inv)

    apply_planes((tb, cb), 2, 12, load_w, lambda i, y, z: stat[0, i, y, z], emit)

    sub = lax.broadcasted_iota(jnp.int32, REG, 0)
    own_rows = (sub >= 2) & (sub < 6)

    def masked_sum(val, count):
        return jnp.sum(jnp.where(own_rows & (lane < count), val, 0.0))

    num = jnp.zeros(REG, f32)
    den = jnp.zeros(REG, f32)
    for i in range(6, 10):
        for y in range(4):
            for z in range(2):
                for c in range(3):
                    b = load[c, i, y, z]
                    v = b * dinv[i, y, z]
                    num = num + v * w0[c, i, y, z]
                    den = den + v * b
    totals = [masked_sum(num, 64), masked_sum(den, 64)]

    f1 = [[[stat[1, 2 * k + 4, y, 0]] for y in (0, 2)] for k in range(5)]
    c1 = []
    for k in range(5):
        i = 2 * k + 4
        c1.append([])
        for c in range(3):
            c1[k].append(restrict_plane([get_plane(load, c, j) for j in (i - 1, i, i + 1)], f1[k]))
    y1 = []
    for k in range(6):
        both = added(get_plane(stat, 0, 2 * k + 2), get_plane(stat, 0, 2 * k + 3))
        y1.append([[0.125 * (both[y][0] + both[y][1] + both[y + 1][0] + both[y + 1][1])] for y in (0, 2)])

    def level_sums(nodes, elements, frees, scale, lanes):
        count = len(frees) - 1
        num = jnp.zeros(REG, f32)
        den = jnp.zeros(REG, f32)
        groups = len(frees[0])
        modes = []
        for k in range(count + 1):
            total = added(low_sum(elements[k]), low_sum(elements[k + 1]))
            inv = [inverse_diagonal(total[y][0], frees[k][y][0], scale) for y in range(groups)]
            v = [[nodes[k][c][y][0] * inv[y] for y in range(groups)] for c in range(3)]
            zs = [z_modes([[v[c][y] * frees[k][y][0]] for c in range(3)]) for y in range(groups)]
            zs.append(rows_above(zs[0]))
            modes.append([y_modes(zs[y], zs[y + 1]) for y in range(groups)])
            if k < count:
                for c in range(3):
                    for y in range(groups):
                        num = num + jnp.where(frees[k][y][0] > 0.5, 0.0, v[c][y] * v[c][y])
                        den = den + v[c][y] * nodes[k][c][y][0]
        for k in range(count):
            for y in range(groups):
                u, f = element_forces(
                    [modes[k][y][c][0] for c in range(3)],
                    [modes[k + 1][y][c][0] for c in range(3)],
                    elements[k + 1][y][0] * scale,
                )
                for key in f:
                    num = num + u[key] * f[key]
        return [masked_sum(num, lanes), masked_sum(den, lanes)]

    totals += level_sums(c1[1:4], y1[1:5], f1[1:4], 2.0, 64)

    pick = matrix(lambda r, c: to_f(r == 2 * (c % 64)))
    mean = matrix(lambda r, c: to_f((r == 2 * (c % 64)) | (r == 2 * (c % 64) + 1), 0.5))
    half = matrix(
        lambda r, c: to_f(r == 2 * (c % 64)) + to_f((r == 2 * (c % 64) + 1) | (r == (2 * (c % 64) - 1) % 128), 0.5)
    )
    f2 = [[[dot(f1[k][0][0], pick)]] for k in (1, 3)]
    c2 = []
    for n, k in enumerate((1, 3)):
        c2.append([])
        for c in range(3):
            x = [c1[k][c][y][0] + 0.5 * (c1[k - 1][c][y][0] + c1[k + 1][c][y][0]) for y in range(2)]
            val = x[0] + 0.5 * (x[1] + roll(x[1], 1, 0))
            c2[n].append([[dot(val, half) * f2[n][0][0]]])
    y2 = []
    for k in (0, 2, 4):
        val = 0.25 * (y1[k][0][0] + y1[k][1][0] + y1[k + 1][0][0] + y1[k + 1][1][0])
        y2.append([[dot(val, mean)]])
    totals += level_sums(c2, y2, f2, 4.0, 32)

    row = lax.broadcasted_iota(jnp.int32, REG, 0)
    out = jnp.zeros(REG, f32)
    for k, total in enumerate(totals):
        out = jnp.where(row == k, total, out)
    sums[...] = out

    for n, planes in enumerate((y1[2:4], f1[1:3])):
        static[n] = side_by_side(planes, rows16)


def restrict_plane(planes, free=None):
    low, mid, high = planes
    x = [[b + 0.5 * (a + c) for a, b, c in zip(*p)] for p in zip(low, mid, high)]
    y = []
    for n in range(2):
        below = [roll(v, 1, 0) for v in x[3]] if n == 0 else x[1]
        y.append([b + 0.5 * (a + c) for a, b, c in zip(below, x[2 * n], x[2 * n + 1])])
    out = []
    for n in range(2):
        even, odd = y[n]
        val = even + 0.5 * (odd + roll(odd, 1, 1))
        out.append([val if free is None else val * free[n][0]])
    return out


def side_by_side(planes, rows16):
    vals = []
    for n, plane in enumerate(planes):
        for y in range(2):
            rows16[n, pl.ds(y, 8, stride=2)] = plane[y][0]
        vals.append(rows16[n, 4:12])
    return jnp.where(lanes_of() < 64, vals[0], roll(vals[1], 64, 1))


def second_kernel(stat, dinv, w0, w1, w2, full, tb, cb):
    def run(src, lo, n, dst):
        def load_w(i, y):
            scaled = [dinv[i, y, z] * stat[1, i, y, z] for z in range(2)]
            return [[src[c, i, y, z] * scaled[z] for z in range(2)] for c in range(3)]

        def emit(i, y, g):
            for z in range(2):
                free = stat[1, i, y, z]
                inv = dinv[i, y, z]
                for c in range(3):
                    dst(c, i, y, z, jnp.where(free > 0.5, g[c][z], src[c, i, y, z] * inv))

        apply_planes((tb, cb), lo, n, load_w, lambda i, y, z: stat[0, i, y, z], emit)

    def put_full(c, i, y, z, val):
        full[c, i, y, z] = val

    def put_last(c, i, y, z, val):
        w2[c, i - 4, y, z] = val

    run(w0, 3, 10, put_full)
    run(full, 4, 8, put_last)
    for c in range(3):
        for k in range(8):
            w1[c, k] = full[c, k + 4]


def estimate_of(sums, level):
    return jnp.max(sums[2 * level : 2 * level + 1, :] / sums[2 * level + 1 : 2 * level + 2, :])


def polynomial():
    theta, delta = centre_share, half_share
    sigma = theta / delta
    rho0 = 1.0 / sigma
    rho1 = 1.0 / (2.0 * sigma - rho0)
    rho2 = 1.0 / (2.0 * sigma - rho1)
    a10 = rho1 * rho0 / theta + 2.0 * rho1 / delta
    a11 = -2.0 * rho1 / (delta * theta)
    a20 = rho2 * rho1 * a10 + 2.0 * rho2 / delta
    a21 = rho2 * rho1 * a11 - (2.0 * rho2 / delta) * (1.0 / theta + a10)
    a22 = -(2.0 * rho2 / delta) * a11
    return 1.0 / theta + a10 + a20, a11 + a21, a22


def turns():
    sigma = centre_share / half_share
    rho = 1.0 / sigma
    out = []
    for _ in range(2):
        new = 1.0 / (2.0 * sigma - rho)
        out.append((new * rho, 2.0 * new / half_share))
        rho = new
    return out


def third_kernel(sums, load, dinv, w0, w1, w2, static, res, pre, pack, rows16):
    inv = 1.0 / estimate_of(sums, 0)
    k0, k1, k2 = polynomial()
    b0 = k0 * inv
    b1 = k1 * inv * inv
    b2 = k2 * inv * inv * inv

    def step(k, carry):
        for c in range(3):
            res[c, k] = load[c, k + 4] - (b0 * w0[c, k + 4] + b1 * w1[c, k] + b2 * w2[c, k])
        return carry

    lax.fori_loop(0, 8, step, 0)
    for k in range(4):
        for c in range(3):
            pre[c, k] = dinv[k + 6] * (b0 * load[c, k + 6] + b1 * w0[c, k + 6] + b2 * w1[c, k + 2])
    parts = [static[0], static[1]]
    for c in range(3):
        planes = [restrict_plane([get_plane(res, c, j) for j in (i - 1, i, i + 1)]) for i in (2, 4)]
        parts.append(side_by_side(planes, rows16.at[c]) * static[1])
    split = dot(jnp.concatenate(parts, axis=0), split_matrix(64))
    for a in range(5):
        pack[a] = split[8 * a : 8 * a + 8]


def join_chips_kernel(mine, right, opposite, left, out):
    lane = lanes_of()
    for r, (near, far) in enumerate(((mine, opposite), (right, left))):
        for k in range(2):
            for a in range(5):
                one, two = near[k, a], far[k, a]
                out[a, 4 * r + 2 * k] = jnp.where(lane < 64, one, roll(two, 64, 1))
                out[a, 4 * r + 2 * k + 1] = jnp.where(lane < 64, roll(one, 64, 1), two)


def pack_coarse_kernel(t0, t1, t2, t3, t4, first, last):
    lane = lanes_of() % 64
    for t, tile in enumerate((t0, t1, t2, t3, t4)):
        for a in range(5):
            acc = [jnp.zeros(REG, f32) for _ in range(4)]
            for i in range(8):
                val = tile[a, i]
                inside = (lane >= 8 * i) & (lane < 8 * i + 8)
                for n, start in enumerate((0, 32, 24, 56)):
                    acc[n] = jnp.where(inside, roll(val, 8 * i - start, 1), acc[n])
            for z in range(2):
                first[t, a, z] = acc[z]
                last[t, a, z] = acc[2 + z]


def wrap(ref, planes, *at):
    for y in range(ref.shape[-4]):
        for z in range(ref.shape[-3]):
            ref[at + (0, y, z)] = roll(ref[at + (planes, y, z)], 64, 1)
            ref[at + (planes + 1, y, z)] = roll(ref[at + (1, y, z)], 64, 1)


def smooth(bufs, planes, young, free, dinv, res, x, inv, steps):
    groups, parts = res.shape[-4:-2]
    for src, dst, keep, gain in steps:

        def load_w(i, y, src=src):
            mask = [free[i + 1, y, z] for z in range(parts)]
            return [[src[c, i + 1, y, z] * mask[z] for z in range(parts)] for c in range(3)]

        def emit(i, y, g, src=src, dst=dst, keep=keep, gain=gain):
            for z in range(parts):
                mask = free[i + 1, y, z]
                scaled = None if dst is None else (gain * inv) * dinv[i, y, z]
                for c in range(3):
                    d = src[c, i + 1, y, z]
                    left = res[c, i, y, z] - jnp.where(mask > 0.5, g[c][z], d)
                    res[c, i, y, z] = left
                    if dst is not None:
                        new = keep * d + scaled * left if keep else scaled * left
                        dst[c, i + 1, y, z] = new
                        x[c, i, y, z] = x[c, i, y, z] + new

        apply_planes(bufs, 0, planes, load_w, lambda i, y, z: young[i + 1, y, z], emit)
        if dst is not None:
            for c in range(3):
                wrap(dst, planes, c)


def coarse_kernel(
    sums, core, t0, t1, t2, t3, t4, from_left, from_right, out,
    nat, young, free, dinv, res, d_a, d_b, x,
    nat2, young2, free2, dinv2, res2, d2_a, d2_b, x2,
    nat3, young3, free3, dinv3, res3, x3, rows_e, rows_o,
    tb, cb, tb2, cb2, tb3, cb3,
):
    lane = lanes_of()
    in_half = lane % 64
    for t, tile in enumerate((t0, t1, t2, t3, t4)):
        for a in range(5):
            for i in range(8):
                val = tile[a, i]
                for z in range(2):
                    here = jnp.where((in_half >= 8) & (in_half < 40), roll(val, 8 - 32 * z, 1), 0.0)
                    right = roll(from_right[t, a, z], 40 - 8 * i, 1)
                    left = roll(from_left[t, a, z], -8 * i, 1)
                    here = jnp.where((in_half >= 40) & (in_half < 48), right, here)
                    nat[a, i, z, 8 * t : 8 * t + 8] = jnp.where(in_half < 8, left, here)
    for i in range(8):
        for y in range(5):
            rows = pl.ds(y, 8, stride=5)
            for z in range(2):
                young[i + 1, y, z] = 2.0 * nat[0, i, z, rows]
                free[i + 1, y, z] = nat[1, i, z, rows]
                for c in range(3):
                    res[c, i, y, z] = nat[2 + c, i, z, rows]
    wrap(young, 8)
    wrap(free, 8)

    inv1 = 1.0 / estimate_of(sums, 1)
    inv2 = 1.0 / estimate_of(sums, 2)
    start = 1.0 / centre_share
    later = turns()

    def begin(i, carry):
        total = added(low_sum(get_plane(young, i + 1)), low_sum(get_plane(young, i)))
        for y in range(5):
            for z in range(2):
                inverse = inverse_diagonal(total[y][z], free[i + 1, y, z], 1.0)
                dinv[i, y, z] = inverse
                for c in range(3):
                    d = (start * inv1) * inverse * res[c, i, y, z]
                    d_a[c, i + 1, y, z] = d
                    x[c, i, y, z] = d
        return carry

    lax.fori_loop(0, 8, begin, 0)
    for c in range(3):
        wrap(d_a, 8, c)
    steps = [(d_a, d_b) + later[0], (d_b, d_a) + later[1], (d_a, None, 0.0, 0.0)]
    smooth((tb, cb), 8, young, free, dinv, res, x, inv1, steps)

    for a in range(5):
        for k in range(4):
            nat2[a, k, 0:8] = jnp.zeros(REG, f32)
            nat2[a, k, 48:56] = jnp.zeros(REG, f32)
    for k in range(4):
        for y in range(5):
            rows = pl.ds(8 + y, 8, stride=5)
            both = [young[2 * k + 1, y, z] + young[2 * k + 2, y, z] for z in range(2)]
            nat2[0, k, rows] = both[0] + both[1]
            nat2[1, k, rows] = free[2 * k + 1, y, 0]
            for c in range(3):
                part = []
                for z in range(2):
                    below = res[c, 2 * k - 1, y, z] if k else roll(res[c, 7, y, z], 64, 1)
                    part.append(res[c, 2 * k, y, z] + 0.5 * (below + res[c, 2 * k + 1, y, z]))
                nat2[2 + c, k, rows] = part[0] + 0.5 * (part[1] + roll(part[1], 1, 1))
        for y in range(3):
            at = [pl.ds(8 + 2 * y + n, 8, stride=6) for n in (-1, 0, 1)]
            young2[k + 1, y, 0] = 0.25 * (nat2[0, k, at[1]] + nat2[0, k, at[2]])
            mask = nat2[1, k, at[1]]
            free2[k + 1, y, 0] = mask
            for c in range(3):
                val = nat2[2 + c, k, at[1]] + 0.5 * (nat2[2 + c, k, at[0]] + nat2[2 + c, k, at[2]])
                res2[c, k, y, 0] = val * mask
    wrap(young2, 4)
    wrap(free2, 4)
    for k in range(4):
        total = added(low_sum(get_plane(young2, k + 1)), low_sum(get_plane(young2, k)))
        for y in range(3):
            inverse = inverse_diagonal(total[y][0], free2[k + 1, y, 0], 1.0)
            dinv2[k, y, 0] = inverse
            for c in range(3):
                d = (start * inv2) * inverse * res2[c, k, y, 0]
                d2_a[c, k + 1, y, 0] = d
                x2[c, k, y, 0] = d
    for c in range(3):
        wrap(d2_a, 4, c)
    steps = [(d2_a, d2_b) + later[0], (d2_b, d2_a) + later[1]]
    smooth((tb2, cb2), 4, young2, free2, dinv2, res2, x2, inv2, steps)

    for i in range(8):
        for z in range(2):
            for y in range(5):
                rows = pl.ds(y, 8, stride=5)
                nat[0, i, z, rows] = dinv[i, y, z]
                for c in range(3):
                    nat[1 + c, i, z, rows] = res[c, i, y, z]
            for y in range(3):
                rows = pl.ds(8 + y, 8, stride=3)
                dinv3[i, y, z] = nat[0, i, z, rows]
                for c in range(3):
                    res3[c, i, y, z] = nat[1 + c, i, z, rows]
    for i in range(8):
        for z in range(2):
            for y in range(5):
                rows = pl.ds(y, 8, stride=5)
                nat[0, i, z, rows] = young[i + 1, y, z]
                nat[1, i, z, rows] = free[i + 1, y, z]
                for c in range(3):
                    nat[2 + c, i, z, rows] = x[c, i, y, z]
            for y in range(3):
                rows = pl.ds(8 + y, 8, stride=3)
                young3[i + 1, y, z] = nat[0, i, z, rows]
                free3[i + 1, y, z] = nat[1, i, z, rows]
                for c in range(3):
                    x3[c, i, y, z] = nat[2 + c, i, z, rows]
    wrap(young3, 8)
    wrap(free3, 8)
    d3_a, d3_b = d_a, d_b
    for c in range(3):
        for k in range(4):
            here = [x2[c, k, y, 0] for y in range(3)]
            if k < 3:
                nxt = [x2[c, k + 1, y, 0] for y in range(3)]
            else:
                nxt = [roll(x2[c, 0, y, 0], 64, 1) for y in range(3)]
            for n, val in enumerate((here, [0.5 * (p + q) for p, q in zip(here, nxt)])):
                above = val[1:] + [roll(val[0], -1, 0)]
                for y in range(3):
                    nat3[n, pl.ds(2 * y, 8, stride=6)] = val[y]
                    nat3[n, pl.ds(2 * y + 1, 8, stride=6)] = 0.5 * (val[y] + above[y])
                i = 2 * k + n
                for y in range(3):
                    even = nat3[n, pl.ds(8 + y, 8, stride=3)]
                    odd = 0.5 * (even + roll(even, -1, 1))
                    for z, e in enumerate((even, odd)):
                        e = e * free3[i + 1, y, z]
                        d3_b[c, i + 1, y, z] = e
                        x3[c, i, y, z] = x3[c, i, y, z] + e
        wrap(d3_b, 8, c)
    steps = [(d3_b, d3_a, 0.0, start), (d3_a, d3_b) + later[0], (d3_b, d3_a) + later[1]]
    smooth((tb3, cb3), 8, young3, free3, dinv3, res3, x3, inv1, steps)

    place = 2 * core[0]
    for k in range(6):
        plane = (place + (14 + k)) & 15
        i = plane & 7
        swap = plane > 7
        for c in range(3):
            for y in range(3):
                rows = pl.ds(24 * (3 * k + c) + y, 8, stride=3)
                for z, dst in enumerate((rows_e, rows_o)):
                    val = x3[c, i, y, z]
                    dst[rows] = jnp.where(swap, roll(val, 64, 1), val)
    place_e = matrix(lambda r, c: to_f((r < 48) & (c == (2 * r + 112) % 128)))
    place_o = matrix(lambda r, c: to_f((r < 48) & (c == (2 * r + 113) % 128)))
    out[...] = (dot(rows_e[...], place_e) + dot(rows_o[...], place_o)).reshape(6, 3, 24, 128)


def last_kernel(sums, stat, dinv, res_in, pre, x1, out, e0, res, d_a, d_b, rows, tb, cb):
    inv = 1.0 / estimate_of(sums, 0)
    start = 1.0 / centre_share
    later = turns()

    def raised(c, k):
        at = [x1[k, c, pl.ds(4 + n, 8, stride=2)] for n in range(3)]
        groups = [at[0], 0.5 * (at[0] + at[1]), at[1], 0.5 * (at[1] + at[2])]
        return [[v, 0.5 * (v + roll(v, -1, 1))] for v in groups]

    for c in range(3):
        here = raised(c, 0)
        for k in range(6):
            nxt = raised(c, k + 1) if k < 5 else None
            for y in range(4):
                for z in range(2):
                    e0[c, 2 * k, y, z] = here[y][z] * stat[1, 2 * k + 2, y, z]
                    if k < 5:
                        e0[c, 2 * k + 1, y, z] = 0.5 * (here[y][z] + nxt[y][z]) * stat[1, 2 * k + 3, y, z]
            here = nxt

    def loader(ref, shift):
        def load_w(i, y):
            mask = [stat[1, i, y, z] for z in range(2)]
            return [[ref[c, i - shift, y, z] * mask[z] for z in range(2)] for c in range(3)]

        return load_w

    def emit_e(i, y, g):
        for z in range(2):
            mask = stat[1, i, y, z]
            scaled = (start * inv) * dinv[i, y, z]
            for c in range(3):
                left = res_in[c, i - 4, y, z] - jnp.where(mask > 0.5, g[c][z], e0[c, i - 2, y, z])
                res[c, i - 4, y, z] = left
                d_a[c, i - 4, y, z] = scaled * left

    def emit_a(i, y, g):
        keep, gain = later[0]
        for z in range(2):
            mask = stat[1, i, y, z]
            scaled = (gain * inv) * dinv[i, y, z]
            for c in range(3):
                d = d_a[c, i - 4, y, z]
                left = res[c, i - 4, y, z] - jnp.where(mask > 0.5, g[c][z], d)
                res[c, i - 4, y, z] = left
                d_b[c, i - 4, y, z] = keep * d + scaled * left

    def emit_b(i, y, g):
        keep, gain = later[1]
        total = [[None, None] for _ in range(3)]
        for z in range(2):
            mask = stat[1, i, y, z]
            scaled = (gain * inv) * dinv[i, y, z]
            for c in range(3):
                d = d_b[c, i - 4, y, z]
                left = res[c, i - 4, y, z] - jnp.where(mask > 0.5, g[c][z], d)
                new = keep * d + scaled * left
                old = pre[c, i - 6, y, z] + e0[c, i - 2, y, z] + d_a[c, i - 4, y, z]
                total[c][z] = old + d + new
        for c in range(3):
            val = jnp.where(lanes_of() < 64, total[c][0], roll(total[c][1], 64, 1))
            rows[c, i - 6, pl.ds(y, 8, stride=4)] = val

    young = lambda i, y, z: stat[0, i, y, z]
    apply_planes((tb, cb), 4, 8, loader(e0, 2), young, emit_e)
    apply_planes((tb, cb), 5, 6, loader(d_a, 4), young, emit_a)
    apply_planes((tb, cb), 6, 4, loader(d_b, 4), young, emit_b)
    join = join_matrix()
    for c in range(3):
        for k in range(4):
            out[c, k] = dot(rows[c, k, 8:24], join)


def call(kernel, outs, scratch=(), smem=None, flops=0):
    def run(*args):
        specs = [pl.BlockSpec(memory_space=pltpu.SMEM if n == smem else pltpu.VMEM) for n in range(len(args))]
        return pl.pallas_call(
            kernel,
            in_specs=specs,
            out_specs=[pl.BlockSpec(memory_space=pltpu.VMEM) for _ in outs],
            out_shape=[jax.ShapeDtypeStruct(shape, f32) for shape in outs],
            scratch_shapes=[s if not isinstance(s, tuple) else pltpu.VMEM(s, f32) for s in scratch],
            compiler_params=pltpu.CompilerParams(vmem_limit_bytes=VMEM_LIMIT),
            cost_estimate=pl.CostEstimate(flops=flops, bytes_accessed=1 << 20, transcendentals=0),
        )(*args)

    return run


def send(value, axis, shift):
    count = lax.axis_size(axis)
    return lax.ppermute(value, axis, [(i, (i + shift) % count) for i in range(count)])


def swap_core(value):
    return lax.ppermute(value, "gx", [(i, i ^ 1) for i in range(lax.axis_size("gx"))])


def total_of(sums):
    sums = sums + swap_core(sums)
    sums = sums + send(sums, "gx", 2) + send(sums, "gx", -2) + send(sums, "gx", 4)
    sums = sums + send(sums, "gz", 1) + send(sums, "gz", -1) + send(sums, "gz", 2)
    sums = sums + send(sums, "gy", 4)
    return sums + send(sums, "gy", 1) + send(sums, "gy", -1) + send(sums, "gy", 2)


def local(density_level, support_mask, load_mask, load_vector):
    own, low, high = call(prepare_kernel, [(5, 4, 16, 128), (5, 1, 16, 128), (5, 2, 16, 128)])(
        density_level, support_mask, load_mask, load_vector
    )
    left, right = send(own, "gx", 1), send(own, "gx", -1)
    far_left, far_right = send(high, "gx", 2), send(low, "gx", -2)
    low, high = call(join_x_kernel, [(5, NXE, 8, 128)] * 2)(own, left, right, far_left, far_right)
    up, down = send(high, "gy", 1), send(low, "gy", -1)
    first, last = call(pack_z_kernel, [(5, 32, 128)] * 2)(up, low, high, down)
    from_left, from_right = send(last, "gz", 1), send(first, "gz", -1)
    fine = (4, 2) + REG
    stat, load, dinv, w0, static, sums = call(
        first_kernel,
        [(2, NXE) + fine, (3, NXE) + fine, (NXE,) + fine, (3, NXE) + fine, (2,) + REG, REG],
        [(5, NXE, 32, 128), (2, 16, 128)] + work_buffers(4, 2),
    )(up, low, high, down, from_left, from_right)
    w1, w2 = call(second_kernel, [(3, 8) + fine] * 2, [(3, NXE) + fine] + work_buffers(4, 2), flops=1 << 26)(
        stat, dinv, w0
    )
    sums = total_of(sums)
    res, pre, pack = call(third_kernel, [(3, 8) + fine, (3, 4) + fine, (5,) + REG], [(3, 2, 16, 128)])(
        sums, load, dinv, w0, w1, w2, static
    )
    core = lax.axis_index("gx") & 1
    other = swap_core(pack)
    pair = jnp.stack([jnp.where(core == 0, pack, other), jnp.where(core == 0, other, pack)])
    chips = call(join_chips_kernel, [(5, 8) + REG])(
        pair, send(pair, "gx", -2), send(pair, "gx", 4), send(pair, "gx", 2)
    )[0]
    tiles = [send(chips, "gy", 2), send(chips, "gy", 1), chips, send(chips, "gy", -1), send(chips, "gy", -2)]
    first, last = call(pack_coarse_kernel, [(5, 5, 2) + REG] * 2)(*tiles)
    from_left, from_right = send(last, "gz", 1), send(first, "gz", -1)
    five, three, one = (5, 2) + REG, (3, 2) + REG, (3, 1) + REG
    x1 = call(
        coarse_kernel,
        [(6, 3, 24, 128)],
        [(5, 8, 2, 40, 128), (10,) + five, (10,) + five, (8,) + five]
        + [(3, 8) + five, (3, 10) + five, (3, 10) + five, (3, 8) + five]
        + [(5, 4, 56, 128), (6,) + one, (6,) + one, (4,) + one]
        + [(3, 4) + one, (3, 6) + one, (3, 6) + one, (3, 4) + one]
        + [(2, 48, 128), (10,) + three, (10,) + three, (8,) + three]
        + [(3, 8) + three, (3, 8) + three, (432, 128), (432, 128)]
        + work_buffers(5, 2)
        + work_buffers(3, 1)
        + work_buffers(3, 2),
        smem=1,
    )(sums, core.reshape(1).astype(jnp.int32), *tiles, from_left, from_right)[0]
    return call(
        last_kernel,
        [(3, 4, 16, 128)],
        [(3, 12) + fine, (3, 8) + fine, (3, 8) + fine, (3, 8) + fine, (3, 4, 32, 128)] + work_buffers(4, 2),
    )(sums, stat, dinv, res, pre, x1)[0]


def solution(mesh):
    block = P("gx", "gy", "gz")
    return jax.shard_map(
        local,
        mesh=mesh,
        in_specs=(block, block, block, P(None, "gx", "gy", "gz")),
        out_specs=P(None, "gx", "gy", "gz"),
        check_vma=False,
    )
```

```python
import jax
import jax.numpy as jnp
from jax import lax
from jax.experimental import pallas as pl
from jax.experimental.pallas import tpu as pltpu
from jax.sharding import PartitionSpec as P

f32 = jnp.float32
young_floor = 0.001
poisson = 0.3
headroom = 1.5
floor_share = 0.3
lam = poisson / ((1.0 + poisson) * (1.0 - 2.0 * poisson))
mu = 1.0 / (2.0 * (1.0 + poisson))
diag_entry = (lam + 2 * mu + 2 * mu) / 16 + (2 * (lam + 3 * mu) + 2 * mu) / 48 + (lam + 4 * mu) / 144
centre_share = 0.5 * headroom * (1.0 + floor_share)
half_share = 0.5 * headroom * (1.0 - floor_share)

NXE = 15
SS, SD, DS, DD = 0, 1, 2, 3
REG = (8, 128)


def roll(v, amount, axis):
    return pltpu.roll(v, amount % v.shape[axis], axis=axis)


def lanes_of(shape=REG):
    return lax.broadcasted_iota(jnp.int32, shape, 1)


def z_next(p):
    return [p[1], roll(p[0], -1, 1)] if len(p) == 2 else [roll(p[0], -1, 1)]


def z_prev(p):
    return [roll(p[1], 1, 1), p[0]] if len(p) == 2 else [roll(p[0], 1, 1)]


def y_next(plane):
    return plane[1:] + [[roll(v, -1, 0) for v in plane[0]]]


def y_prev(plane):
    return [[roll(v, 1, 0) for v in plane[-1]]] + plane[:-1]


def added(one, two):
    return [[a + b for a, b in zip(p, q)] for p, q in zip(one, two)]


def get_plane(ref, *at):
    groups, parts = ref.shape[-4:-2]
    return [[ref[at + (y, z)] for z in range(parts)] for y in range(groups)]


def element_forces(t0, t1, e):
    u = {}
    for c in range(3):
        for m in range(4):
            u[c, "d", m] = t1[c][m] - t0[c][m]
            if m != SS:
                u[c, "s", m] = t1[c][m] + t0[c][m]
    f = {}
    e_a, e_b, e_c = e * (lam / 16), e * (2 * mu / 16), e * (mu / 16)
    e_d, e_e, e_f = e * (lam / 48), e * (3 * mu / 48), e * (mu / 48)
    e_g = e * ((lam + 4 * mu) / 144)
    normal = ((0, "d", SS), (1, "s", DS), (2, "s", SD))
    t = e_a * (u[normal[0]] + u[normal[1]] + u[normal[2]])
    for key in normal:
        f[key] = t + e_b * u[key]
    for one, two in (((0, "s", DS), (1, "d", SS)), ((1, "s", SD), (2, "s", DS)), ((0, "s", SD), (2, "d", SS))):
        f[one] = f[two] = e_c * (u[one] + u[two])
    for one, two in (((0, "d", DS), (2, "s", DD)), ((0, "d", SD), (1, "s", DD)), ((1, "d", DS), (2, "d", SD))):
        p = e_d * (u[one] + u[two])
        f[one] = p + e_e * u[one]
        f[two] = p + e_e * u[two]
    triple = ((0, "s", DD), (1, "d", SD), (2, "d", DS))
    q = u[triple[0]] + u[triple[1]] + u[triple[2]]
    for key in triple:
        f[key] = e_f * (u[key] + q)
    for c in range(3):
        f[c, "d", DD] = e_g * u[c, "d", DD]
    return u, f


def z_modes(w):
    out = []
    for p in w:
        out.append([(a + b, b - a) for a, b in zip(p, z_next(p))])
    return out


def y_modes(cur, nxt):
    return [[(s + su, d + du, su - s, du - d) for (s, d), (su, du) in zip(p, q)] for p, q in zip(cur, nxt)]


def rows_above(first):
    return [[tuple(roll(v, -1, 0) for v in pair) for pair in p] for p in first]


def forward_plane(t, groups, load_w):
    first = cur = z_modes(load_w(0))
    for y in range(groups):
        nxt = z_modes(load_w(y + 1)) if y < groups - 1 else rows_above(first)
        for c, p in enumerate(y_modes(cur, nxt)):
            for z, vals in enumerate(p):
                for m, val in enumerate(vals):
                    t[4 * c + m, y, z] = val
        cur = nxt


def finish_rows(low, high):
    res = []
    for one, two in zip(low, high):
        s = [a[0] + b[0] for a, b in zip(one, two)]
        d = [a[1] + b[1] for a, b in zip(one, two)]
        down = [a - b for a, b in zip(s, d)]
        up = z_prev([a + b for a, b in zip(s, d)])
        res.append([a + b for a, b in zip(down, up)])
    return res


def element_plane(t0_ref, t1_ref, c_ref, groups, parts, load_w, load_e, emit, fresh):
    first = cur = z_modes(load_w(0))
    prev = start = None
    for y in range(groups):
        nxt = z_modes(load_w(y + 1)) if y < groups - 1 else rows_above(first)
        t1 = y_modes(cur, nxt)
        low = [[None] * parts for _ in range(3)]
        high = [[None] * parts for _ in range(3)]
        for z in range(parts):
            t0 = [[t0_ref[4 * c + m, y, z] for m in range(4)] for c in range(3)]
            for c in range(3):
                for m in range(4):
                    t1_ref[4 * c + m, y, z] = t1[c][z][m]
            u, f = element_forces(t0, [t1[c][z] for c in range(3)], load_e(y, z))
            for c in range(3):
                g = []
                for m in range(4):
                    d = f[c, "d", m]
                    if not fresh:
                        old = c_ref[4 * c + m, y, z]
                        g.append(old - d if m == SS else old + (f[c, "s", m] - d))
                    c_ref[4 * c + m, y, z] = d if m == SS else f[c, "s", m] + d
                if not fresh:
                    low[c][z] = (g[SS] - g[DS], g[SD] - g[DD])
                    high[c][z] = (g[SS] + g[DS], g[SD] + g[DD])
        if not fresh:
            if y == 0:
                start = low
            else:
                emit(y, finish_rows(low, prev))
            prev = high
        cur = nxt
    if not fresh:
        last = [[tuple(roll(v, 1, 0) for v in pair) for pair in p] for p in prev]
        emit(0, finish_rows(start, last))


def apply_planes(bufs, lo, n, load_w, load_e, emit):
    t_ref, c_ref = bufs
    groups, parts = c_ref.shape[1:3]

    def one(i, a, fresh=False):
        element_plane(
            t_ref.at[a],
            t_ref.at[1 - a],
            c_ref,
            groups,
            parts,
            lambda y: load_w(i + 1, y),
            lambda y, z: load_e(i, y, z),
            lambda y, res: emit(i, y, res),
            fresh,
        )

    forward_plane(t_ref.at[0], groups, lambda y: load_w(lo - 1, y))
    one(lo - 1, 0, True)

    def step(j, carry):
        one(lo + 2 * j, 1)
        one(lo + 2 * j + 1, 0)
        return carry

    lax.fori_loop(0, n // 2, step, 0)


def work_buffers(groups, parts):
    return [pltpu.VMEM((2, 12, groups, parts) + REG, f32), pltpu.VMEM((12, groups, parts) + REG, f32)]


def low_sum(plane):
    plane = [[a + b for a, b in zip(p, z_prev(p))] for p in plane]
    return added(plane, y_prev(plane))


def inverse_diagonal(e_sum, free, scale):
    return jnp.where(free > 0.5, 1.0 / (e_sum * (diag_entry * scale)), 1.0)


def matrix(fun):
    shape = (128, 128)
    r = lax.broadcasted_iota(jnp.int32, shape, 0)
    c = lax.broadcasted_iota(jnp.int32, shape, 1)
    return fun(r, c)


def dot(a, b):
    return jnp.dot(a, b, precision=lax.Precision.HIGHEST, preferred_element_type=f32)


def to_f(cond, val=1.0):
    return jnp.where(cond, f32(val), f32(0.0))


def split_matrix(width):
    def fun(r, c):
        z = r % width
        return to_f(c == r - z + (z % 2) * (width // 2) + z // 2)

    return matrix(fun)


def join_matrix():
    return matrix(lambda r, c: to_f(c == (r % 64) * 2 + r // 64))


def prepare_kernel(density, support, load, vector, own, low, high):
    scaled = density[...].astype(f32) / 255.0
    young = young_floor + (1.0 - young_floor) * scaled * scaled * scaled
    free = 1.0 - support[...].astype(f32)
    masked = free * load[...].astype(f32)
    split = split_matrix(128)
    rows = [young, free] + [masked * vector[c] for c in range(3)]
    for a, val in enumerate(rows):
        val = dot(val.reshape(64, 128), split).reshape(4, 16, 128)
        own[a] = val
        low[a] = val[0:1]
        high[a] = val[2:4]


def join_x_kernel(own, left, right, far_left, far_right, low, high):
    for out, rows in ((low, slice(0, 8)), (high, slice(8, 16))):
        for a in range(5):
            out[a, 0:2] = far_left[a, :, rows]
            out[a, 2:6] = left[a, :, rows]
            out[a, 6:10] = own[a, :, rows]
            out[a, 10:14] = right[a, :, rows]
            out[a, 14:15] = far_right[a, :, rows]


def pack_z_kernel(up, low, high, down, first, last):
    tiles = (up, low, high, down)
    lane = lanes_of() % 64
    for a in range(5):
        for t in range(4):
            acc_first = jnp.zeros(REG, f32)
            acc_last = jnp.zeros(REG, f32)
            for g in range(NXE):
                val = tiles[t][a, g]
                inside = (lane >= 4 * g) & (lane < 4 * g + 4)
                acc_first = jnp.where(inside, roll(val, 4 * g, 1), acc_first)
                acc_last = jnp.where(inside, roll(val, 4 * g - 60, 1), acc_last)
            first[a, 8 * t : 8 * t + 8] = acc_first
            last[a, 8 * t : 8 * t + 8] = acc_last


def first_kernel(up, low, high, down, from_left, from_right, stat, load, dinv, w0, static, sums, nat, rows16, tb, cb):
    lane = lanes_of()
    for a in range(5):
        for g in range(NXE):
            for t, tile in enumerate((up, low, high, down)):
                nat[a, g, 8 * t : 8 * t + 8] = tile[a, g]
    for a in range(5):
        for y in range(4):
            rows = pl.ds(y, 8, stride=4)
            left = from_left[a, rows]
            right = from_right[a, rows]
            for g in range(NXE):
                own = nat[a, g, rows]
                even = jnp.where(lane < 64, own, 0.0)
                even = jnp.where((lane >= 64) & (lane < 68), roll(right, 64 - 4 * g, 1), even)
                even = jnp.where(lane >= 124, roll(left, 124 - 4 * g, 1), even)
                odd = jnp.where(lane < 64, roll(own, 64, 1), 0.0)
                odd = jnp.where((lane >= 64) & (lane < 68), roll(right, -4 * g, 1), odd)
                odd = jnp.where(lane >= 124, roll(left, 60 - 4 * g, 1), odd)
                for z, val in enumerate((even, odd)):
                    if a < 2:
                        stat[a, g, y, z] = val
                    else:
                        load[a - 2, g, y, z] = val

    def diag_step(i, carry):
        total = added(low_sum(get_plane(stat, 0, i)), low_sum(get_plane(stat, 0, jnp.maximum(i - 1, 0))))
        for y in range(4):
            for z in range(2):
                dinv[i, y, z] = inverse_diagonal(total[y][z], stat[1, i, y, z], 1.0)
        return carry

    lax.fori_loop(0, NXE, diag_step, 0)

    def load_w(i, y):
        scaled = [dinv[i, y, z] * stat[1, i, y, z] for z in range(2)]
        return [[load[c, i, y, z] * scaled[z] for z in range(2)] for c in range(3)]

    def emit(i, y, g):
        for z in range(2):
            free = stat[1, i, y, z]
            inv = dinv[i, y, z]
            for c in range(3):
                w0[c, i, y, z] = jnp.where(free > 0.5, g[c][z], load[c, i, y, z] * inv)

    apply_planes((tb, cb), 2, 12, load_w, lambda i, y, z: stat[0, i, y, z], emit)

    sub = lax.broadcasted_iota(jnp.int32, REG, 0)
    own_rows = (sub >= 2) & (sub < 6)

    def masked_sum(val, count):
        return jnp.sum(jnp.where(own_rows & (lane < count), val, 0.0))

    num = jnp.zeros(REG, f32)
    den = jnp.zeros(REG, f32)
    for i in range(6, 10):
        for y in range(4):
            for z in range(2):
                for c in range(3):
                    b = load[c, i, y, z]
                    v = b * dinv[i, y, z]
                    num = num + v * w0[c, i, y, z]
                    den = den + v * b
    totals = [masked_sum(num, 64), masked_sum(den, 64)]

    f1 = [[[stat[1, 2 * k + 4, y, 0]] for y in (0, 2)] for k in range(5)]
    c1 = []
    for k in range(5):
        i = 2 * k + 4
        c1.append([])
        for c in range(3):
            c1[k].append(restrict_plane([get_plane(load, c, j) for j in (i - 1, i, i + 1)], f1[k]))
    y1 = []
    for k in range(6):
        both = added(get_plane(stat, 0, 2 * k + 2), get_plane(stat, 0, 2 * k + 3))
        y1.append([[0.125 * (both[y][0] + both[y][1] + both[y + 1][0] + both[y + 1][1])] for y in (0, 2)])

    def level_sums(nodes, elements, frees, scale, lanes):
        count = len(frees) - 1
        num = jnp.zeros(REG, f32)
        den = jnp.zeros(REG, f32)
        groups = len(frees[0])
        modes = []
        for k in range(count + 1):
            total = added(low_sum(elements[k]), low_sum(elements[k + 1]))
            inv = [inverse_diagonal(total[y][0], frees[k][y][0], scale) for y in range(groups)]
            v = [[nodes[k][c][y][0] * inv[y] for y in range(groups)] for c in range(3)]
            zs = [z_modes([[v[c][y] * frees[k][y][0]] for c in range(3)]) for y in range(groups)]
            zs.append(rows_above(zs[0]))
            modes.append([y_modes(zs[y], zs[y + 1]) for y in range(groups)])
            if k < count:
                for c in range(3):
                    for y in range(groups):
                        num = num + jnp.where(frees[k][y][0] > 0.5, 0.0, v[c][y] * v[c][y])
                        den = den + v[c][y] * nodes[k][c][y][0]
        for k in range(count):
            for y in range(groups):
                u, f = element_forces(
                    [modes[k][y][c][0] for c in range(3)],
                    [modes[k + 1][y][c][0] for c in range(3)],
                    elements[k + 1][y][0] * scale,
                )
                for key in f:
                    num = num + u[key] * f[key]
        return [masked_sum(num, lanes), masked_sum(den, lanes)]

    totals += level_sums(c1[1:4], y1[1:5], f1[1:4], 2.0, 64)

    pick = matrix(lambda r, c: to_f(r == 2 * (c % 64)))
    mean = matrix(lambda r, c: to_f((r == 2 * (c % 64)) | (r == 2 * (c % 64) + 1), 0.5))
    half = matrix(
        lambda r, c: to_f(r == 2 * (c % 64)) + to_f((r == 2 * (c % 64) + 1) | (r == (2 * (c % 64) - 1) % 128), 0.5)
    )
    f2 = [[[dot(f1[k][0][0], pick)]] for k in (1, 3)]
    c2 = []
    for n, k in enumerate((1, 3)):
        c2.append([])
        for c in range(3):
            x = [c1[k][c][y][0] + 0.5 * (c1[k - 1][c][y][0] + c1[k + 1][c][y][0]) for y in range(2)]
            val = x[0] + 0.5 * (x[1] + roll(x[1], 1, 0))
            c2[n].append([[dot(val, half) * f2[n][0][0]]])
    y2 = []
    for k in (0, 2, 4):
        val = 0.25 * (y1[k][0][0] + y1[k][1][0] + y1[k + 1][0][0] + y1[k + 1][1][0])
        y2.append([[dot(val, mean)]])
    totals += level_sums(c2, y2, f2, 4.0, 32)

    row = lax.broadcasted_iota(jnp.int32, REG, 0)
    out = jnp.zeros(REG, f32)
    for k, total in enumerate(totals):
        out = jnp.where(row == k, total, out)
    for n in range(32):
        sums[n] = out

    for n, planes in enumerate((y1[2:4], f1[1:3])):
        static[n] = side_by_side(planes, rows16)


def restrict_plane(planes, free=None):
    low, mid, high = planes
    x = [[b + 0.5 * (a + c) for a, b, c in zip(*p)] for p in zip(low, mid, high)]
    y = []
    for n in range(2):
        below = [roll(v, 1, 0) for v in x[3]] if n == 0 else x[1]
        y.append([b + 0.5 * (a + c) for a, b, c in zip(below, x[2 * n], x[2 * n + 1])])
    out = []
    for n in range(2):
        even, odd = y[n]
        val = even + 0.5 * (odd + roll(odd, 1, 1))
        out.append([val if free is None else val * free[n][0]])
    return out


def side_by_side(planes, rows16):
    vals = []
    for n, plane in enumerate(planes):
        for y in range(2):
            rows16[n, pl.ds(y, 8, stride=2)] = plane[y][0]
        vals.append(rows16[n, 4:12])
    return jnp.where(lanes_of() < 64, vals[0], roll(vals[1], 64, 1))


def second_kernel(stat, dinv, w0, w1, w2, full, tb, cb):
    def run(src, lo, n, dst):
        def load_w(i, y):
            scaled = [dinv[i, y, z] * stat[1, i, y, z] for z in range(2)]
            return [[src[c, i, y, z] * scaled[z] for z in range(2)] for c in range(3)]

        def emit(i, y, g):
            for z in range(2):
                free = stat[1, i, y, z]
                inv = dinv[i, y, z]
                for c in range(3):
                    dst(c, i, y, z, jnp.where(free > 0.5, g[c][z], src[c, i, y, z] * inv))

        apply_planes((tb, cb), lo, n, load_w, lambda i, y, z: stat[0, i, y, z], emit)

    def put_full(c, i, y, z, val):
        full[c, i, y, z] = val

    def put_last(c, i, y, z, val):
        w2[c, i - 4, y, z] = val

    run(w0, 3, 10, put_full)
    run(full, 4, 8, put_last)
    for c in range(3):
        for k in range(8):
            w1[c, k] = full[c, k + 4]


def estimate_of(parts, level):
    sums = parts[0]
    for n in range(1, 8):
        sums = sums + parts[n]
    return jnp.max(sums[2 * level : 2 * level + 1, :] / sums[2 * level + 1 : 2 * level + 2, :])


def polynomial():
    theta, delta = centre_share, half_share
    sigma = theta / delta
    rho0 = 1.0 / sigma
    rho1 = 1.0 / (2.0 * sigma - rho0)
    rho2 = 1.0 / (2.0 * sigma - rho1)
    a10 = rho1 * rho0 / theta + 2.0 * rho1 / delta
    a11 = -2.0 * rho1 / (delta * theta)
    a20 = rho2 * rho1 * a10 + 2.0 * rho2 / delta
    a21 = rho2 * rho1 * a11 - (2.0 * rho2 / delta) * (1.0 / theta + a10)
    a22 = -(2.0 * rho2 / delta) * a11
    return 1.0 / theta + a10 + a20, a11 + a21, a22


def turns():
    sigma = centre_share / half_share
    rho = 1.0 / sigma
    out = []
    for _ in range(2):
        new = 1.0 / (2.0 * sigma - rho)
        out.append((new * rho, 2.0 * new / half_share))
        rho = new
    return out


def third_kernel(sums, load, dinv, w0, w1, w2, static, res, pre, pack, rows16):
    inv = 1.0 / estimate_of(sums, 0)
    k0, k1, k2 = polynomial()
    b0 = k0 * inv
    b1 = k1 * inv * inv
    b2 = k2 * inv * inv * inv

    def step(k, carry):
        for c in range(3):
            res[c, k] = load[c, k + 4] - (b0 * w0[c, k + 4] + b1 * w1[c, k] + b2 * w2[c, k])
        return carry

    lax.fori_loop(0, 8, step, 0)
    for k in range(4):
        for c in range(3):
            pre[c, k] = dinv[k + 6] * (b0 * load[c, k + 6] + b1 * w0[c, k + 6] + b2 * w1[c, k + 2])
    parts = [static[0], static[1]]
    for c in range(3):
        planes = [restrict_plane([get_plane(res, c, j) for j in (i - 1, i, i + 1)]) for i in (2, 4)]
        parts.append(side_by_side(planes, rows16.at[c]) * static[1])
    split = dot(jnp.concatenate(parts, axis=0), split_matrix(64))
    for a in range(5):
        pack[a] = split[8 * a : 8 * a + 8]


def join_chips_kernel(mine, right, opposite, left, out):
    lane = lanes_of()
    for r, (near, far) in enumerate(((mine, opposite), (right, left))):
        for k in range(2):
            for a in range(5):
                one, two = near[k, a], far[k, a]
                out[a, 4 * r + 2 * k] = jnp.where(lane < 64, one, roll(two, 64, 1))
                out[a, 4 * r + 2 * k + 1] = jnp.where(lane < 64, roll(one, 64, 1), two)


def pack_coarse_kernel(t0, t1, t2, t3, t4, first, last):
    lane = lanes_of() % 64
    for t, tile in enumerate((t0, t1, t2, t3, t4)):
        for a in range(5):
            acc = [jnp.zeros(REG, f32) for _ in range(4)]
            for i in range(8):
                val = tile[a, i]
                inside = (lane >= 8 * i) & (lane < 8 * i + 8)
                for n, start in enumerate((0, 32, 24, 56)):
                    acc[n] = jnp.where(inside, roll(val, 8 * i - start, 1), acc[n])
            for z in range(2):
                first[t, a, z] = acc[z]
                last[t, a, z] = acc[2 + z]


def wrap(ref, planes, *at):
    for y in range(ref.shape[-4]):
        for z in range(ref.shape[-3]):
            ref[at + (0, y, z)] = roll(ref[at + (planes, y, z)], 64, 1)
            ref[at + (planes + 1, y, z)] = roll(ref[at + (1, y, z)], 64, 1)


def smooth(bufs, planes, young, free, dinv, res, x, inv, steps):
    groups, parts = res.shape[-4:-2]
    for src, dst, keep, gain in steps:

        def load_w(i, y, src=src):
            mask = [free[i + 1, y, z] for z in range(parts)]
            return [[src[c, i + 1, y, z] * mask[z] for z in range(parts)] for c in range(3)]

        def emit(i, y, g, src=src, dst=dst, keep=keep, gain=gain):
            for z in range(parts):
                mask = free[i + 1, y, z]
                scaled = None if dst is None else (gain * inv) * dinv[i, y, z]
                for c in range(3):
                    d = src[c, i + 1, y, z]
                    left = res[c, i, y, z] - jnp.where(mask > 0.5, g[c][z], d)
                    res[c, i, y, z] = left
                    if dst is not None:
                        new = keep * d + scaled * left if keep else scaled * left
                        dst[c, i + 1, y, z] = new
                        x[c, i, y, z] = x[c, i, y, z] + new

        apply_planes(bufs, 0, planes, load_w, lambda i, y, z: young[i + 1, y, z], emit)
        if dst is not None:
            for c in range(3):
                wrap(dst, planes, c)


def coarse_kernel(
    sums, core, t0, t1, t2, t3, t4, from_left, from_right, out,
    nat, young, free, dinv, res, d_a, d_b, x,
    nat2, young2, free2, dinv2, res2, d2_a, d2_b, x2,
    nat3, young3, free3, dinv3, res3, x3, rows_e, rows_o,
    tb, cb, tb2, cb2, tb3, cb3,
):
    lane = lanes_of()
    in_half = lane % 64
    for t, tile in enumerate((t0, t1, t2, t3, t4)):
        for a in range(5):
            for i in range(8):
                val = tile[a, i]
                for z in range(2):
                    here = jnp.where((in_half >= 8) & (in_half < 40), roll(val, 8 - 32 * z, 1), 0.0)
                    right = roll(from_right[t, a, z], 40 - 8 * i, 1)
                    left = roll(from_left[t, a, z], -8 * i, 1)
                    here = jnp.where((in_half >= 40) & (in_half < 48), right, here)
                    nat[a, i, z, 8 * t : 8 * t + 8] = jnp.where(in_half < 8, left, here)
    for i in range(8):
        for y in range(5):
            rows = pl.ds(y, 8, stride=5)
            for z in range(2):
                young[i + 1, y, z] = 2.0 * nat[0, i, z, rows]
                free[i + 1, y, z] = nat[1, i, z, rows]
                for c in range(3):
                    res[c, i, y, z] = nat[2 + c, i, z, rows]
    wrap(young, 8)
    wrap(free, 8)

    inv1 = 1.0 / estimate_of(sums, 1)
    inv2 = 1.0 / estimate_of(sums, 2)
    start = 1.0 / centre_share
    later = turns()

    def begin(i, carry):
        total = added(low_sum(get_plane(young, i + 1)), low_sum(get_plane(young, i)))
        for y in range(5):
            for z in range(2):
                inverse = inverse_diagonal(total[y][z], free[i + 1, y, z], 1.0)
                dinv[i, y, z] = inverse
                for c in range(3):
                    d = (start * inv1) * inverse * res[c, i, y, z]
                    d_a[c, i + 1, y, z] = d
                    x[c, i, y, z] = d
        return carry

    lax.fori_loop(0, 8, begin, 0)
    for c in range(3):
        wrap(d_a, 8, c)
    steps = [(d_a, d_b) + later[0], (d_b, d_a) + later[1], (d_a, None, 0.0, 0.0)]
    smooth((tb, cb), 8, young, free, dinv, res, x, inv1, steps)

    for a in range(5):
        for k in range(4):
            nat2[a, k, 0:8] = jnp.zeros(REG, f32)
            nat2[a, k, 48:56] = jnp.zeros(REG, f32)
    for k in range(4):
        for y in range(5):
            rows = pl.ds(8 + y, 8, stride=5)
            both = [young[2 * k + 1, y, z] + young[2 * k + 2, y, z] for z in range(2)]
            nat2[0, k, rows] = both[0] + both[1]
            nat2[1, k, rows] = free[2 * k + 1, y, 0]
            for c in range(3):
                part = []
                for z in range(2):
                    below = res[c, 2 * k - 1, y, z] if k else roll(res[c, 7, y, z], 64, 1)
                    part.append(res[c, 2 * k, y, z] + 0.5 * (below + res[c, 2 * k + 1, y, z]))
                nat2[2 + c, k, rows] = part[0] + 0.5 * (part[1] + roll(part[1], 1, 1))
        for y in range(3):
            at = [pl.ds(8 + 2 * y + n, 8, stride=6) for n in (-1, 0, 1)]
            young2[k + 1, y, 0] = 0.25 * (nat2[0, k, at[1]] + nat2[0, k, at[2]])
            mask = nat2[1, k, at[1]]
            free2[k + 1, y, 0] = mask
            for c in range(3):
                val = nat2[2 + c, k, at[1]] + 0.5 * (nat2[2 + c, k, at[0]] + nat2[2 + c, k, at[2]])
                res2[c, k, y, 0] = val * mask
    wrap(young2, 4)
    wrap(free2, 4)
    for k in range(4):
        total = added(low_sum(get_plane(young2, k + 1)), low_sum(get_plane(young2, k)))
        for y in range(3):
            inverse = inverse_diagonal(total[y][0], free2[k + 1, y, 0], 1.0)
            dinv2[k, y, 0] = inverse
            for c in range(3):
                d = (start * inv2) * inverse * res2[c, k, y, 0]
                d2_a[c, k + 1, y, 0] = d
                x2[c, k, y, 0] = d
    for c in range(3):
        wrap(d2_a, 4, c)
    steps = [(d2_a, d2_b) + later[0], (d2_b, d2_a) + later[1]]
    smooth((tb2, cb2), 4, young2, free2, dinv2, res2, x2, inv2, steps)

    for i in range(8):
        for z in range(2):
            for y in range(5):
                rows = pl.ds(y, 8, stride=5)
                nat[0, i, z, rows] = dinv[i, y, z]
                for c in range(3):
                    nat[1 + c, i, z, rows] = res[c, i, y, z]
            for y in range(3):
                rows = pl.ds(8 + y, 8, stride=3)
                dinv3[i, y, z] = nat[0, i, z, rows]
                for c in range(3):
                    res3[c, i, y, z] = nat[1 + c, i, z, rows]
    for i in range(8):
        for z in range(2):
            for y in range(5):
                rows = pl.ds(y, 8, stride=5)
                nat[0, i, z, rows] = young[i + 1, y, z]
                nat[1, i, z, rows] = free[i + 1, y, z]
                for c in range(3):
                    nat[2 + c, i, z, rows] = x[c, i, y, z]
            for y in range(3):
                rows = pl.ds(8 + y, 8, stride=3)
                young3[i + 1, y, z] = nat[0, i, z, rows]
                free3[i + 1, y, z] = nat[1, i, z, rows]
                for c in range(3):
                    x3[c, i, y, z] = nat[2 + c, i, z, rows]
    wrap(young3, 8)
    wrap(free3, 8)
    d3_a, d3_b = d_a, d_b
    for c in range(3):
        for k in range(4):
            here = [x2[c, k, y, 0] for y in range(3)]
            if k < 3:
                nxt = [x2[c, k + 1, y, 0] for y in range(3)]
            else:
                nxt = [roll(x2[c, 0, y, 0], 64, 1) for y in range(3)]
            for n, val in enumerate((here, [0.5 * (p + q) for p, q in zip(here, nxt)])):
                above = val[1:] + [roll(val[0], -1, 0)]
                for y in range(3):
                    nat3[n, pl.ds(2 * y, 8, stride=6)] = val[y]
                    nat3[n, pl.ds(2 * y + 1, 8, stride=6)] = 0.5 * (val[y] + above[y])
                i = 2 * k + n
                for y in range(3):
                    even = nat3[n, pl.ds(8 + y, 8, stride=3)]
                    odd = 0.5 * (even + roll(even, -1, 1))
                    for z, e in enumerate((even, odd)):
                        e = e * free3[i + 1, y, z]
                        d3_b[c, i + 1, y, z] = e
                        x3[c, i, y, z] = x3[c, i, y, z] + e
        wrap(d3_b, 8, c)
    steps = [(d3_b, d3_a, 0.0, start), (d3_a, d3_b) + later[0], (d3_b, d3_a) + later[1]]
    smooth((tb3, cb3), 8, young3, free3, dinv3, res3, x3, inv1, steps)

    place = 2 * core[0]
    for k in range(6):
        plane = (place + (14 + k)) & 15
        i = plane & 7
        swap = plane > 7
        for c in range(3):
            for y in range(3):
                rows = pl.ds(24 * (3 * k + c) + y, 8, stride=3)
                for z, dst in enumerate((rows_e, rows_o)):
                    val = x3[c, i, y, z]
                    dst[rows] = jnp.where(swap, roll(val, 64, 1), val)
    place_e = matrix(lambda r, c: to_f((r < 48) & (c == (2 * r + 112) % 128)))
    place_o = matrix(lambda r, c: to_f((r < 48) & (c == (2 * r + 113) % 128)))
    out[...] = (dot(rows_e[...], place_e) + dot(rows_o[...], place_o)).reshape(6, 3, 24, 128)


def last_kernel(sums, stat, dinv, res_in, pre, x1, out, e0, res, d_a, d_b, rows, tb, cb):
    inv = 1.0 / estimate_of(sums, 0)
    start = 1.0 / centre_share
    later = turns()

    def raised(c, k):
        at = [x1[k, c, pl.ds(4 + n, 8, stride=2)] for n in range(3)]
        groups = [at[0], 0.5 * (at[0] + at[1]), at[1], 0.5 * (at[1] + at[2])]
        return [[v, 0.5 * (v + roll(v, -1, 1))] for v in groups]

    for c in range(3):
        here = raised(c, 0)
        for k in range(6):
            nxt = raised(c, k + 1) if k < 5 else None
            for y in range(4):
                for z in range(2):
                    e0[c, 2 * k, y, z] = here[y][z] * stat[1, 2 * k + 2, y, z]
                    if k < 5:
                        e0[c, 2 * k + 1, y, z] = 0.5 * (here[y][z] + nxt[y][z]) * stat[1, 2 * k + 3, y, z]
            here = nxt

    def loader(ref, shift):
        def load_w(i, y):
            mask = [stat[1, i, y, z] for z in range(2)]
            return [[ref[c, i - shift, y, z] * mask[z] for z in range(2)] for c in range(3)]

        return load_w

    def emit_e(i, y, g):
        for z in range(2):
            mask = stat[1, i, y, z]
            scaled = (start * inv) * dinv[i, y, z]
            for c in range(3):
                left = res_in[c, i - 4, y, z] - jnp.where(mask > 0.5, g[c][z], e0[c, i - 2, y, z])
                res[c, i - 4, y, z] = left
                d_a[c, i - 4, y, z] = scaled * left

    def emit_a(i, y, g):
        keep, gain = later[0]
        for z in range(2):
            mask = stat[1, i, y, z]
            scaled = (gain * inv) * dinv[i, y, z]
            for c in range(3):
                d = d_a[c, i - 4, y, z]
                left = res[c, i - 4, y, z] - jnp.where(mask > 0.5, g[c][z], d)
                res[c, i - 4, y, z] = left
                d_b[c, i - 4, y, z] = keep * d + scaled * left

    def emit_b(i, y, g):
        keep, gain = later[1]
        total = [[None, None] for _ in range(3)]
        for z in range(2):
            mask = stat[1, i, y, z]
            scaled = (gain * inv) * dinv[i, y, z]
            for c in range(3):
                d = d_b[c, i - 4, y, z]
                left = res[c, i - 4, y, z] - jnp.where(mask > 0.5, g[c][z], d)
                new = keep * d + scaled * left
                old = pre[c, i - 6, y, z] + e0[c, i - 2, y, z] + d_a[c, i - 4, y, z]
                total[c][z] = old + d + new
        for c in range(3):
            val = jnp.where(lanes_of() < 64, total[c][0], roll(total[c][1], 64, 1))
            rows[c, i - 6, pl.ds(y, 8, stride=4)] = val

    young = lambda i, y, z: stat[0, i, y, z]
    apply_planes((tb, cb), 4, 8, loader(e0, 2), young, emit_e)
    apply_planes((tb, cb), 5, 6, loader(d_a, 4), young, emit_a)
    apply_planes((tb, cb), 6, 4, loader(d_b, 4), young, emit_b)
    join = join_matrix()
    for c in range(3):
        for k in range(4):
            out[c, k] = dot(rows[c, k, 8:24], join)


def call(kernel, outs, scratch=(), smem=None, flops=0, limit=12, plain_in=False, plain_out=False):
    def run(*args):
        specs = [pl.BlockSpec(memory_space=pltpu.SMEM if n == smem else pltpu.VMEM) for n in range(len(args))]
        if not plain_in:
            args = [a if n == smem else pltpu.with_memory_space_constraint(a, pltpu.VMEM) for n, a in enumerate(args)]
        return pl.pallas_call(
            kernel,
            in_specs=specs,
            out_specs=[pl.BlockSpec(memory_space=pltpu.VMEM) for _ in outs],
            out_shape=[jax.ShapeDtypeStruct(s, f32) if plain_out else pltpu.VMEM(s, f32) for s in outs],
            scratch_shapes=[s if not isinstance(s, tuple) else pltpu.VMEM(s, f32) for s in scratch],
            compiler_params=pltpu.CompilerParams(vmem_limit_bytes=limit * 1024 * 1024),
            cost_estimate=pl.CostEstimate(flops=flops, bytes_accessed=1 << 20, transcendentals=0),
        )(*args)

    return run


def send(value, axis, shift):
    count = lax.axis_size(axis)
    return lax.ppermute(value, axis, [(i, (i + shift) % count) for i in range(count)])


def swap_core(value):
    return lax.ppermute(value, "gx", [(i, i ^ 1) for i in range(lax.axis_size("gx"))])


def sum_kernel(parts, out):
    total = parts[0]
    for n in range(1, parts.shape[0]):
        total = total + parts[n]
    for n in range(out.shape[0]):
        out[n] = total


def total_of(sums):
    parts = lax.all_to_all(sums, ("gx", "gz"), 0, 0)
    return lax.all_to_all(call(sum_kernel, [(8,) + REG])(parts)[0], "gy", 0, 0)


def local(density_level, support_mask, load_mask, load_vector):
    own, low, high = call(prepare_kernel, [(5, 4, 16, 128), (5, 1, 16, 128), (5, 2, 16, 128)], plain_in=True)(
        density_level, support_mask, load_mask, load_vector
    )
    left, right = send(own, "gx", 1), send(own, "gx", -1)
    far_left, far_right = send(high, "gx", 2), send(low, "gx", -2)
    low, high = call(join_x_kernel, [(5, NXE, 8, 128)] * 2)(own, left, right, far_left, far_right)
    up, down = send(high, "gy", 1), send(low, "gy", -1)
    first, last = call(pack_z_kernel, [(5, 32, 128)] * 2)(up, low, high, down)
    from_left, from_right = send(last, "gz", 1), send(first, "gz", -1)
    fine = (4, 2) + REG
    stat, load, dinv, w0, static, sums = call(
        first_kernel,
        [(2, NXE) + fine, (3, NXE) + fine, (NXE,) + fine, (3, NXE) + fine, (2,) + REG, (32,) + REG],
        [(5, NXE, 32, 128), (2, 16, 128)] + work_buffers(4, 2),
    )(up, low, high, down, from_left, from_right)
    w1, w2 = call(second_kernel, [(3, 8) + fine] * 2, [(3, NXE) + fine] + work_buffers(4, 2), flops=1 << 26)(
        stat, dinv, w0
    )
    sums = total_of(sums)
    res, pre, pack = call(third_kernel, [(3, 8) + fine, (3, 4) + fine, (5,) + REG], [(3, 2, 16, 128)])(
        sums, load, dinv, w0, w1, w2, static
    )
    core = lax.axis_index("gx") & 1
    other = swap_core(pack)
    pair = jnp.stack([jnp.where(core == 0, pack, other), jnp.where(core == 0, other, pack)])
    chips = call(join_chips_kernel, [(5, 8) + REG])(
        pair, send(pair, "gx", -2), send(pair, "gx", 4), send(pair, "gx", 2)
    )[0]
    tiles = [send(chips, "gy", 2), send(chips, "gy", 1), chips, send(chips, "gy", -1), send(chips, "gy", -2)]
    first, last = call(pack_coarse_kernel, [(5, 5, 2) + REG] * 2)(*tiles)
    from_left, from_right = send(last, "gz", 1), send(first, "gz", -1)
    five, three, one = (5, 2) + REG, (3, 2) + REG, (3, 1) + REG
    x1 = call(
        coarse_kernel,
        [(6, 3, 24, 128)],
        [(5, 8, 2, 40, 128), (10,) + five, (10,) + five, (8,) + five]
        + [(3, 8) + five, (3, 10) + five, (3, 10) + five, (3, 8) + five]
        + [(5, 4, 56, 128), (6,) + one, (6,) + one, (4,) + one]
        + [(3, 4) + one, (3, 6) + one, (3, 6) + one, (3, 4) + one]
        + [(2, 48, 128), (10,) + three, (10,) + three, (8,) + three]
        + [(3, 8) + three, (3, 8) + three, (432, 128), (432, 128)]
        + work_buffers(5, 2)
        + work_buffers(3, 1)
        + work_buffers(3, 2),
        smem=1,
        limit=28,
    )(sums, core.reshape(1).astype(jnp.int32), *tiles, from_left, from_right)[0]
    return call(
        last_kernel,
        [(3, 4, 16, 128)],
        [(3, 12) + fine, (3, 8) + fine, (3, 8) + fine, (3, 8) + fine, (3, 4, 32, 128)] + work_buffers(4, 2),
        plain_out=True,
    )(sums, stat, dinv, res, pre, x1)[0]


def solution(mesh):
    block = P("gx", "gy", "gz")
    return jax.shard_map(
        local,
        mesh=mesh,
        in_specs=(block, block, block, P(None, "gx", "gy", "gz")),
        out_specs=P(None, "gx", "gy", "gz"),
        check_vma=False,
    )
```

```python
import jax
import jax.numpy as jnp
from jax import lax
from jax.experimental import pallas as pl
from jax.experimental.pallas import tpu as pltpu
from jax.sharding import PartitionSpec as P

f32 = jnp.float32
young_floor = 0.001
poisson = 0.3
headroom = 1.5
floor_share = 0.3
lam = poisson / ((1.0 + poisson) * (1.0 - 2.0 * poisson))
mu = 1.0 / (2.0 * (1.0 + poisson))
diag_entry = (lam + 2 * mu + 2 * mu) / 16 + (2 * (lam + 3 * mu) + 2 * mu) / 48 + (lam + 4 * mu) / 144
centre_share = 0.5 * headroom * (1.0 + floor_share)
half_share = 0.5 * headroom * (1.0 - floor_share)

NXE = 15
SS, SD, DS, DD = 0, 1, 2, 3
REG = (8, 128)


def roll(v, amount, axis):
    return pltpu.roll(v, amount % v.shape[axis], axis=axis)


def lanes_of(shape=REG):
    return lax.broadcasted_iota(jnp.int32, shape, 1)


def z_next(p):
    return [p[1], roll(p[0], -1, 1)] if len(p) == 2 else [roll(p[0], -1, 1)]


def z_prev(p):
    return [roll(p[1], 1, 1), p[0]] if len(p) == 2 else [roll(p[0], 1, 1)]


def y_next(plane):
    return plane[1:] + [[roll(v, -1, 0) for v in plane[0]]]


def y_prev(plane):
    return [[roll(v, 1, 0) for v in plane[-1]]] + plane[:-1]


def added(one, two):
    return [[a + b for a, b in zip(p, q)] for p, q in zip(one, two)]


def get_plane(ref, *at):
    groups, parts = ref.shape[-4:-2]
    return [[ref[at + (y, z)] for z in range(parts)] for y in range(groups)]


def element_forces(t0, t1, e):
    u = {}
    for c in range(3):
        for m in range(4):
            u[c, "d", m] = t1[c][m] - t0[c][m]
            if m != SS:
                u[c, "s", m] = t1[c][m] + t0[c][m]
    f = {}
    e_a, e_b, e_c = e * (lam / 16), e * (2 * mu / 16), e * (mu / 16)
    e_d, e_e, e_f = e * (lam / 48), e * (3 * mu / 48), e * (mu / 48)
    e_g = e * ((lam + 4 * mu) / 144)
    normal = ((0, "d", SS), (1, "s", DS), (2, "s", SD))
    t = e_a * (u[normal[0]] + u[normal[1]] + u[normal[2]])
    for key in normal:
        f[key] = t + e_b * u[key]
    for one, two in (((0, "s", DS), (1, "d", SS)), ((1, "s", SD), (2, "s", DS)), ((0, "s", SD), (2, "d", SS))):
        f[one] = f[two] = e_c * (u[one] + u[two])
    for one, two in (((0, "d", DS), (2, "s", DD)), ((0, "d", SD), (1, "s", DD)), ((1, "d", DS), (2, "d", SD))):
        p = e_d * (u[one] + u[two])
        f[one] = p + e_e * u[one]
        f[two] = p + e_e * u[two]
    triple = ((0, "s", DD), (1, "d", SD), (2, "d", DS))
    q = u[triple[0]] + u[triple[1]] + u[triple[2]]
    for key in triple:
        f[key] = e_f * (u[key] + q)
    for c in range(3):
        f[c, "d", DD] = e_g * u[c, "d", DD]
    return u, f


def z_modes(w):
    out = []
    for p in w:
        out.append([(a + b, b - a) for a, b in zip(p, z_next(p))])
    return out


def y_modes(cur, nxt):
    return [[(s + su, d + du, su - s, du - d) for (s, d), (su, du) in zip(p, q)] for p, q in zip(cur, nxt)]


def rows_above(first):
    return [[tuple(roll(v, -1, 0) for v in pair) for pair in p] for p in first]


def forward_plane(t, groups, load_w):
    first = cur = z_modes(load_w(0))
    for y in range(groups):
        nxt = z_modes(load_w(y + 1)) if y < groups - 1 else rows_above(first)
        for c, p in enumerate(y_modes(cur, nxt)):
            for z, vals in enumerate(p):
                for m, val in enumerate(vals):
                    t[4 * c + m, y, z] = val
        cur = nxt


def finish_rows(low, high):
    res = []
    for one, two in zip(low, high):
        s = [a[0] + b[0] for a, b in zip(one, two)]
        d = [a[1] + b[1] for a, b in zip(one, two)]
        down = [a - b for a, b in zip(s, d)]
        up = z_prev([a + b for a, b in zip(s, d)])
        res.append([a + b for a, b in zip(down, up)])
    return res


def element_plane(t0_ref, t1_ref, c_ref, groups, parts, load_w, load_e, emit, fresh):
    first = cur = z_modes(load_w(0))
    prev = start = None
    for y in range(groups):
        nxt = z_modes(load_w(y + 1)) if y < groups - 1 else rows_above(first)
        t1 = y_modes(cur, nxt)
        low = [[None] * parts for _ in range(3)]
        high = [[None] * parts for _ in range(3)]
        for z in range(parts):
            t0 = [[t0_ref[4 * c + m, y, z] for m in range(4)] for c in range(3)]
            for c in range(3):
                for m in range(4):
                    t1_ref[4 * c + m, y, z] = t1[c][z][m]
            u, f = element_forces(t0, [t1[c][z] for c in range(3)], load_e(y, z))
            for c in range(3):
                g = []
                for m in range(4):
                    d = f[c, "d", m]
                    if not fresh:
                        old = c_ref[4 * c + m, y, z]
                        g.append(old - d if m == SS else old + (f[c, "s", m] - d))
                    c_ref[4 * c + m, y, z] = d if m == SS else f[c, "s", m] + d
                if not fresh:
                    low[c][z] = (g[SS] - g[DS], g[SD] - g[DD])
                    high[c][z] = (g[SS] + g[DS], g[SD] + g[DD])
        if not fresh:
            if y == 0:
                start = low
            else:
                emit(y, finish_rows(low, prev))
            prev = high
        cur = nxt
    if not fresh:
        last = [[tuple(roll(v, 1, 0) for v in pair) for pair in p] for p in prev]
        emit(0, finish_rows(start, last))


def apply_planes(bufs, lo, n, load_w, load_e, emit):
    t_ref, c_ref = bufs
    groups, parts = c_ref.shape[1:3]

    def one(i, a, fresh=False):
        element_plane(
            t_ref.at[a],
            t_ref.at[1 - a],
            c_ref,
            groups,
            parts,
            lambda y: load_w(i + 1, y),
            lambda y, z: load_e(i, y, z),
            lambda y, res: emit(i, y, res),
            fresh,
        )

    forward_plane(t_ref.at[0], groups, lambda y: load_w(lo - 1, y))
    one(lo - 1, 0, True)

    def step(j, carry):
        one(lo + 2 * j, 1)
        one(lo + 2 * j + 1, 0)
        return carry

    lax.fori_loop(0, n // 2, step, 0)


def work_buffers(groups, parts):
    return [pltpu.VMEM((2, 12, groups, parts) + REG, f32), pltpu.VMEM((12, groups, parts) + REG, f32)]


def low_sum(plane):
    plane = [[a + b for a, b in zip(p, z_prev(p))] for p in plane]
    return added(plane, y_prev(plane))


def inverse_diagonal(e_sum, free, scale):
    return jnp.where(free > 0.5, 1.0 / (e_sum * (diag_entry * scale)), 1.0)


def matrix(fun):
    shape = (128, 128)
    r = lax.broadcasted_iota(jnp.int32, shape, 0)
    c = lax.broadcasted_iota(jnp.int32, shape, 1)
    return fun(r, c)


def dot(a, b):
    return jnp.dot(a, b, precision=lax.Precision.HIGHEST, preferred_element_type=f32)


def to_f(cond, val=1.0):
    return jnp.where(cond, f32(val), f32(0.0))


def split_matrix(width):
    def fun(r, c):
        z = r % width
        return to_f(c == r - z + (z % 2) * (width // 2) + z // 2)

    return matrix(fun)


def join_matrix():
    return matrix(lambda r, c: to_f(c == (r % 64) * 2 + r // 64))


def prepare_kernel(density, support, load, vector, low, high, a_buf, b_buf, c_buf, v_buf, sem):
    copies = []
    for n, (src, dst) in enumerate(((density, a_buf), (support, b_buf), (load, c_buf), (vector, v_buf))):
        copies.append(pltpu.make_async_copy(src, dst, sem.at[n]))
        copies[-1].start()
    for copy in copies:
        copy.wait()
    scaled = a_buf[...].astype(f32) / 255.0
    young = young_floor + (1.0 - young_floor) * scaled * scaled * scaled
    free = 1.0 - b_buf[...].astype(f32)
    masked = free * c_buf[...].astype(f32)
    split = split_matrix(128)
    rows = [young, free] + [masked * v_buf[c] for c in range(3)]
    for a, val in enumerate(rows):
        val = dot(val.reshape(64, 128), split).reshape(4, 16, 128)
        low[a] = val[:, 0:8]
        high[a] = val[:, 8:16]


def join_y_kernel(up, low, high, down, own, first, last):
    for t, tile in enumerate((up, low, high, down)):
        rows = slice(8 * t, 8 * t + 8)
        for a in range(5):
            own[a, :, rows] = tile[a]
            first[a, :, rows] = tile[a, 0:1]
            last[a, :, rows] = tile[a, 2:4]


def plane_refs(far_left, left, own, right, far_right):
    return [(ref, k) for ref, n in ((far_left, 2), (left, 4), (own, 4), (right, 4), (far_right, 1)) for k in range(n)]


def pack_z_kernel(far_left, left, own, right, far_right, first, last):
    planes = plane_refs(far_left, left, own, right, far_right)
    lane = lanes_of() % 64
    for a in range(5):
        for t in range(4):
            acc_first = jnp.zeros(REG, f32)
            acc_last = jnp.zeros(REG, f32)
            for g in range(NXE):
                ref, k = planes[g]
                val = ref[a, k, 8 * t : 8 * t + 8]
                inside = (lane >= 4 * g) & (lane < 4 * g + 4)
                acc_first = jnp.where(inside, roll(val, 4 * g, 1), acc_first)
                acc_last = jnp.where(inside, roll(val, 4 * g - 60, 1), acc_last)
            first[a, 8 * t : 8 * t + 8] = acc_first
            last[a, 8 * t : 8 * t + 8] = acc_last


def first_kernel(
    far_left, left, mid, right, far_right, from_left, from_right,
    stat, load_out, dinv, w0, static, sums, load, rows16, tb, cb, sem,
):
    lane = lanes_of()
    planes = plane_refs(far_left, left, mid, right, far_right)
    for a in range(5):
        for y in range(4):
            rows = pl.ds(y, 8, stride=4)
            left = from_left[a, rows]
            right = from_right[a, rows]
            for g in range(NXE):
                ref, k = planes[g]
                own = ref[a, k, rows]
                even = jnp.where(lane < 64, own, 0.0)
                even = jnp.where((lane >= 64) & (lane < 68), roll(right, 64 - 4 * g, 1), even)
                even = jnp.where(lane >= 124, roll(left, 124 - 4 * g, 1), even)
                odd = jnp.where(lane < 64, roll(own, 64, 1), 0.0)
                odd = jnp.where((lane >= 64) & (lane < 68), roll(right, -4 * g, 1), odd)
                odd = jnp.where(lane >= 124, roll(left, 60 - 4 * g, 1), odd)
                for z, val in enumerate((even, odd)):
                    if a < 2:
                        stat[a, g, y, z] = val
                    else:
                        load[a - 2, g, y, z] = val
    copy = pltpu.make_async_copy(load, load_out, sem)
    copy.start()

    def diag_step(i, carry):
        total = added(low_sum(get_plane(stat, 0, i)), low_sum(get_plane(stat, 0, jnp.maximum(i - 1, 0))))
        for y in range(4):
            for z in range(2):
                dinv[i, y, z] = inverse_diagonal(total[y][z], stat[1, i, y, z], 1.0)
        return carry

    lax.fori_loop(0, NXE, diag_step, 0)

    def load_w(i, y):
        scaled = [dinv[i, y, z] * stat[1, i, y, z] for z in range(2)]
        return [[load[c, i, y, z] * scaled[z] for z in range(2)] for c in range(3)]

    def emit(i, y, g):
        for z in range(2):
            free = stat[1, i, y, z]
            inv = dinv[i, y, z]
            for c in range(3):
                w0[c, i, y, z] = jnp.where(free > 0.5, g[c][z], load[c, i, y, z] * inv)

    apply_planes((tb, cb), 2, 12, load_w, lambda i, y, z: stat[0, i, y, z], emit)

    sub = lax.broadcasted_iota(jnp.int32, REG, 0)
    own_rows = (sub >= 2) & (sub < 6)

    def masked_sum(val, count):
        return jnp.sum(jnp.where(own_rows & (lane < count), val, 0.0))

    num = jnp.zeros(REG, f32)
    den = jnp.zeros(REG, f32)
    for i in range(6, 10):
        for y in range(4):
            for z in range(2):
                for c in range(3):
                    b = load[c, i, y, z]
                    v = b * dinv[i, y, z]
                    num = num + v * w0[c, i, y, z]
                    den = den + v * b
    totals = [masked_sum(num, 64), masked_sum(den, 64)]

    f1 = [[[stat[1, 2 * k + 4, y, 0]] for y in (0, 2)] for k in range(5)]
    c1 = []
    for k in range(5):
        i = 2 * k + 4
        c1.append([])
        for c in range(3):
            c1[k].append(restrict_plane([get_plane(load, c, j) for j in (i - 1, i, i + 1)], f1[k]))
    y1 = []
    for k in range(6):
        both = added(get_plane(stat, 0, 2 * k + 2), get_plane(stat, 0, 2 * k + 3))
        y1.append([[0.125 * (both[y][0] + both[y][1] + both[y + 1][0] + both[y + 1][1])] for y in (0, 2)])

    def level_sums(nodes, elements, frees, scale, lanes):
        count = len(frees) - 1
        num = jnp.zeros(REG, f32)
        den = jnp.zeros(REG, f32)
        groups = len(frees[0])
        modes = []
        for k in range(count + 1):
            total = added(low_sum(elements[k]), low_sum(elements[k + 1]))
            inv = [inverse_diagonal(total[y][0], frees[k][y][0], scale) for y in range(groups)]
            v = [[nodes[k][c][y][0] * inv[y] for y in range(groups)] for c in range(3)]
            zs = [z_modes([[v[c][y] * frees[k][y][0]] for c in range(3)]) for y in range(groups)]
            zs.append(rows_above(zs[0]))
            modes.append([y_modes(zs[y], zs[y + 1]) for y in range(groups)])
            if k < count:
                for c in range(3):
                    for y in range(groups):
                        num = num + jnp.where(frees[k][y][0] > 0.5, 0.0, v[c][y] * v[c][y])
                        den = den + v[c][y] * nodes[k][c][y][0]
        for k in range(count):
            for y in range(groups):
                u, f = element_forces(
                    [modes[k][y][c][0] for c in range(3)],
                    [modes[k + 1][y][c][0] for c in range(3)],
                    elements[k + 1][y][0] * scale,
                )
                for key in f:
                    num = num + u[key] * f[key]
        return [masked_sum(num, lanes), masked_sum(den, lanes)]

    totals += level_sums(c1[1:4], y1[1:5], f1[1:4], 2.0, 64)

    pick = matrix(lambda r, c: to_f(r == 2 * (c % 64)))
    mean = matrix(lambda r, c: to_f((r == 2 * (c % 64)) | (r == 2 * (c % 64) + 1), 0.5))
    half = matrix(
        lambda r, c: to_f(r == 2 * (c % 64)) + to_f((r == 2 * (c % 64) + 1) | (r == (2 * (c % 64) - 1) % 128), 0.5)
    )
    f2 = [[[dot(f1[k][0][0], pick)]] for k in (1, 3)]
    c2 = []
    for n, k in enumerate((1, 3)):
        c2.append([])
        for c in range(3):
            x = [c1[k][c][y][0] + 0.5 * (c1[k - 1][c][y][0] + c1[k + 1][c][y][0]) for y in range(2)]
            val = x[0] + 0.5 * (x[1] + roll(x[1], 1, 0))
            c2[n].append([[dot(val, half) * f2[n][0][0]]])
    y2 = []
    for k in (0, 2, 4):
        val = 0.25 * (y1[k][0][0] + y1[k][1][0] + y1[k + 1][0][0] + y1[k + 1][1][0])
        y2.append([[dot(val, mean)]])
    totals += level_sums(c2, y2, f2, 4.0, 32)

    row = lax.broadcasted_iota(jnp.int32, REG, 0)
    out = jnp.zeros(REG, f32)
    for k, total in enumerate(totals):
        out = jnp.where(row == k, total, out)
    for n in range(8):
        sums[n] = out

    for n, planes in enumerate([y1[2:4], f1[1:3]] + [[c1[1][c], c1[2][c]] for c in range(3)]):
        static[n] = side_by_side(planes, rows16.at[n])
    copy.wait()


def restrict_plane(planes, free=None):
    low, mid, high = planes
    x = [[b + 0.5 * (a + c) for a, b, c in zip(*p)] for p in zip(low, mid, high)]
    y = []
    for n in range(2):
        below = [roll(v, 1, 0) for v in x[3]] if n == 0 else x[1]
        y.append([b + 0.5 * (a + c) for a, b, c in zip(below, x[2 * n], x[2 * n + 1])])
    out = []
    for n in range(2):
        even, odd = y[n]
        val = even + 0.5 * (odd + roll(odd, 1, 1))
        out.append([val if free is None else val * free[n][0]])
    return out


def side_by_side(planes, rows16):
    vals = []
    for n, plane in enumerate(planes):
        for y in range(2):
            rows16[n, pl.ds(y, 8, stride=2)] = plane[y][0]
        vals.append(rows16[n, 4:12])
    return jnp.where(lanes_of() < 64, vals[0], roll(vals[1], 64, 1))


def second_kernel(stat, dinv, w0, static, w1_out, w2_out, pack, w1, w2, rows16, tb, cb, sem):
    def run(src, lo, n, dst, first):
        def load_w(i, y):
            scaled = [dinv[i, y, z] * stat[1, i, y, z] for z in range(2)]
            return [[src[c, i, y, z] * scaled[z] for z in range(2)] for c in range(3)]

        def emit(i, y, g):
            for z in range(2):
                free = stat[1, i, y, z]
                inv = dinv[i, y, z]
                for c in range(3):
                    dst[c, i - first, y, z] = jnp.where(free > 0.5, g[c][z], src[c, i, y, z] * inv)

        apply_planes((tb, cb), lo, n, load_w, lambda i, y, z: stat[0, i, y, z], emit)

    run(w0, 3, 10, w1, 0)
    copies = [pltpu.make_async_copy(w1, w1_out, sem.at[0]), pltpu.make_async_copy(w2, w2_out, sem.at[1])]
    copies[0].start()
    run(w1, 4, 8, w2, 4)
    copies[1].start()
    parts = [static[n] for n in range(5)]
    for n, (w, first) in enumerate(((w0, 0), (w1, 0), (w2, 4))):
        for c in range(3):
            planes = [restrict_plane([get_plane(w, c, j - first) for j in (i - 1, i, i + 1)]) for i in (6, 8)]
            parts.append(side_by_side(planes, rows16.at[n, c]) * static[1])
    split = dot(jnp.concatenate(parts, axis=0), split_matrix(64))
    for a in range(14):
        pack[a] = split[8 * a : 8 * a + 8]
    for copy in copies:
        copy.wait()


def estimate_of(sums, level):
    return jnp.max(sums[2 * level : 2 * level + 1, :] / sums[2 * level + 1 : 2 * level + 2, :])


def polynomial():
    theta, delta = centre_share, half_share
    sigma = theta / delta
    rho0 = 1.0 / sigma
    rho1 = 1.0 / (2.0 * sigma - rho0)
    rho2 = 1.0 / (2.0 * sigma - rho1)
    a10 = rho1 * rho0 / theta + 2.0 * rho1 / delta
    a11 = -2.0 * rho1 / (delta * theta)
    a20 = rho2 * rho1 * a10 + 2.0 * rho2 / delta
    a21 = rho2 * rho1 * a11 - (2.0 * rho2 / delta) * (1.0 / theta + a10)
    a22 = -(2.0 * rho2 / delta) * a11
    return 1.0 / theta + a10 + a20, a11 + a21, a22


def turns():
    sigma = centre_share / half_share
    rho = 1.0 / sigma
    out = []
    for _ in range(2):
        new = 1.0 / (2.0 * sigma - rho)
        out.append((new * rho, 2.0 * new / half_share))
        rho = new
    return out


def residual_factors(sums):
    inv = 1.0 / estimate_of(sums, 0)
    k0, k1, k2 = polynomial()
    return k0 * inv, k1 * inv * inv, k2 * inv * inv * inv


def residual_kernel(sums, load, dinv, w0, w1, w2, res, pre):
    b0, b1, b2 = residual_factors(sums)

    def step(k, carry):
        for c in range(3):
            res[c, k] = load[c, k + 4] - (b0 * w0[c, k + 4] + b1 * w1[c, k + 4] + b2 * w2[c, k])
        return carry

    lax.fori_loop(0, 8, step, 0)
    for k in range(4):
        for c in range(3):
            pre[c, k] = dinv[k + 6] * (b0 * load[c, k + 6] + b1 * w0[c, k + 6] + b2 * w1[c, k + 6])


def sum_kernel(parts, pack, out):
    total = parts[0]
    for n in range(1, parts.shape[0]):
        total = total + parts[n]
    for n in range(out.shape[0]):
        out[n] = total


def combine_kernel(parts, t0, t1, t2, t3, t4, out, sums):
    total = parts[0]
    for n in range(1, 32):
        total = total + parts[n]
    sums[...] = total
    b0, b1, b2 = residual_factors(sums)
    for t, tile in enumerate((t0, t1, t2, t3, t4)):
        out[t, 0:2] = tile[0:2]
        out[t, 2:5] = tile[2:5] - (b0 * tile[5:8] + b1 * tile[8:11] + b2 * tile[11:14])


def join_chips_kernel(core, mine, right, opposite, left, mine2, right2, opposite2, left2, out, first, last):
    lane = lanes_of()
    in_half = lane % 64

    def run(ours, others):
        for t in range(5):
            for a in range(5):
                planes = []
                for near, far in ((0, 2), (1, 3)):
                    for part in (ours, others):
                        one, two = part[near][t, a], part[far][t, a]
                        planes.append(jnp.where(lane < 64, one, roll(two, 64, 1)))
                        planes.append(jnp.where(lane < 64, roll(one, 64, 1), two))
                for i, val in enumerate(planes):
                    out[t, a, i] = val
                acc = [jnp.zeros(REG, f32) for _ in range(4)]
                for i in range(8):
                    val = out[t, a, i]
                    inside = (in_half >= 8 * i) & (in_half < 8 * i + 8)
                    for n, start in enumerate((0, 32, 24, 56)):
                        acc[n] = jnp.where(inside, roll(val, 8 * i - start, 1), acc[n])
                for z in range(2):
                    first[t, a, z] = acc[z]
                    last[t, a, z] = acc[2 + z]

    one, two = (mine, right, opposite, left), (mine2, right2, opposite2, left2)

    @pl.when(core[0] == 0)
    def _():
        run(one, two)

    @pl.when(core[0] != 0)
    def _():
        run(two, one)


def wrap(ref, planes, *at):
    for y in range(ref.shape[-4]):
        for z in range(ref.shape[-3]):
            ref[at + (0, y, z)] = roll(ref[at + (planes, y, z)], 64, 1)
            ref[at + (planes + 1, y, z)] = roll(ref[at + (1, y, z)], 64, 1)


def smooth(bufs, planes, young, free, dinv, res, x, inv, steps):
    groups, parts = res.shape[-4:-2]
    for src, dst, keep, gain in steps:

        def load_w(i, y, src=src):
            mask = [free[i + 1, y, z] for z in range(parts)]
            return [[src[c, i + 1, y, z] * mask[z] for z in range(parts)] for c in range(3)]

        def emit(i, y, g, src=src, dst=dst, keep=keep, gain=gain):
            for z in range(parts):
                mask = free[i + 1, y, z]
                scaled = None if dst is None else (gain * inv) * dinv[i, y, z]
                for c in range(3):
                    d = src[c, i + 1, y, z]
                    left = res[c, i, y, z] - jnp.where(mask > 0.5, g[c][z], d)
                    res[c, i, y, z] = left
                    if dst is not None:
                        new = keep * d + scaled * left if keep else scaled * left
                        dst[c, i + 1, y, z] = new
                        x[c, i, y, z] = x[c, i, y, z] + new

        apply_planes(bufs, 0, planes, load_w, lambda i, y, z: young[i + 1, y, z], emit)
        if dst is not None:
            for c in range(3):
                wrap(dst, planes, c)


def coarse_kernel(
    sums, core, chips, from_left, from_right, out,
    nat, young, free, dinv, res, d_a, d_b, x,
    nat2, young2, free2, dinv2, res2, d2_a, d2_b, x2,
    nat3, young3, free3, dinv3, res3, x3, rows_e, rows_o,
    tb, cb, tb2, cb2, tb3, cb3,
):
    lane = lanes_of()
    in_half = lane % 64
    for t in range(5):
        for a in range(5):
            for i in range(8):
                val = chips[t, a, i]
                for z in range(2):
                    here = jnp.where((in_half >= 8) & (in_half < 40), roll(val, 8 - 32 * z, 1), 0.0)
                    right = roll(from_right[t, a, z], 40 - 8 * i, 1)
                    left = roll(from_left[t, a, z], -8 * i, 1)
                    here = jnp.where((in_half >= 40) & (in_half < 48), right, here)
                    nat[a, i, z, 8 * t : 8 * t + 8] = jnp.where(in_half < 8, left, here)
    for i in range(8):
        for y in range(5):
            rows = pl.ds(y, 8, stride=5)
            for z in range(2):
                young[i + 1, y, z] = 2.0 * nat[0, i, z, rows]
                free[i + 1, y, z] = nat[1, i, z, rows]
                for c in range(3):
                    res[c, i, y, z] = nat[2 + c, i, z, rows]
    wrap(young, 8)
    wrap(free, 8)

    inv1 = 1.0 / estimate_of(sums, 1)
    inv2 = 1.0 / estimate_of(sums, 2)
    start = 1.0 / centre_share
    later = turns()

    def begin(i, carry):
        total = added(low_sum(get_plane(young, i + 1)), low_sum(get_plane(young, i)))
        for y in range(5):
            for z in range(2):
                inverse = inverse_diagonal(total[y][z], free[i + 1, y, z], 1.0)
                dinv[i, y, z] = inverse
                for c in range(3):
                    d = (start * inv1) * inverse * res[c, i, y, z]
                    d_a[c, i + 1, y, z] = d
                    x[c, i, y, z] = d
        return carry

    lax.fori_loop(0, 8, begin, 0)
    for c in range(3):
        wrap(d_a, 8, c)
    steps = [(d_a, d_b) + later[0], (d_b, d_a) + later[1], (d_a, None, 0.0, 0.0)]
    smooth((tb, cb), 8, young, free, dinv, res, x, inv1, steps)

    for a in range(5):
        for k in range(4):
            nat2[a, k, 0:8] = jnp.zeros(REG, f32)
            nat2[a, k, 48:56] = jnp.zeros(REG, f32)
    for k in range(4):
        for y in range(5):
            rows = pl.ds(8 + y, 8, stride=5)
            both = [young[2 * k + 1, y, z] + young[2 * k + 2, y, z] for z in range(2)]
            nat2[0, k, rows] = both[0] + both[1]
            nat2[1, k, rows] = free[2 * k + 1, y, 0]
            for c in range(3):
                part = []
                for z in range(2):
                    below = res[c, 2 * k - 1, y, z] if k else roll(res[c, 7, y, z], 64, 1)
                    part.append(res[c, 2 * k, y, z] + 0.5 * (below + res[c, 2 * k + 1, y, z]))
                nat2[2 + c, k, rows] = part[0] + 0.5 * (part[1] + roll(part[1], 1, 1))
        for y in range(3):
            at = [pl.ds(8 + 2 * y + n, 8, stride=6) for n in (-1, 0, 1)]
            young2[k + 1, y, 0] = 0.25 * (nat2[0, k, at[1]] + nat2[0, k, at[2]])
            mask = nat2[1, k, at[1]]
            free2[k + 1, y, 0] = mask
            for c in range(3):
                val = nat2[2 + c, k, at[1]] + 0.5 * (nat2[2 + c, k, at[0]] + nat2[2 + c, k, at[2]])
                res2[c, k, y, 0] = val * mask
    wrap(young2, 4)
    wrap(free2, 4)
    for k in range(4):
        total = added(low_sum(get_plane(young2, k + 1)), low_sum(get_plane(young2, k)))
        for y in range(3):
            inverse = inverse_diagonal(total[y][0], free2[k + 1, y, 0], 1.0)
            dinv2[k, y, 0] = inverse
            for c in range(3):
                d = (start * inv2) * inverse * res2[c, k, y, 0]
                d2_a[c, k + 1, y, 0] = d
                x2[c, k, y, 0] = d
    for c in range(3):
        wrap(d2_a, 4, c)
    steps = [(d2_a, d2_b) + later[0], (d2_b, d2_a) + later[1]]
    smooth((tb2, cb2), 4, young2, free2, dinv2, res2, x2, inv2, steps)

    for i in range(8):
        for z in range(2):
            for y in range(5):
                rows = pl.ds(y, 8, stride=5)
                nat[0, i, z, rows] = dinv[i, y, z]
                for c in range(3):
                    nat[1 + c, i, z, rows] = res[c, i, y, z]
            for y in range(3):
                rows = pl.ds(8 + y, 8, stride=3)
                dinv3[i, y, z] = nat[0, i, z, rows]
                for c in range(3):
                    res3[c, i, y, z] = nat[1 + c, i, z, rows]
    for i in range(8):
        for z in range(2):
            for y in range(5):
                rows = pl.ds(y, 8, stride=5)
                nat[0, i, z, rows] = young[i + 1, y, z]
                nat[1, i, z, rows] = free[i + 1, y, z]
                for c in range(3):
                    nat[2 + c, i, z, rows] = x[c, i, y, z]
            for y in range(3):
                rows = pl.ds(8 + y, 8, stride=3)
                young3[i + 1, y, z] = nat[0, i, z, rows]
                free3[i + 1, y, z] = nat[1, i, z, rows]
                for c in range(3):
                    x3[c, i, y, z] = nat[2 + c, i, z, rows]
    wrap(young3, 8)
    wrap(free3, 8)
    d3_a, d3_b = d_a, d_b
    for c in range(3):
        for k in range(4):
            here = [x2[c, k, y, 0] for y in range(3)]
            if k < 3:
                nxt = [x2[c, k + 1, y, 0] for y in range(3)]
            else:
                nxt = [roll(x2[c, 0, y, 0], 64, 1) for y in range(3)]
            for n, val in enumerate((here, [0.5 * (p + q) for p, q in zip(here, nxt)])):
                above = val[1:] + [roll(val[0], -1, 0)]
                for y in range(3):
                    nat3[n, pl.ds(2 * y, 8, stride=6)] = val[y]
                    nat3[n, pl.ds(2 * y + 1, 8, stride=6)] = 0.5 * (val[y] + above[y])
                i = 2 * k + n
                for y in range(3):
                    even = nat3[n, pl.ds(8 + y, 8, stride=3)]
                    odd = 0.5 * (even + roll(even, -1, 1))
                    for z, e in enumerate((even, odd)):
                        e = e * free3[i + 1, y, z]
                        d3_b[c, i + 1, y, z] = e
                        x3[c, i, y, z] = x3[c, i, y, z] + e
        wrap(d3_b, 8, c)
    steps = [(d3_b, d3_a, 0.0, start), (d3_a, d3_b) + later[0], (d3_b, d3_a) + later[1]]
    smooth((tb3, cb3), 8, young3, free3, dinv3, res3, x3, inv1, steps)

    place = 2 * core[0]
    for k in range(6):
        plane = (place + (14 + k)) & 15
        i = plane & 7
        swap = plane > 7
        for c in range(3):
            for y in range(3):
                rows = pl.ds(24 * (3 * k + c) + y, 8, stride=3)
                for z, dst in enumerate((rows_e, rows_o)):
                    val = x3[c, i, y, z]
                    dst[rows] = jnp.where(swap, roll(val, 64, 1), val)
    place_e = matrix(lambda r, c: to_f((r < 48) & (c == (2 * r + 112) % 128)))
    place_o = matrix(lambda r, c: to_f((r < 48) & (c == (2 * r + 113) % 128)))
    out[...] = (dot(rows_e[...], place_e) + dot(rows_o[...], place_o)).reshape(6, 3, 24, 128)


def last_kernel(sums, stat, dinv, res_in, pre, x1, out, e0, res, d_a, d_b, rows, tb, cb):
    inv = 1.0 / estimate_of(sums, 0)
    start = 1.0 / centre_share
    later = turns()

    def raised(c, k):
        at = [x1[k, c, pl.ds(4 + n, 8, stride=2)] for n in range(3)]
        groups = [at[0], 0.5 * (at[0] + at[1]), at[1], 0.5 * (at[1] + at[2])]
        return [[v, 0.5 * (v + roll(v, -1, 1))] for v in groups]

    for c in range(3):
        here = raised(c, 0)
        for k in range(6):
            nxt = raised(c, k + 1) if k < 5 else None
            for y in range(4):
                for z in range(2):
                    e0[c, 2 * k, y, z] = here[y][z] * stat[1, 2 * k + 2, y, z]
                    if k < 5:
                        e0[c, 2 * k + 1, y, z] = 0.5 * (here[y][z] + nxt[y][z]) * stat[1, 2 * k + 3, y, z]
            here = nxt

    def loader(ref, shift):
        def load_w(i, y):
            mask = [stat[1, i, y, z] for z in range(2)]
            return [[ref[c, i - shift, y, z] * mask[z] for z in range(2)] for c in range(3)]

        return load_w

    def emit_e(i, y, g):
        for z in range(2):
            mask = stat[1, i, y, z]
            scaled = (start * inv) * dinv[i, y, z]
            for c in range(3):
                left = res_in[c, i - 4, y, z] - jnp.where(mask > 0.5, g[c][z], e0[c, i - 2, y, z])
                res[c, i - 4, y, z] = left
                d_a[c, i - 4, y, z] = scaled * left

    def emit_a(i, y, g):
        keep, gain = later[0]
        for z in range(2):
            mask = stat[1, i, y, z]
            scaled = (gain * inv) * dinv[i, y, z]
            for c in range(3):
                d = d_a[c, i - 4, y, z]
                left = res[c, i - 4, y, z] - jnp.where(mask > 0.5, g[c][z], d)
                res[c, i - 4, y, z] = left
                d_b[c, i - 4, y, z] = keep * d + scaled * left

    def emit_b(i, y, g):
        keep, gain = later[1]
        total = [[None, None] for _ in range(3)]
        for z in range(2):
            mask = stat[1, i, y, z]
            scaled = (gain * inv) * dinv[i, y, z]
            for c in range(3):
                d = d_b[c, i - 4, y, z]
                left = res[c, i - 4, y, z] - jnp.where(mask > 0.5, g[c][z], d)
                new = keep * d + scaled * left
                old = pre[c, i - 6, y, z] + e0[c, i - 2, y, z] + d_a[c, i - 4, y, z]
                total[c][z] = old + d + new
        for c in range(3):
            val = jnp.where(lanes_of() < 64, total[c][0], roll(total[c][1], 64, 1))
            rows[c, i - 6, pl.ds(y, 8, stride=4)] = val

    young = lambda i, y, z: stat[0, i, y, z]
    apply_planes((tb, cb), 4, 8, loader(e0, 2), young, emit_e)
    apply_planes((tb, cb), 5, 6, loader(d_a, 4), young, emit_a)
    apply_planes((tb, cb), 6, 4, loader(d_b, 4), young, emit_b)
    join = join_matrix()
    for c in range(3):
        for k in range(4):
            out[c, k] = dot(rows[c, k, 8:24], join)


def call(kernel, outs, scratch=(), smem=None, flops=0, limit=3, in_hbm=(), hbm_in=False, plain_out=False):
    def run(*args):
        where = pltpu.HBM if hbm_in else pltpu.VMEM
        specs = [pl.BlockSpec(memory_space=pltpu.SMEM if n == smem else where) for n in range(len(args))]
        args = [a if n == smem else pltpu.with_memory_space_constraint(a, where) for n, a in enumerate(args)]
        spaces = [pltpu.HBM if n in in_hbm else pltpu.VMEM for n in range(len(outs))]
        return pl.pallas_call(
            kernel,
            in_specs=specs,
            out_specs=[pl.BlockSpec(memory_space=space) for space in spaces],
            out_shape=[jax.ShapeDtypeStruct(s, f32) if plain_out else space(s, f32) for s, space in zip(outs, spaces)],
            scratch_shapes=[s if not isinstance(s, tuple) else pltpu.VMEM(s, f32) for s in scratch],
            compiler_params=pltpu.CompilerParams(vmem_limit_bytes=limit * 1024 * 1024),
            cost_estimate=pl.CostEstimate(flops=flops, bytes_accessed=1 << 20, transcendentals=0),
        )(*args)

    return run


def send(value, axis, shift):
    count = lax.axis_size(axis)
    return lax.ppermute(value, axis, [(i, (i + shift) % count) for i in range(count)])


def swap_core(value):
    return lax.ppermute(value, "gx", [(i, i ^ 1) for i in range(lax.axis_size("gx"))])


def local(density_level, support_mask, load_mask, load_vector):
    block = density_level.shape
    ints = [pltpu.VMEM(block, jnp.int32)] * 3
    low, high = call(
        prepare_kernel, [(5, 4, 8, 128)] * 2, ints + [(3,) + block, pltpu.SemaphoreType.DMA((4,))], hbm_in=True
    )(density_level, support_mask, load_mask, load_vector)
    up, down = send(high, "gy", 1), send(low, "gy", -1)
    own, first, last = call(join_y_kernel, [(5, 4, 32, 128), (5, 1, 32, 128), (5, 2, 32, 128)])(up, low, high, down)
    planes = [send(last, "gx", 2), send(own, "gx", 1), own, send(own, "gx", -1), send(first, "gx", -2)]
    first, last = call(pack_z_kernel, [(5, 32, 128)] * 2)(*planes)
    from_left, from_right = send(last, "gz", 1), send(first, "gz", -1)
    fine = (4, 2) + REG
    stat, load, dinv, w0, static, sums = call(
        first_kernel,
        [(2, NXE) + fine, (3, NXE) + fine, (NXE,) + fine, (3, NXE) + fine, (5,) + REG, (8,) + REG],
        [(3, NXE) + fine, (5, 2, 16, 128)] + work_buffers(4, 2) + [pltpu.SemaphoreType.DMA],
        limit=8,
        in_hbm=(1,),
    )(*planes, from_left, from_right)
    w1, w2, pack = call(
        second_kernel,
        [(3, NXE) + fine, (3, 8) + fine, (14,) + REG],
        [(3, NXE) + fine, (3, 8) + fine, (3, 3, 2, 16, 128)] + work_buffers(4, 2) + [pltpu.SemaphoreType.DMA((2,))],
        flops=1 << 26,
        limit=9,
        in_hbm=(0, 1),
    )(stat, dinv, w0, static)
    sums = call(sum_kernel, [(32,) + REG])(lax.all_to_all(sums, "gy", 0, 0), pack)[0]
    tiles = [send(pack, "gy", 2), send(pack, "gy", 1), pack, send(pack, "gy", -1), send(pack, "gy", -2)]
    parts = lax.all_to_all(sums, ("gx", "gz"), 0, 0)
    mine, sums = call(combine_kernel, [(5, 5) + REG, REG])(parts, *tiles)
    res, pre = call(residual_kernel, [(3, 8) + fine, (3, 4) + fine], flops=1 << 22)(sums, load, dinv, w0, w1, w2)
    chips = [mine, send(mine, "gx", -2), send(mine, "gx", 4), send(mine, "gx", 2)]
    chips += [swap_core(val) for val in chips]
    core = (lax.axis_index("gx") & 1).reshape(1).astype(jnp.int32)
    chips, first, last = call(join_chips_kernel, [(5, 5, 8) + REG] + [(5, 5, 2) + REG] * 2, smem=0)(core, *chips)
    from_left, from_right = send(last, "gz", 1), send(first, "gz", -1)
    five, three, one = (5, 2) + REG, (3, 2) + REG, (3, 1) + REG
    x1 = call(
        coarse_kernel,
        [(6, 3, 24, 128)],
        [(5, 8, 2, 40, 128), (10,) + five, (10,) + five, (8,) + five]
        + [(3, 8) + five, (3, 10) + five, (3, 10) + five, (3, 8) + five]
        + [(5, 4, 56, 128), (6,) + one, (6,) + one, (4,) + one]
        + [(3, 4) + one, (3, 6) + one, (3, 6) + one, (3, 4) + one]
        + [(2, 48, 128), (10,) + three, (10,) + three, (8,) + three]
        + [(3, 8) + three, (3, 8) + three, (432, 128), (432, 128)]
        + work_buffers(5, 2)
        + work_buffers(3, 1)
        + work_buffers(3, 2),
        smem=1,
        limit=20,
    )(sums, core, chips, from_left, from_right)[0]
    return call(
        last_kernel,
        [(3, 4, 16, 128)],
        [(3, 12) + fine, (3, 8) + fine, (3, 8) + fine, (3, 8) + fine, (3, 4, 32, 128)] + work_buffers(4, 2),
        plain_out=True,
        limit=9,
    )(sums, stat, dinv, res, pre, x1)[0]


def solution(mesh):
    block = P("gx", "gy", "gz")
    return jax.shard_map(
        local,
        mesh=mesh,
        in_specs=(block, block, block, P(None, "gx", "gy", "gz")),
        out_specs=P(None, "gx", "gy", "gz"),
        check_vma=False,
    )
```

```python
import jax
import jax.numpy as jnp
from jax import lax
from jax.experimental import pallas as pl
from jax.experimental.pallas import tpu as pltpu
from jax.sharding import PartitionSpec as P

f32 = jnp.float32
young_floor = 0.001
poisson = 0.3
headroom = 1.5
floor_share = 0.3
lam = poisson / ((1.0 + poisson) * (1.0 - 2.0 * poisson))
mu = 1.0 / (2.0 * (1.0 + poisson))
diag_entry = (lam + 2 * mu + 2 * mu) / 16 + (2 * (lam + 3 * mu) + 2 * mu) / 48 + (lam + 4 * mu) / 144
centre_share = 0.5 * headroom * (1.0 + floor_share)
half_share = 0.5 * headroom * (1.0 - floor_share)

NXE = 15
SS, SD, DS, DD = 0, 1, 2, 3
REG = (8, 128)


def roll(v, amount, axis):
    return pltpu.roll(v, amount % v.shape[axis], axis=axis)


def lanes_of(shape=REG):
    return lax.broadcasted_iota(jnp.int32, shape, 1)


def z_next(p):
    return [p[1], roll(p[0], -1, 1)] if len(p) == 2 else [roll(p[0], -1, 1)]


def z_prev(p):
    return [roll(p[1], 1, 1), p[0]] if len(p) == 2 else [roll(p[0], 1, 1)]


def y_next(plane):
    return plane[1:] + [[roll(v, -1, 0) for v in plane[0]]]


def y_prev(plane):
    return [[roll(v, 1, 0) for v in plane[-1]]] + plane[:-1]


def added(one, two):
    return [[a + b for a, b in zip(p, q)] for p, q in zip(one, two)]


def get_plane(ref, *at):
    groups, parts = ref.shape[-4:-2]
    return [[ref[at + (y, z)] for z in range(parts)] for y in range(groups)]


def element_forces(t0, t1, e):
    u = {}
    for c in range(3):
        for m in range(4):
            u[c, "d", m] = t1[c][m] - t0[c][m]
            if m != SS:
                u[c, "s", m] = t1[c][m] + t0[c][m]
    f = {}
    e_a, e_b, e_c = e * (lam / 16), e * (2 * mu / 16), e * (mu / 16)
    e_d, e_e, e_f = e * (lam / 48), e * (3 * mu / 48), e * (mu / 48)
    e_g = e * ((lam + 4 * mu) / 144)
    normal = ((0, "d", SS), (1, "s", DS), (2, "s", SD))
    t = e_a * (u[normal[0]] + u[normal[1]] + u[normal[2]])
    for key in normal:
        f[key] = t + e_b * u[key]
    for one, two in (((0, "s", DS), (1, "d", SS)), ((1, "s", SD), (2, "s", DS)), ((0, "s", SD), (2, "d", SS))):
        f[one] = f[two] = e_c * (u[one] + u[two])
    for one, two in (((0, "d", DS), (2, "s", DD)), ((0, "d", SD), (1, "s", DD)), ((1, "d", DS), (2, "d", SD))):
        p = e_d * (u[one] + u[two])
        f[one] = p + e_e * u[one]
        f[two] = p + e_e * u[two]
    triple = ((0, "s", DD), (1, "d", SD), (2, "d", DS))
    q = u[triple[0]] + u[triple[1]] + u[triple[2]]
    for key in triple:
        f[key] = e_f * (u[key] + q)
    for c in range(3):
        f[c, "d", DD] = e_g * u[c, "d", DD]
    return u, f


def z_modes(w):
    out = []
    for p in w:
        out.append([(a + b, b - a) for a, b in zip(p, z_next(p))])
    return out


def y_modes(cur, nxt):
    return [[(s + su, d + du, su - s, du - d) for (s, d), (su, du) in zip(p, q)] for p, q in zip(cur, nxt)]


def rows_above(first):
    return [[tuple(roll(v, -1, 0) for v in pair) for pair in p] for p in first]


def forward_plane(t, groups, load_w):
    first = cur = z_modes(load_w(0))
    for y in range(groups):
        nxt = z_modes(load_w(y + 1)) if y < groups - 1 else rows_above(first)
        for c, p in enumerate(y_modes(cur, nxt)):
            for z, vals in enumerate(p):
                for m, val in enumerate(vals):
                    t[4 * c + m, y, z] = val
        cur = nxt


def finish_rows(low, high):
    res = []
    for one, two in zip(low, high):
        s = [a[0] + b[0] for a, b in zip(one, two)]
        d = [a[1] + b[1] for a, b in zip(one, two)]
        down = [a - b for a, b in zip(s, d)]
        up = z_prev([a + b for a, b in zip(s, d)])
        res.append([a + b for a, b in zip(down, up)])
    return res


def element_plane(t0_ref, t1_ref, c_ref, groups, parts, load_w, load_e, emit, fresh):
    first = cur = z_modes(load_w(0))
    prev = start = None
    for y in range(groups):
        nxt = z_modes(load_w(y + 1)) if y < groups - 1 else rows_above(first)
        t1 = y_modes(cur, nxt)
        low = [[None] * parts for _ in range(3)]
        high = [[None] * parts for _ in range(3)]
        for z in range(parts):
            t0 = [[t0_ref[4 * c + m, y, z] for m in range(4)] for c in range(3)]
            for c in range(3):
                for m in range(4):
                    t1_ref[4 * c + m, y, z] = t1[c][z][m]
            u, f = element_forces(t0, [t1[c][z] for c in range(3)], load_e(y, z))
            for c in range(3):
                g = []
                for m in range(4):
                    d = f[c, "d", m]
                    if not fresh:
                        old = c_ref[4 * c + m, y, z]
                        g.append(old - d if m == SS else old + (f[c, "s", m] - d))
                    c_ref[4 * c + m, y, z] = d if m == SS else f[c, "s", m] + d
                if not fresh:
                    low[c][z] = (g[SS] - g[DS], g[SD] - g[DD])
                    high[c][z] = (g[SS] + g[DS], g[SD] + g[DD])
        if not fresh:
            if y == 0:
                start = low
            else:
                emit(y, finish_rows(low, prev))
            prev = high
        cur = nxt
    if not fresh:
        last = [[tuple(roll(v, 1, 0) for v in pair) for pair in p] for p in prev]
        emit(0, finish_rows(start, last))


def apply_planes(bufs, lo, n, load_w, load_e, emit):
    t_ref, c_ref = bufs
    groups, parts = c_ref.shape[1:3]

    def one(i, a, fresh=False):
        element_plane(
            t_ref.at[a],
            t_ref.at[1 - a],
            c_ref,
            groups,
            parts,
            lambda y: load_w(i + 1, y),
            lambda y, z: load_e(i, y, z),
            lambda y, res: emit(i, y, res),
            fresh,
        )

    forward_plane(t_ref.at[0], groups, lambda y: load_w(lo - 1, y))
    one(lo - 1, 0, True)

    def step(j, carry):
        one(lo + 2 * j, 1)
        one(lo + 2 * j + 1, 0)
        return carry

    lax.fori_loop(0, n // 2, step, 0)


def work_buffers(groups, parts):
    return [pltpu.VMEM((2, 12, groups, parts) + REG, f32), pltpu.VMEM((12, groups, parts) + REG, f32)]


def low_sum(plane):
    plane = [[a + b for a, b in zip(p, z_prev(p))] for p in plane]
    return added(plane, y_prev(plane))


def inverse_diagonal(e_sum, free, scale):
    return jnp.where(free > 0.5, 1.0 / (e_sum * (diag_entry * scale)), 1.0)


def matrix(fun):
    shape = (128, 128)
    r = lax.broadcasted_iota(jnp.int32, shape, 0)
    c = lax.broadcasted_iota(jnp.int32, shape, 1)
    return fun(r, c)


def dot(a, b):
    return jnp.dot(a, b, precision=lax.Precision.HIGHEST, preferred_element_type=f32)


def to_f(cond, val=1.0):
    return jnp.where(cond, f32(val), f32(0.0))


def split_matrix(width):
    def fun(r, c):
        z = r % width
        return to_f(c == r - z + (z % 2) * (width // 2) + z // 2)

    return matrix(fun)


def join_matrix():
    return matrix(lambda r, c: to_f(c == (r % 64) * 2 + r // 64))


def prepare_kernel(density, support, load, vector, low, high, a_buf, b_buf, c_buf, v_buf, sem):
    copies = []
    for n, (src, dst) in enumerate(((density, a_buf), (support, b_buf), (load, c_buf), (vector, v_buf))):
        copies.append(pltpu.make_async_copy(src, dst, sem.at[n]))
        copies[-1].start()
    for copy in copies:
        copy.wait()
    scaled = a_buf[...].astype(f32) / 255.0
    young = young_floor + (1.0 - young_floor) * scaled * scaled * scaled
    free = 1.0 - b_buf[...].astype(f32)
    masked = free * c_buf[...].astype(f32)
    split = split_matrix(128)
    rows = [young, free] + [masked * v_buf[c] for c in range(3)]
    for a, val in enumerate(rows):
        val = dot(val.reshape(64, 128), split).reshape(4, 16, 128)
        low[a] = val[:, 0:8]
        high[a] = val[:, 8:16]


def join_y_kernel(up, low, high, down, own, first, last):
    for t, tile in enumerate((up, low, high, down)):
        rows = slice(8 * t, 8 * t + 8)
        for a in range(5):
            own[a, :, rows] = tile[a]
            first[a, :, rows] = tile[a, 0:1]
            last[a, :, rows] = tile[a, 2:4]


def plane_refs(far_left, left, own, right, far_right):
    return [(ref, k) for ref, n in ((far_left, 2), (left, 4), (own, 4), (right, 4), (far_right, 1)) for k in range(n)]


def pack_z_kernel(far_left, left, own, right, far_right, first, last):
    planes = plane_refs(far_left, left, own, right, far_right)
    lane = lanes_of() % 64
    for a in range(5):
        for t in range(4):
            acc_first = jnp.zeros(REG, f32)
            acc_last = jnp.zeros(REG, f32)
            for g in range(NXE):
                ref, k = planes[g]
                val = ref[a, k, 8 * t : 8 * t + 8]
                inside = (lane >= 4 * g) & (lane < 4 * g + 4)
                acc_first = jnp.where(inside, roll(val, 4 * g, 1), acc_first)
                acc_last = jnp.where(inside, roll(val, 4 * g - 60, 1), acc_last)
            first[a, 8 * t : 8 * t + 8] = acc_first
            last[a, 8 * t : 8 * t + 8] = acc_last


def first_kernel(
    far_left, left, mid, right, far_right, from_left, from_right,
    stat, load_out, dinv, w0, static, sums, load, rows16, tb, cb, sem,
):
    lane = lanes_of()
    planes = plane_refs(far_left, left, mid, right, far_right)
    outer = ((lane >= 64) & (lane < 68)) | (lane >= 124)
    for a in range(5):
        for y in range(4):
            rows = pl.ds(y, 8, stride=4)
            left = from_left[a, rows]
            right = from_right[a, rows]
            halo_e = jnp.where(lane < 60, right, roll(left, 60, 1))
            halo_o = jnp.where(lane < 60, roll(right, 64, 1), roll(left, -4, 1))
            for g in range(NXE):
                ref, k = planes[g]
                own = ref[a, k, rows]
                even = jnp.where(outer, roll(halo_e, 64 - 4 * g, 1), jnp.where(lane < 64, own, 0.0))
                odd = jnp.where(outer, roll(halo_o, 64 - 4 * g, 1), jnp.where(lane < 64, roll(own, 64, 1), 0.0))
                for z, val in enumerate((even, odd)):
                    if a < 2:
                        stat[a, g, y, z] = val
                    else:
                        load[a - 2, g, y, z] = val
    copy = pltpu.make_async_copy(load, load_out, sem)
    copy.start()

    def diag_step(i, carry):
        total = added(low_sum(get_plane(stat, 0, i)), low_sum(get_plane(stat, 0, jnp.maximum(i - 1, 0))))
        for y in range(4):
            for z in range(2):
                dinv[i, y, z] = inverse_diagonal(total[y][z], stat[1, i, y, z], 1.0)
        return carry

    lax.fori_loop(0, NXE, diag_step, 0)

    def load_w(i, y):
        scaled = [dinv[i, y, z] * stat[1, i, y, z] for z in range(2)]
        return [[load[c, i, y, z] * scaled[z] for z in range(2)] for c in range(3)]

    def emit(i, y, g):
        for z in range(2):
            free = stat[1, i, y, z]
            inv = dinv[i, y, z]
            for c in range(3):
                w0[c, i, y, z] = jnp.where(free > 0.5, g[c][z], load[c, i, y, z] * inv)

    apply_planes((tb, cb), 2, 12, load_w, lambda i, y, z: stat[0, i, y, z], emit)

    sub = lax.broadcasted_iota(jnp.int32, REG, 0)
    own_rows = (sub >= 2) & (sub < 6)

    def masked_sum(val, count):
        return jnp.sum(jnp.where(own_rows & (lane < count), val, 0.0))

    num = jnp.zeros(REG, f32)
    den = jnp.zeros(REG, f32)
    for i in range(6, 10):
        for y in range(4):
            for z in range(2):
                for c in range(3):
                    b = load[c, i, y, z]
                    v = b * dinv[i, y, z]
                    num = num + v * w0[c, i, y, z]
                    den = den + v * b
    totals = [masked_sum(num, 64), masked_sum(den, 64)]

    f1 = [[[stat[1, 2 * k + 4, y, 0]] for y in (0, 2)] for k in range(5)]
    c1 = []
    for k in range(5):
        i = 2 * k + 4
        c1.append([])
        for c in range(3):
            c1[k].append(restrict_plane([get_plane(load, c, j) for j in (i - 1, i, i + 1)], f1[k]))
    y1 = []
    for k in range(6):
        both = added(get_plane(stat, 0, 2 * k + 2), get_plane(stat, 0, 2 * k + 3))
        y1.append([[0.125 * (both[y][0] + both[y][1] + both[y + 1][0] + both[y + 1][1])] for y in (0, 2)])

    def level_sums(nodes, elements, frees, scale, lanes):
        count = len(frees) - 1
        num = jnp.zeros(REG, f32)
        den = jnp.zeros(REG, f32)
        groups = len(frees[0])
        modes = []
        for k in range(count + 1):
            total = added(low_sum(elements[k]), low_sum(elements[k + 1]))
            inv = [inverse_diagonal(total[y][0], frees[k][y][0], scale) for y in range(groups)]
            v = [[nodes[k][c][y][0] * inv[y] for y in range(groups)] for c in range(3)]
            zs = [z_modes([[v[c][y] * frees[k][y][0]] for c in range(3)]) for y in range(groups)]
            zs.append(rows_above(zs[0]))
            modes.append([y_modes(zs[y], zs[y + 1]) for y in range(groups)])
            if k < count:
                for c in range(3):
                    for y in range(groups):
                        num = num + jnp.where(frees[k][y][0] > 0.5, 0.0, v[c][y] * v[c][y])
                        den = den + v[c][y] * nodes[k][c][y][0]
        for k in range(count):
            for y in range(groups):
                u, f = element_forces(
                    [modes[k][y][c][0] for c in range(3)],
                    [modes[k + 1][y][c][0] for c in range(3)],
                    elements[k + 1][y][0] * scale,
                )
                for key in f:
                    num = num + u[key] * f[key]
        return [masked_sum(num, lanes), masked_sum(den, lanes)]

    totals += level_sums(c1[1:4], y1[1:5], f1[1:4], 2.0, 64)

    pick = matrix(lambda r, c: to_f(r == 2 * (c % 64)))
    mean = matrix(lambda r, c: to_f((r == 2 * (c % 64)) | (r == 2 * (c % 64) + 1), 0.5))
    half = matrix(
        lambda r, c: to_f(r == 2 * (c % 64)) + to_f((r == 2 * (c % 64) + 1) | (r == (2 * (c % 64) - 1) % 128), 0.5)
    )
    f2 = [[[dot(f1[k][0][0], pick)]] for k in (1, 3)]
    c2 = []
    for n, k in enumerate((1, 3)):
        c2.append([])
        for c in range(3):
            x = [c1[k][c][y][0] + 0.5 * (c1[k - 1][c][y][0] + c1[k + 1][c][y][0]) for y in range(2)]
            val = x[0] + 0.5 * (x[1] + roll(x[1], 1, 0))
            c2[n].append([[dot(val, half) * f2[n][0][0]]])
    y2 = []
    for k in (0, 2, 4):
        val = 0.25 * (y1[k][0][0] + y1[k][1][0] + y1[k + 1][0][0] + y1[k + 1][1][0])
        y2.append([[dot(val, mean)]])
    totals += level_sums(c2, y2, f2, 4.0, 32)

    row = lax.broadcasted_iota(jnp.int32, REG, 0)
    out = jnp.zeros(REG, f32)
    for k, total in enumerate(totals):
        out = jnp.where(row == k, total, out)
    for n in range(8):
        sums[n] = out

    for n, planes in enumerate([y1[2:4], f1[1:3]] + [[c1[1][c], c1[2][c]] for c in range(3)]):
        static[n] = side_by_side(planes, rows16.at[n])
    copy.wait()


def restrict_plane(planes, free=None):
    low, mid, high = planes
    x = [[b + 0.5 * (a + c) for a, b, c in zip(*p)] for p in zip(low, mid, high)]
    y = []
    for n in range(2):
        below = [roll(v, 1, 0) for v in x[3]] if n == 0 else x[1]
        y.append([b + 0.5 * (a + c) for a, b, c in zip(below, x[2 * n], x[2 * n + 1])])
    out = []
    for n in range(2):
        even, odd = y[n]
        val = even + 0.5 * (odd + roll(odd, 1, 1))
        out.append([val if free is None else val * free[n][0]])
    return out


def side_by_side(planes, rows16):
    vals = []
    for n, plane in enumerate(planes):
        for y in range(2):
            rows16[n, pl.ds(y, 8, stride=2)] = plane[y][0]
        vals.append(rows16[n, 4:12])
    return jnp.where(lanes_of() < 64, vals[0], roll(vals[1], 64, 1))


def second_kernel(stat, dinv, w0, static, w1_out, w2_out, pack, w1, w2, rows16, tb, cb, sem):
    def run(src, lo, n, dst, first):
        def load_w(i, y):
            scaled = [dinv[i, y, z] * stat[1, i, y, z] for z in range(2)]
            return [[src[c, i, y, z] * scaled[z] for z in range(2)] for c in range(3)]

        def emit(i, y, g):
            for z in range(2):
                free = stat[1, i, y, z]
                inv = dinv[i, y, z]
                for c in range(3):
                    dst[c, i - first, y, z] = jnp.where(free > 0.5, g[c][z], src[c, i, y, z] * inv)

        apply_planes((tb, cb), lo, n, load_w, lambda i, y, z: stat[0, i, y, z], emit)

    run(w0, 3, 10, w1, 0)
    copies = [pltpu.make_async_copy(w1, w1_out, sem.at[0]), pltpu.make_async_copy(w2, w2_out, sem.at[1])]
    copies[0].start()
    run(w1, 4, 8, w2, 4)
    copies[1].start()
    parts = [static[n] for n in range(5)]
    for n, (w, first) in enumerate(((w0, 0), (w1, 0), (w2, 4))):
        for c in range(3):
            planes = [restrict_plane([get_plane(w, c, j - first) for j in (i - 1, i, i + 1)]) for i in (6, 8)]
            parts.append(side_by_side(planes, rows16.at[n, c]) * static[1])
    split = dot(jnp.concatenate(parts, axis=0), split_matrix(64))
    for a in range(14):
        pack[a] = split[8 * a : 8 * a + 8]
    for copy in copies:
        copy.wait()


def estimate_of(sums, level):
    return jnp.max(sums[2 * level : 2 * level + 1, :] / sums[2 * level + 1 : 2 * level + 2, :])


def polynomial():
    theta, delta = centre_share, half_share
    sigma = theta / delta
    rho0 = 1.0 / sigma
    rho1 = 1.0 / (2.0 * sigma - rho0)
    rho2 = 1.0 / (2.0 * sigma - rho1)
    a10 = rho1 * rho0 / theta + 2.0 * rho1 / delta
    a11 = -2.0 * rho1 / (delta * theta)
    a20 = rho2 * rho1 * a10 + 2.0 * rho2 / delta
    a21 = rho2 * rho1 * a11 - (2.0 * rho2 / delta) * (1.0 / theta + a10)
    a22 = -(2.0 * rho2 / delta) * a11
    return 1.0 / theta + a10 + a20, a11 + a21, a22


def turns():
    sigma = centre_share / half_share
    rho = 1.0 / sigma
    out = []
    for _ in range(2):
        new = 1.0 / (2.0 * sigma - rho)
        out.append((new * rho, 2.0 * new / half_share))
        rho = new
    return out


def residual_factors(sums):
    inv = 1.0 / estimate_of(sums, 0)
    k0, k1, k2 = polynomial()
    return k0 * inv, k1 * inv * inv, k2 * inv * inv * inv


def residual_kernel(sums, load, dinv, w0, w1, w2, res, pre):
    b0, b1, b2 = residual_factors(sums)

    def step(k, carry):
        for c in range(3):
            res[c, k] = load[c, k + 4] - (b0 * w0[c, k + 4] + b1 * w1[c, k + 4] + b2 * w2[c, k])
        return carry

    lax.fori_loop(0, 8, step, 0)
    for k in range(4):
        for c in range(3):
            pre[c, k] = dinv[k + 6] * (b0 * load[c, k + 6] + b1 * w0[c, k + 6] + b2 * w1[c, k + 6])


def sum_kernel(parts, pack, out):
    total = parts[0]
    for n in range(1, parts.shape[0]):
        total = total + parts[n]
    for n in range(out.shape[0]):
        out[n] = total


def combine_kernel(parts, t0, t1, t2, t3, t4, out, sums):
    total = parts[0]
    for n in range(1, 32):
        total = total + parts[n]
    sums[...] = total
    b0, b1, b2 = residual_factors(sums)
    for t, tile in enumerate((t0, t1, t2, t3, t4)):
        out[t, 0:2] = tile[0:2]
        out[t, 2:5] = tile[2:5] - (b0 * tile[5:8] + b1 * tile[8:11] + b2 * tile[11:14])


DST = {(0, 0): 0, (0, 32): 8, (1, 24): -40, (1, 56): -32}


def join_chips_kernel(mine, right, opposite, left, mine2, right2, opposite2, left2, out, first, last):
    lane = lanes_of()
    in_half = lane % 64

    def run(ours, others):
        for t in range(5):
            for a in range(5):
                planes = []
                for near, far in ((0, 2), (1, 3)):
                    for part in (ours, others):
                        one, two = part[near][t, a], part[far][t, a]
                        planes.append(jnp.where(lane < 64, one, roll(two, 64, 1)))
                        planes.append(jnp.where(lane < 64, roll(one, 64, 1), two))
                for i, val in enumerate(planes):
                    out[t, a, i] = val
                for n in range(2):
                    acc = [jnp.zeros(REG, f32) for _ in range(2)]
                    for j in range(4):
                        val = out[t, a, 4 * n + j]
                        for (m, src), offset in DST.items():
                            dst = (offset + 16 * j) % 64
                            inside = (in_half >= dst) & (in_half < dst + 8)
                            acc[m] = jnp.where(inside, roll(val, offset + 16 * j - src, 1), acc[m])
                    first[t, a, n] = acc[0]
                    last[t, a, n] = acc[1]

    one, two = (mine, right, opposite, left), (mine2, right2, opposite2, left2)

    core = lax.axis_index("gx") & 1

    @pl.when(core == 0)
    def _():
        run(one, two)

    @pl.when(core != 0)
    def _():
        run(two, one)


def wrap(ref, planes, *at):
    for y in range(ref.shape[-4]):
        for z in range(ref.shape[-3]):
            ref[at + (0, y, z)] = roll(ref[at + (planes, y, z)], 64, 1)
            ref[at + (planes + 1, y, z)] = roll(ref[at + (1, y, z)], 64, 1)


def smooth(bufs, planes, young, free, dinv, res, x, inv, steps):
    groups, parts = res.shape[-4:-2]
    for src, dst, keep, gain in steps:

        def load_w(i, y, src=src):
            mask = [free[i + 1, y, z] for z in range(parts)]
            return [[src[c, i + 1, y, z] * mask[z] for z in range(parts)] for c in range(3)]

        def emit(i, y, g, src=src, dst=dst, keep=keep, gain=gain):
            for z in range(parts):
                mask = free[i + 1, y, z]
                scaled = None if dst is None else (gain * inv) * dinv[i, y, z]
                for c in range(3):
                    d = src[c, i + 1, y, z]
                    left = res[c, i, y, z] - jnp.where(mask > 0.5, g[c][z], d)
                    res[c, i, y, z] = left
                    if dst is not None:
                        new = keep * d + scaled * left if keep else scaled * left
                        dst[c, i + 1, y, z] = new
                        x[c, i, y, z] = x[c, i, y, z] + new

        apply_planes(bufs, 0, planes, load_w, lambda i, y, z: young[i + 1, y, z], emit)
        if dst is not None:
            for c in range(3):
                wrap(dst, planes, c)


def coarse_kernel(
    sums, chips, from_left, from_right, out,
    nat, young, free, dinv, res, d_a, d_b, x,
    nat2, young2, free2, dinv2, res2, d2_a, d2_b, x2,
    nat3, young3, free3, dinv3, res3, x3, rows_e, rows_o,
    tb, cb, tb2, cb2, tb3, cb3,
):
    lane = lanes_of()
    in_half = lane % 64
    outer = (in_half < 8) | ((in_half >= 40) & (in_half < 48))
    low_slot = lane % 16 < 8
    for t in range(5):
        for a in range(5):
            halos = []
            for n in range(2):
                right, left = from_right[t, a, n], from_left[t, a, n]
                halos.append((jnp.where(low_slot, right, left), jnp.where(low_slot, left, right)))
            for i in range(8):
                val = chips[t, a, i]
                for z in range(2):
                    here = jnp.where((in_half >= 8) & (in_half < 40), roll(val, 8 - 32 * z, 1), 0.0)
                    halo = roll(halos[i // 4][z], 40 - 8 * z - 16 * (i % 4), 1)
                    here = jnp.where(outer, halo, here)
                    nat[a, i, z, 8 * t : 8 * t + 8] = here
    for i in range(8):
        for y in range(5):
            rows = pl.ds(y, 8, stride=5)
            for z in range(2):
                young[i + 1, y, z] = 2.0 * nat[0, i, z, rows]
                free[i + 1, y, z] = nat[1, i, z, rows]
                for c in range(3):
                    res[c, i, y, z] = nat[2 + c, i, z, rows]
    wrap(young, 8)
    wrap(free, 8)

    inv1 = 1.0 / estimate_of(sums, 1)
    inv2 = 1.0 / estimate_of(sums, 2)
    start = 1.0 / centre_share
    later = turns()

    def begin(i, carry):
        total = added(low_sum(get_plane(young, i + 1)), low_sum(get_plane(young, i)))
        for y in range(5):
            for z in range(2):
                inverse = inverse_diagonal(total[y][z], free[i + 1, y, z], 1.0)
                dinv[i, y, z] = inverse
                for c in range(3):
                    d = (start * inv1) * inverse * res[c, i, y, z]
                    d_a[c, i + 1, y, z] = d
                    x[c, i, y, z] = d
        return carry

    lax.fori_loop(0, 8, begin, 0)
    for c in range(3):
        wrap(d_a, 8, c)
    steps = [(d_a, d_b) + later[0], (d_b, d_a) + later[1], (d_a, None, 0.0, 0.0)]
    smooth((tb, cb), 8, young, free, dinv, res, x, inv1, steps)

    for a in range(5):
        for k in range(4):
            nat2[a, k, 0:8] = jnp.zeros(REG, f32)
            nat2[a, k, 48:56] = jnp.zeros(REG, f32)
    for k in range(4):
        for y in range(5):
            rows = pl.ds(8 + y, 8, stride=5)
            both = [young[2 * k + 1, y, z] + young[2 * k + 2, y, z] for z in range(2)]
            nat2[0, k, rows] = both[0] + both[1]
            nat2[1, k, rows] = free[2 * k + 1, y, 0]
            for c in range(3):
                part = []
                for z in range(2):
                    below = res[c, 2 * k - 1, y, z] if k else roll(res[c, 7, y, z], 64, 1)
                    part.append(res[c, 2 * k, y, z] + 0.5 * (below + res[c, 2 * k + 1, y, z]))
                nat2[2 + c, k, rows] = part[0] + 0.5 * (part[1] + roll(part[1], 1, 1))
        for y in range(3):
            at = [pl.ds(8 + 2 * y + n, 8, stride=6) for n in (-1, 0, 1)]
            young2[k + 1, y, 0] = 0.25 * (nat2[0, k, at[1]] + nat2[0, k, at[2]])
            mask = nat2[1, k, at[1]]
            free2[k + 1, y, 0] = mask
            for c in range(3):
                val = nat2[2 + c, k, at[1]] + 0.5 * (nat2[2 + c, k, at[0]] + nat2[2 + c, k, at[2]])
                res2[c, k, y, 0] = val * mask
    wrap(young2, 4)
    wrap(free2, 4)
    for k in range(4):
        total = added(low_sum(get_plane(young2, k + 1)), low_sum(get_plane(young2, k)))
        for y in range(3):
            inverse = inverse_diagonal(total[y][0], free2[k + 1, y, 0], 1.0)
            dinv2[k, y, 0] = inverse
            for c in range(3):
                d = (start * inv2) * inverse * res2[c, k, y, 0]
                d2_a[c, k + 1, y, 0] = d
                x2[c, k, y, 0] = d
    for c in range(3):
        wrap(d2_a, 4, c)
    steps = [(d2_a, d2_b) + later[0], (d2_b, d2_a) + later[1]]
    smooth((tb2, cb2), 4, young2, free2, dinv2, res2, x2, inv2, steps)

    for i in range(8):
        for z in range(2):
            for y in range(5):
                rows = pl.ds(y, 8, stride=5)
                nat[0, i, z, rows] = dinv[i, y, z]
                for c in range(3):
                    nat[1 + c, i, z, rows] = res[c, i, y, z]
            for y in range(3):
                rows = pl.ds(8 + y, 8, stride=3)
                dinv3[i, y, z] = nat[0, i, z, rows]
                for c in range(3):
                    res3[c, i, y, z] = nat[1 + c, i, z, rows]
    for i in range(8):
        for z in range(2):
            for y in range(5):
                rows = pl.ds(y, 8, stride=5)
                nat[0, i, z, rows] = young[i + 1, y, z]
                nat[1, i, z, rows] = free[i + 1, y, z]
                for c in range(3):
                    nat[2 + c, i, z, rows] = x[c, i, y, z]
            for y in range(3):
                rows = pl.ds(8 + y, 8, stride=3)
                young3[i + 1, y, z] = nat[0, i, z, rows]
                free3[i + 1, y, z] = nat[1, i, z, rows]
                for c in range(3):
                    x3[c, i, y, z] = nat[2 + c, i, z, rows]
    wrap(young3, 8)
    wrap(free3, 8)
    d3_a, d3_b = d_a, d_b
    for c in range(3):
        for k in range(4):
            here = [x2[c, k, y, 0] for y in range(3)]
            if k < 3:
                nxt = [x2[c, k + 1, y, 0] for y in range(3)]
            else:
                nxt = [roll(x2[c, 0, y, 0], 64, 1) for y in range(3)]
            for n, val in enumerate((here, [0.5 * (p + q) for p, q in zip(here, nxt)])):
                above = val[1:] + [roll(val[0], -1, 0)]
                for y in range(3):
                    nat3[n, pl.ds(2 * y, 8, stride=6)] = val[y]
                    nat3[n, pl.ds(2 * y + 1, 8, stride=6)] = 0.5 * (val[y] + above[y])
                i = 2 * k + n
                for y in range(3):
                    even = nat3[n, pl.ds(8 + y, 8, stride=3)]
                    odd = 0.5 * (even + roll(even, -1, 1))
                    for z, e in enumerate((even, odd)):
                        e = e * free3[i + 1, y, z]
                        d3_b[c, i + 1, y, z] = e
                        x3[c, i, y, z] = x3[c, i, y, z] + e
        wrap(d3_b, 8, c)
    steps = [(d3_b, d3_a, 0.0, start), (d3_a, d3_b) + later[0], (d3_b, d3_a) + later[1]]
    smooth((tb3, cb3), 8, young3, free3, dinv3, res3, x3, inv1, steps)

    place = 2 * (lax.axis_index("gx") & 1)
    for k in range(6):
        plane = (place + (14 + k)) & 15
        i = plane & 7
        swap = plane > 7
        for c in range(3):
            for y in range(3):
                rows = pl.ds(24 * (3 * k + c) + y, 8, stride=3)
                for z, dst in enumerate((rows_e, rows_o)):
                    val = x3[c, i, y, z]
                    dst[rows] = jnp.where(swap, roll(val, 64, 1), val)
    place_e = matrix(lambda r, c: to_f((r < 48) & (c == (2 * r + 112) % 128)))
    place_o = matrix(lambda r, c: to_f((r < 48) & (c == (2 * r + 113) % 128)))
    out[...] = (dot(rows_e[...], place_e) + dot(rows_o[...], place_o)).reshape(6, 3, 24, 128)


def last_kernel(sums, stat, dinv, res_in, pre, x1, out, e0, res, d_a, d_b, rows, tb, cb):
    inv = 1.0 / estimate_of(sums, 0)
    start = 1.0 / centre_share
    later = turns()

    def raised(c, k):
        at = [x1[k, c, pl.ds(4 + n, 8, stride=2)] for n in range(3)]
        groups = [at[0], 0.5 * (at[0] + at[1]), at[1], 0.5 * (at[1] + at[2])]
        return [[v, 0.5 * (v + roll(v, -1, 1))] for v in groups]

    for c in range(3):
        here = raised(c, 0)
        for k in range(6):
            nxt = raised(c, k + 1) if k < 5 else None
            for y in range(4):
                for z in range(2):
                    e0[c, 2 * k, y, z] = here[y][z] * stat[1, 2 * k + 2, y, z]
                    if k < 5:
                        e0[c, 2 * k + 1, y, z] = 0.5 * (here[y][z] + nxt[y][z]) * stat[1, 2 * k + 3, y, z]
            here = nxt

    def loader(ref, shift):
        def load_w(i, y):
            mask = [stat[1, i, y, z] for z in range(2)]
            return [[ref[c, i - shift, y, z] * mask[z] for z in range(2)] for c in range(3)]

        return load_w

    def emit_e(i, y, g):
        for z in range(2):
            mask = stat[1, i, y, z]
            scaled = (start * inv) * dinv[i, y, z]
            for c in range(3):
                left = res_in[c, i - 4, y, z] - jnp.where(mask > 0.5, g[c][z], e0[c, i - 2, y, z])
                res[c, i - 4, y, z] = left
                d_a[c, i - 4, y, z] = scaled * left

    def emit_a(i, y, g):
        keep, gain = later[0]
        for z in range(2):
            mask = stat[1, i, y, z]
            scaled = (gain * inv) * dinv[i, y, z]
            for c in range(3):
                d = d_a[c, i - 4, y, z]
                left = res[c, i - 4, y, z] - jnp.where(mask > 0.5, g[c][z], d)
                res[c, i - 4, y, z] = left
                d_b[c, i - 4, y, z] = keep * d + scaled * left

    def emit_b(i, y, g):
        keep, gain = later[1]
        total = [[None, None] for _ in range(3)]
        for z in range(2):
            mask = stat[1, i, y, z]
            scaled = (gain * inv) * dinv[i, y, z]
            for c in range(3):
                d = d_b[c, i - 4, y, z]
                left = res[c, i - 4, y, z] - jnp.where(mask > 0.5, g[c][z], d)
                new = keep * d + scaled * left
                old = pre[c, i - 6, y, z] + e0[c, i - 2, y, z] + d_a[c, i - 4, y, z]
                total[c][z] = old + d + new
        for c in range(3):
            val = jnp.where(lanes_of() < 64, total[c][0], roll(total[c][1], 64, 1))
            rows[c, i - 6, pl.ds(y, 8, stride=4)] = val

    young = lambda i, y, z: stat[0, i, y, z]
    apply_planes((tb, cb), 4, 8, loader(e0, 2), young, emit_e)
    apply_planes((tb, cb), 5, 6, loader(d_a, 4), young, emit_a)
    apply_planes((tb, cb), 6, 4, loader(d_b, 4), young, emit_b)
    join = join_matrix()
    for c in range(3):
        for k in range(4):
            out[c, k] = dot(rows[c, k, 8:24], join)


def call(kernel, outs, scratch=(), smem=None, flops=0, limit=3, in_hbm=(), hbm_in=False, plain_out=False):
    def run(*args):
        where = pltpu.HBM if hbm_in else pltpu.VMEM
        specs = [pl.BlockSpec(memory_space=pltpu.SMEM if n == smem else where) for n in range(len(args))]
        args = [a if n == smem else pltpu.with_memory_space_constraint(a, where) for n, a in enumerate(args)]
        spaces = [pltpu.HBM if n in in_hbm else pltpu.VMEM for n in range(len(outs))]
        return pl.pallas_call(
            kernel,
            in_specs=specs,
            out_specs=[pl.BlockSpec(memory_space=space) for space in spaces],
            out_shape=[jax.ShapeDtypeStruct(s, f32) if plain_out else space(s, f32) for s, space in zip(outs, spaces)],
            scratch_shapes=[s if not isinstance(s, tuple) else pltpu.VMEM(s, f32) for s in scratch],
            compiler_params=pltpu.CompilerParams(vmem_limit_bytes=limit * 1024 * 1024),
            cost_estimate=pl.CostEstimate(flops=flops, bytes_accessed=1 << 20, transcendentals=0),
        )(*args)

    return run


def send(value, axis, shift):
    count = lax.axis_size(axis)
    return lax.ppermute(value, axis, [(i, (i + shift) % count) for i in range(count)])


def swap_core(value):
    return lax.ppermute(value, "gx", [(i, i ^ 1) for i in range(lax.axis_size("gx"))])


def local(density_level, support_mask, load_mask, load_vector):
    block = density_level.shape
    ints = [pltpu.VMEM(block, jnp.int32)] * 3
    low, high = call(
        prepare_kernel, [(5, 4, 8, 128)] * 2, ints + [(3,) + block, pltpu.SemaphoreType.DMA((4,))], hbm_in=True
    )(density_level, support_mask, load_mask, load_vector)
    up, down = send(high, "gy", 1), send(low, "gy", -1)
    own, first, last = call(join_y_kernel, [(5, 4, 32, 128), (5, 1, 32, 128), (5, 2, 32, 128)])(up, low, high, down)
    planes = [send(last, "gx", 2), send(own, "gx", 1), own, send(own, "gx", -1), send(first, "gx", -2)]
    first, last = call(pack_z_kernel, [(5, 32, 128)] * 2)(*planes)
    from_left, from_right = send(last, "gz", 1), send(first, "gz", -1)
    fine = (4, 2) + REG
    stat, load, dinv, w0, static, sums = call(
        first_kernel,
        [(2, NXE) + fine, (3, NXE) + fine, (NXE,) + fine, (3, NXE) + fine, (5,) + REG, (8,) + REG],
        [(3, NXE) + fine, (5, 2, 16, 128)] + work_buffers(4, 2) + [pltpu.SemaphoreType.DMA],
        limit=8,
        in_hbm=(1,),
    )(*planes, from_left, from_right)
    w1, w2, pack = call(
        second_kernel,
        [(3, NXE) + fine, (3, 8) + fine, (14,) + REG],
        [(3, NXE) + fine, (3, 8) + fine, (3, 3, 2, 16, 128)] + work_buffers(4, 2) + [pltpu.SemaphoreType.DMA((2,))],
        flops=1 << 26,
        limit=9,
        in_hbm=(0, 1),
    )(stat, dinv, w0, static)
    sums = call(sum_kernel, [(32,) + REG])(lax.all_to_all(sums, "gy", 0, 0), pack)[0]
    tiles = [send(pack, "gy", 2), send(pack, "gy", 1), pack, send(pack, "gy", -1), send(pack, "gy", -2)]
    parts = lax.all_to_all(sums, ("gx", "gz"), 0, 0)
    mine, sums = call(combine_kernel, [(5, 5) + REG, REG])(parts, *tiles)
    res, pre = call(residual_kernel, [(3, 8) + fine, (3, 4) + fine], flops=1 << 22)(sums, load, dinv, w0, w1, w2)
    chips = [mine, send(mine, "gx", -2), send(mine, "gx", 4), send(mine, "gx", 2)]
    chips += [swap_core(val) for val in chips]
    chips, first, last = call(join_chips_kernel, [(5, 5, 8) + REG] + [(5, 5, 2) + REG] * 2)(*chips)
    from_left, from_right = send(last, "gz", 1), send(first, "gz", -1)
    five, three, one = (5, 2) + REG, (3, 2) + REG, (3, 1) + REG
    x1 = call(
        coarse_kernel,
        [(6, 3, 24, 128)],
        [(5, 8, 2, 40, 128), (10,) + five, (10,) + five, (8,) + five]
        + [(3, 8) + five, (3, 10) + five, (3, 10) + five, (3, 8) + five]
        + [(5, 4, 56, 128), (6,) + one, (6,) + one, (4,) + one]
        + [(3, 4) + one, (3, 6) + one, (3, 6) + one, (3, 4) + one]
        + [(2, 48, 128), (10,) + three, (10,) + three, (8,) + three]
        + [(3, 8) + three, (3, 8) + three, (432, 128), (432, 128)]
        + work_buffers(5, 2)
        + work_buffers(3, 1)
        + work_buffers(3, 2),
        limit=20,
    )(sums, chips, from_left, from_right)[0]
    return call(
        last_kernel,
        [(3, 4, 16, 128)],
        [(3, 12) + fine, (3, 8) + fine, (3, 8) + fine, (3, 8) + fine, (3, 4, 32, 128)] + work_buffers(4, 2),
        plain_out=True,
        limit=9,
    )(sums, stat, dinv, res, pre, x1)[0]


def solution(mesh):
    block = P("gx", "gy", "gz")
    return jax.shard_map(
        local,
        mesh=mesh,
        in_specs=(block, block, block, P(None, "gx", "gy", "gz")),
        out_specs=P(None, "gx", "gy", "gz"),
        check_vma=False,
    )
```

```python
import jax
import jax.numpy as jnp
from jax import lax
from jax.experimental import pallas as pl
from jax.experimental.pallas import tpu as pltpu
from jax.sharding import PartitionSpec as P

f32 = jnp.float32
young_floor = 0.001
poisson = 0.3
headroom = 1.5
floor_share = 0.3
lam = poisson / ((1.0 + poisson) * (1.0 - 2.0 * poisson))
mu = 1.0 / (2.0 * (1.0 + poisson))
diag_entry = (lam + 2 * mu + 2 * mu) / 16 + (2 * (lam + 3 * mu) + 2 * mu) / 48 + (lam + 4 * mu) / 144
centre_share = 0.5 * headroom * (1.0 + floor_share)
half_share = 0.5 * headroom * (1.0 - floor_share)

NXE = 15
SS, SD, DS, DD = 0, 1, 2, 3
REG = (8, 128)


def roll(v, amount, axis):
    return pltpu.roll(v, amount % v.shape[axis], axis=axis)


def lanes_of(shape=REG):
    return lax.broadcasted_iota(jnp.int32, shape, 1)


def z_next(p):
    return [p[1], roll(p[0], -1, 1)] if len(p) == 2 else [roll(p[0], -1, 1)]


def z_prev(p):
    return [roll(p[1], 1, 1), p[0]] if len(p) == 2 else [roll(p[0], 1, 1)]


def y_next(plane):
    return plane[1:] + [[roll(v, -1, 0) for v in plane[0]]]


def y_prev(plane):
    return [[roll(v, 1, 0) for v in plane[-1]]] + plane[:-1]


def added(one, two):
    return [[a + b for a, b in zip(p, q)] for p, q in zip(one, two)]


def get_plane(ref, *at):
    groups, parts = ref.shape[-4:-2]
    return [[ref[at + (y, z)] for z in range(parts)] for y in range(groups)]


def element_forces(t0, t1, e):
    u = {}
    for c in range(3):
        for m in range(4):
            u[c, "d", m] = t1[c][m] - t0[c][m]
            if m != SS:
                u[c, "s", m] = t1[c][m] + t0[c][m]
    f = {}
    e_a, e_b, e_c = e * (lam / 16), e * (2 * mu / 16), e * (mu / 16)
    e_d, e_e, e_f = e * (lam / 48), e * (3 * mu / 48), e * (mu / 48)
    e_g = e * ((lam + 4 * mu) / 144)
    normal = ((0, "d", SS), (1, "s", DS), (2, "s", SD))
    t = e_a * (u[normal[0]] + u[normal[1]] + u[normal[2]])
    for key in normal:
        f[key] = t + e_b * u[key]
    for one, two in (((0, "s", DS), (1, "d", SS)), ((1, "s", SD), (2, "s", DS)), ((0, "s", SD), (2, "d", SS))):
        f[one] = f[two] = e_c * (u[one] + u[two])
    for one, two in (((0, "d", DS), (2, "s", DD)), ((0, "d", SD), (1, "s", DD)), ((1, "d", DS), (2, "d", SD))):
        p = e_d * (u[one] + u[two])
        f[one] = p + e_e * u[one]
        f[two] = p + e_e * u[two]
    triple = ((0, "s", DD), (1, "d", SD), (2, "d", DS))
    q = u[triple[0]] + u[triple[1]] + u[triple[2]]
    for key in triple:
        f[key] = e_f * (u[key] + q)
    for c in range(3):
        f[c, "d", DD] = e_g * u[c, "d", DD]
    return u, f


def z_modes(w):
    out = []
    for p in w:
        out.append([(a + b, b - a) for a, b in zip(p, z_next(p))])
    return out


def y_modes(cur, nxt):
    return [[(s + su, d + du, su - s, du - d) for (s, d), (su, du) in zip(p, q)] for p, q in zip(cur, nxt)]


def rows_above(first):
    return [[tuple(roll(v, -1, 0) for v in pair) for pair in p] for p in first]


def forward_plane(t, groups, load_w):
    first = cur = z_modes(load_w(0))
    for y in range(groups):
        nxt = z_modes(load_w(y + 1)) if y < groups - 1 else rows_above(first)
        for c, p in enumerate(y_modes(cur, nxt)):
            for z, vals in enumerate(p):
                for m, val in enumerate(vals):
                    t[4 * c + m, y, z] = val
        cur = nxt


def finish_rows(low, high):
    res = []
    for one, two in zip(low, high):
        s = [a[0] + b[0] for a, b in zip(one, two)]
        d = [a[1] + b[1] for a, b in zip(one, two)]
        down = [a - b for a, b in zip(s, d)]
        up = z_prev([a + b for a, b in zip(s, d)])
        res.append([a + b for a, b in zip(down, up)])
    return res


def element_plane(t0_ref, t1_ref, c_ref, groups, parts, load_w, load_e, emit, fresh):
    first = cur = z_modes(load_w(0))
    prev = start = None
    for y in range(groups):
        nxt = z_modes(load_w(y + 1)) if y < groups - 1 else rows_above(first)
        t1 = y_modes(cur, nxt)
        low = [[None] * parts for _ in range(3)]
        high = [[None] * parts for _ in range(3)]
        for z in range(parts):
            t0 = [[t0_ref[4 * c + m, y, z] for m in range(4)] for c in range(3)]
            for c in range(3):
                for m in range(4):
                    t1_ref[4 * c + m, y, z] = t1[c][z][m]
            u, f = element_forces(t0, [t1[c][z] for c in range(3)], load_e(y, z))
            for c in range(3):
                g = []
                for m in range(4):
                    d = f[c, "d", m]
                    if not fresh:
                        old = c_ref[4 * c + m, y, z]
                        g.append(old - d if m == SS else old + (f[c, "s", m] - d))
                    c_ref[4 * c + m, y, z] = d if m == SS else f[c, "s", m] + d
                if not fresh:
                    low[c][z] = (g[SS] - g[DS], g[SD] - g[DD])
                    high[c][z] = (g[SS] + g[DS], g[SD] + g[DD])
        if not fresh:
            if y == 0:
                start = low
            else:
                emit(y, finish_rows(low, prev))
            prev = high
        cur = nxt
    if not fresh:
        last = [[tuple(roll(v, 1, 0) for v in pair) for pair in p] for p in prev]
        emit(0, finish_rows(start, last))


def apply_planes(bufs, lo, n, load_w, load_e, emit):
    t_ref, c_ref = bufs
    groups, parts = c_ref.shape[1:3]

    def one(i, a, fresh=False):
        element_plane(
            t_ref.at[a],
            t_ref.at[1 - a],
            c_ref,
            groups,
            parts,
            lambda y: load_w(i + 1, y),
            lambda y, z: load_e(i, y, z),
            lambda y, res: emit(i, y, res),
            fresh,
        )

    forward_plane(t_ref.at[0], groups, lambda y: load_w(lo - 1, y))
    one(lo - 1, 0, True)

    def step(j, carry):
        one(lo + 2 * j, 1)
        one(lo + 2 * j + 1, 0)
        return carry

    lax.fori_loop(0, n // 2, step, 0)


def work_buffers(groups, parts):
    return [pltpu.VMEM((2, 12, groups, parts) + REG, f32), pltpu.VMEM((12, groups, parts) + REG, f32)]


def low_sum(plane):
    plane = [[a + b for a, b in zip(p, z_prev(p))] for p in plane]
    return added(plane, y_prev(plane))


def inverse_diagonal(e_sum, free, scale):
    return jnp.where(free > 0.5, 1.0 / (e_sum * (diag_entry * scale)), 1.0)


def matrix(fun):
    shape = (128, 128)
    r = lax.broadcasted_iota(jnp.int32, shape, 0)
    c = lax.broadcasted_iota(jnp.int32, shape, 1)
    return fun(r, c)


def dot(a, b):
    return jnp.dot(a, b, precision=lax.Precision.HIGHEST, preferred_element_type=f32)


def to_f(cond, val=1.0):
    return jnp.where(cond, f32(val), f32(0.0))


def split_matrix(width):
    def fun(r, c):
        z = r % width
        return to_f(c == r - z + (z % 2) * (width // 2) + z // 2)

    return matrix(fun)


def join_matrix():
    return matrix(lambda r, c: to_f(c == (r % 64) * 2 + r // 64))


def prepare_kernel(density, support, load, vector, low, high, a_buf, b_buf, c_buf, v_buf, sem):
    copies = []
    for n, (src, dst) in enumerate(((density, a_buf), (support, b_buf), (load, c_buf), (vector, v_buf))):
        copies.append(pltpu.make_async_copy(src, dst, sem.at[n]))
        copies[-1].start()
    for copy in copies:
        copy.wait()
    scaled = a_buf[...].astype(f32) / 255.0
    young = young_floor + (1.0 - young_floor) * scaled * scaled * scaled
    free = 1.0 - b_buf[...].astype(f32)
    masked = free * c_buf[...].astype(f32)
    split = split_matrix(128)
    rows = [young, free] + [masked * v_buf[c] for c in range(3)]
    for a, val in enumerate(rows):
        val = dot(val.reshape(64, 128), split).reshape(4, 16, 128)
        low[a] = val[:, 0:8]
        high[a] = val[:, 8:16]


def join_y_kernel(up, low, high, down, own, first, last):
    for t, tile in enumerate((up, low, high, down)):
        rows = slice(8 * t, 8 * t + 8)
        for a in range(5):
            own[a, :, rows] = tile[a]
            first[a, :, rows] = tile[a, 0:1]
            last[a, :, rows] = tile[a, 2:4]


def plane_refs(far_left, left, own, right, far_right):
    return [(ref, k) for ref, n in ((far_left, 2), (left, 4), (own, 4), (right, 4), (far_right, 1)) for k in range(n)]


def pack_z_kernel(far_left, left, own, right, far_right, first, last):
    planes = plane_refs(far_left, left, own, right, far_right)
    lane = lanes_of() % 64
    for a in range(5):
        for t in range(4):
            acc_first = jnp.zeros(REG, f32)
            acc_last = jnp.zeros(REG, f32)
            for g in range(NXE):
                ref, k = planes[g]
                val = ref[a, k, 8 * t : 8 * t + 8]
                inside = (lane >= 4 * g) & (lane < 4 * g + 4)
                acc_first = jnp.where(inside, roll(val, 4 * g, 1), acc_first)
                acc_last = jnp.where(inside, roll(val, 4 * g - 60, 1), acc_last)
            first[a, 8 * t : 8 * t + 8] = acc_first
            last[a, 8 * t : 8 * t + 8] = acc_last


def first_kernel(
    far_left, left, mid, right, far_right, from_left, from_right,
    stat, load, dinv, w0, static, sums, rows16, tb, cb,
):
    lane = lanes_of()
    planes = plane_refs(far_left, left, mid, right, far_right)
    outer = ((lane >= 64) & (lane < 68)) | (lane >= 124)
    for a in range(5):
        for y in range(4):
            rows = pl.ds(y, 8, stride=4)
            left = from_left[a, rows]
            right = from_right[a, rows]
            halo_e = jnp.where(lane < 60, right, roll(left, 60, 1))
            halo_o = jnp.where(lane < 60, roll(right, 64, 1), roll(left, -4, 1))
            for g in range(NXE):
                ref, k = planes[g]
                own = ref[a, k, rows]
                even = jnp.where(outer, roll(halo_e, 64 - 4 * g, 1), jnp.where(lane < 64, own, 0.0))
                odd = jnp.where(outer, roll(halo_o, 64 - 4 * g, 1), jnp.where(lane < 64, roll(own, 64, 1), 0.0))
                for z, val in enumerate((even, odd)):
                    if a < 2:
                        stat[a, g, y, z] = val
                    else:
                        load[a - 2, g, y, z] = val

    def diag_step(i, carry):
        total = added(low_sum(get_plane(stat, 0, i)), low_sum(get_plane(stat, 0, jnp.maximum(i - 1, 0))))
        for y in range(4):
            for z in range(2):
                dinv[i, y, z] = inverse_diagonal(total[y][z], stat[1, i, y, z], 1.0)
        return carry

    lax.fori_loop(0, NXE, diag_step, 0)

    def load_w(i, y):
        scaled = [dinv[i, y, z] * stat[1, i, y, z] for z in range(2)]
        return [[load[c, i, y, z] * scaled[z] for z in range(2)] for c in range(3)]

    def emit(i, y, g):
        for z in range(2):
            free = stat[1, i, y, z]
            inv = dinv[i, y, z]
            for c in range(3):
                w0[c, i - 6, y, z] = jnp.where(free > 0.5, g[c][z], load[c, i, y, z] * inv)

    apply_planes((tb, cb), 6, 4, load_w, lambda i, y, z: stat[0, i, y, z], emit)

    sub = lax.broadcasted_iota(jnp.int32, REG, 0)
    own_rows = (sub >= 2) & (sub < 6)

    def masked_sum(val, count):
        return jnp.sum(jnp.where(own_rows & (lane < count), val, 0.0))

    num = jnp.zeros(REG, f32)
    den = jnp.zeros(REG, f32)
    for i in range(6, 10):
        for y in range(4):
            for z in range(2):
                for c in range(3):
                    b = load[c, i, y, z]
                    v = b * dinv[i, y, z]
                    num = num + v * w0[c, i - 6, y, z]
                    den = den + v * b
    totals = [masked_sum(num, 64), masked_sum(den, 64)]

    f1 = [[[stat[1, 2 * k + 4, y, 0]] for y in (0, 2)] for k in range(5)]
    c1 = []
    for k in range(5):
        i = 2 * k + 4
        c1.append([])
        for c in range(3):
            c1[k].append(restrict_plane([get_plane(load, c, j) for j in (i - 1, i, i + 1)], f1[k]))
    y1 = []
    for k in range(6):
        both = added(get_plane(stat, 0, 2 * k + 2), get_plane(stat, 0, 2 * k + 3))
        y1.append([[0.125 * (both[y][0] + both[y][1] + both[y + 1][0] + both[y + 1][1])] for y in (0, 2)])

    def level_sums(nodes, elements, frees, scale, lanes):
        count = len(frees) - 1
        num = jnp.zeros(REG, f32)
        den = jnp.zeros(REG, f32)
        groups = len(frees[0])
        modes = []
        for k in range(count + 1):
            total = added(low_sum(elements[k]), low_sum(elements[k + 1]))
            inv = [inverse_diagonal(total[y][0], frees[k][y][0], scale) for y in range(groups)]
            v = [[nodes[k][c][y][0] * inv[y] for y in range(groups)] for c in range(3)]
            zs = [z_modes([[v[c][y] * frees[k][y][0]] for c in range(3)]) for y in range(groups)]
            zs.append(rows_above(zs[0]))
            modes.append([y_modes(zs[y], zs[y + 1]) for y in range(groups)])
            if k < count:
                for c in range(3):
                    for y in range(groups):
                        num = num + jnp.where(frees[k][y][0] > 0.5, 0.0, v[c][y] * v[c][y])
                        den = den + v[c][y] * nodes[k][c][y][0]
        for k in range(count):
            for y in range(groups):
                u, f = element_forces(
                    [modes[k][y][c][0] for c in range(3)],
                    [modes[k + 1][y][c][0] for c in range(3)],
                    elements[k + 1][y][0] * scale,
                )
                for key in f:
                    num = num + u[key] * f[key]
        return [masked_sum(num, lanes), masked_sum(den, lanes)]

    totals += level_sums(c1[1:4], y1[1:5], f1[1:4], 2.0, 64)

    pick = matrix(lambda r, c: to_f(r == 2 * (c % 64)))
    mean = matrix(lambda r, c: to_f((r == 2 * (c % 64)) | (r == 2 * (c % 64) + 1), 0.5))
    half = matrix(
        lambda r, c: to_f(r == 2 * (c % 64)) + to_f((r == 2 * (c % 64) + 1) | (r == (2 * (c % 64) - 1) % 128), 0.5)
    )
    f2 = [[[dot(f1[k][0][0], pick)]] for k in (1, 3)]
    c2 = []
    for n, k in enumerate((1, 3)):
        c2.append([])
        for c in range(3):
            x = [c1[k][c][y][0] + 0.5 * (c1[k - 1][c][y][0] + c1[k + 1][c][y][0]) for y in range(2)]
            val = x[0] + 0.5 * (x[1] + roll(x[1], 1, 0))
            c2[n].append([[dot(val, half) * f2[n][0][0]]])
    y2 = []
    for k in (0, 2, 4):
        val = 0.25 * (y1[k][0][0] + y1[k][1][0] + y1[k + 1][0][0] + y1[k + 1][1][0])
        y2.append([[dot(val, mean)]])
    totals += level_sums(c2, y2, f2, 4.0, 32)

    row = lax.broadcasted_iota(jnp.int32, REG, 0)
    out = jnp.zeros(REG, f32)
    for k, total in enumerate(totals):
        out = jnp.where(row == k, total, out)
    for n in range(8):
        sums[n] = out

    for n, planes in enumerate([y1[2:4], f1[1:3]] + [[c1[1][c], c1[2][c]] for c in range(3)]):
        static[n] = side_by_side(planes, rows16.at[n])


def restrict_plane(planes, free=None):
    low, mid, high = planes
    x = [[b + 0.5 * (a + c) for a, b, c in zip(*p)] for p in zip(low, mid, high)]
    y = []
    for n in range(2):
        below = [roll(v, 1, 0) for v in x[3]] if n == 0 else x[1]
        y.append([b + 0.5 * (a + c) for a, b, c in zip(below, x[2 * n], x[2 * n + 1])])
    out = []
    for n in range(2):
        even, odd = y[n]
        val = even + 0.5 * (odd + roll(odd, 1, 1))
        out.append([val if free is None else val * free[n][0]])
    return out


def side_by_side(planes, rows16):
    vals = []
    for n, plane in enumerate(planes):
        for y in range(2):
            rows16[n, pl.ds(y, 8, stride=2)] = plane[y][0]
        vals.append(rows16[n, 4:12])
    return jnp.where(lanes_of() < 64, vals[0], roll(vals[1], 64, 1))


def second_kernel(
    stat, dinv, own_w0, load, static, w0_out, w1_out, w2_out, pack, w0, w1, w2, rows16, tb, cb, sem
):
    def run(src, lo, n, dst, first):
        def load_w(i, y):
            scaled = [dinv[i, y, z] * stat[1, i, y, z] for z in range(2)]
            return [[src[c, i, y, z] * scaled[z] for z in range(2)] for c in range(3)]

        def emit(i, y, g):
            for z in range(2):
                free = stat[1, i, y, z]
                inv = dinv[i, y, z]
                for c in range(3):
                    dst[c, i - first, y, z] = jnp.where(free > 0.5, g[c][z], src[c, i, y, z] * inv)

        apply_planes((tb, cb), lo, n, load_w, lambda i, y, z: stat[0, i, y, z], emit)

    pairs = ((w0, w0_out), (w1, w1_out), (w2, w2_out))
    copies = [pltpu.make_async_copy(src, dst, sem.at[n]) for n, (src, dst) in enumerate(pairs)]
    for c in range(3):
        for k in range(4):
            w0[c, k + 6] = own_w0[c, k]
    run(load, 2, 4, w0, 0)
    run(load, 10, 4, w0, 0)
    copies[0].start()
    run(w0, 3, 10, w1, 0)
    copies[1].start()
    run(w1, 4, 8, w2, 4)
    copies[2].start()
    parts = [static[n] for n in range(5)]
    for n, (w, first) in enumerate(((w0, 0), (w1, 0), (w2, 4))):
        for c in range(3):
            planes = [restrict_plane([get_plane(w, c, j - first) for j in (i - 1, i, i + 1)]) for i in (6, 8)]
            parts.append(side_by_side(planes, rows16.at[n, c]) * static[1])
    split = dot(jnp.concatenate(parts, axis=0), split_matrix(64))
    for a in range(14):
        pack[a] = split[8 * a : 8 * a + 8]
    for copy in copies:
        copy.wait()


def estimate_of(sums, level):
    return jnp.max(sums[2 * level : 2 * level + 1, :] / sums[2 * level + 1 : 2 * level + 2, :])


def polynomial():
    theta, delta = centre_share, half_share
    sigma = theta / delta
    rho0 = 1.0 / sigma
    rho1 = 1.0 / (2.0 * sigma - rho0)
    rho2 = 1.0 / (2.0 * sigma - rho1)
    a10 = rho1 * rho0 / theta + 2.0 * rho1 / delta
    a11 = -2.0 * rho1 / (delta * theta)
    a20 = rho2 * rho1 * a10 + 2.0 * rho2 / delta
    a21 = rho2 * rho1 * a11 - (2.0 * rho2 / delta) * (1.0 / theta + a10)
    a22 = -(2.0 * rho2 / delta) * a11
    return 1.0 / theta + a10 + a20, a11 + a21, a22


def turns():
    sigma = centre_share / half_share
    rho = 1.0 / sigma
    out = []
    for _ in range(2):
        new = 1.0 / (2.0 * sigma - rho)
        out.append((new * rho, 2.0 * new / half_share))
        rho = new
    return out


def residual_factors(sums):
    inv = 1.0 / estimate_of(sums, 0)
    k0, k1, k2 = polynomial()
    return k0 * inv, k1 * inv * inv, k2 * inv * inv * inv


def residual_kernel(sums, load, dinv, w0, w1, w2, res, pre):
    b0, b1, b2 = residual_factors(sums)

    def step(k, carry):
        for c in range(3):
            res[c, k] = load[c, k + 4] - (b0 * w0[c, k + 4] + b1 * w1[c, k + 4] + b2 * w2[c, k])
        return carry

    lax.fori_loop(0, 8, step, 0)
    for k in range(4):
        for c in range(3):
            pre[c, k] = dinv[k + 6] * (b0 * load[c, k + 6] + b1 * w0[c, k + 6] + b2 * w1[c, k + 6])


def sum_kernel(parts, pack, out):
    total = parts[0]
    for n in range(1, parts.shape[0]):
        total = total + parts[n]
    for n in range(out.shape[0]):
        out[n] = total


def combine_kernel(parts, t0, t1, t2, t3, t4, out, sums):
    total = parts[0]
    for n in range(1, 32):
        total = total + parts[n]
    sums[...] = total
    b0, b1, b2 = residual_factors(sums)
    for t, tile in enumerate((t0, t1, t2, t3, t4)):
        out[t, 0:2] = tile[0:2]
        out[t, 2:5] = tile[2:5] - (b0 * tile[5:8] + b1 * tile[8:11] + b2 * tile[11:14])


DST = {(0, 0): 0, (0, 32): 8, (1, 24): -40, (1, 56): -32}


def join_chips_kernel(mine, right, opposite, left, mine2, right2, opposite2, left2, out, first, last):
    lane = lanes_of()
    in_half = lane % 64

    def run(ours, others):
        for t in range(5):
            for a in range(5):
                planes = []
                for near, far in ((0, 2), (1, 3)):
                    for part in (ours, others):
                        one, two = part[near][t, a], part[far][t, a]
                        planes.append(jnp.where(lane < 64, one, roll(two, 64, 1)))
                        planes.append(jnp.where(lane < 64, roll(one, 64, 1), two))
                for i, val in enumerate(planes):
                    out[t, a, i] = val
                for n in range(2):
                    acc = [jnp.zeros(REG, f32) for _ in range(2)]
                    for j in range(4):
                        val = out[t, a, 4 * n + j]
                        for (m, src), offset in DST.items():
                            dst = (offset + 16 * j) % 64
                            inside = (in_half >= dst) & (in_half < dst + 8)
                            acc[m] = jnp.where(inside, roll(val, offset + 16 * j - src, 1), acc[m])
                    first[t, a, n] = acc[0]
                    last[t, a, n] = acc[1]

    one, two = (mine, right, opposite, left), (mine2, right2, opposite2, left2)

    core = lax.axis_index("gx") & 1

    @pl.when(core == 0)
    def _():
        run(one, two)

    @pl.when(core != 0)
    def _():
        run(two, one)


def wrap(ref, planes, *at):
    for y in range(ref.shape[-4]):
        for z in range(ref.shape[-3]):
            ref[at + (0, y, z)] = roll(ref[at + (planes, y, z)], 64, 1)
            ref[at + (planes + 1, y, z)] = roll(ref[at + (1, y, z)], 64, 1)


def smooth(bufs, planes, young, free, dinv, res, x, inv, steps):
    groups, parts = res.shape[-4:-2]
    for src, dst, keep, gain in steps:

        def load_w(i, y, src=src):
            mask = [free[i + 1, y, z] for z in range(parts)]
            return [[src[c, i + 1, y, z] * mask[z] for z in range(parts)] for c in range(3)]

        def emit(i, y, g, src=src, dst=dst, keep=keep, gain=gain):
            for z in range(parts):
                mask = free[i + 1, y, z]
                scaled = None if dst is None else (gain * inv) * dinv[i, y, z]
                for c in range(3):
                    d = src[c, i + 1, y, z]
                    left = res[c, i, y, z] - jnp.where(mask > 0.5, g[c][z], d)
                    res[c, i, y, z] = left
                    if dst is not None:
                        new = keep * d + scaled * left if keep else scaled * left
                        dst[c, i + 1, y, z] = new
                        x[c, i, y, z] = x[c, i, y, z] + new

        apply_planes(bufs, 0, planes, load_w, lambda i, y, z: young[i + 1, y, z], emit)
        if dst is not None:
            for c in range(3):
                wrap(dst, planes, c)


def coarse_kernel(
    sums, chips, from_left, from_right, out,
    nat, young, free, dinv, res, d_a, d_b, x,
    nat2, young2, free2, dinv2, res2, d2_a, d2_b, x2,
    nat3, young3, free3, dinv3, res3, x3, rows_e, rows_o,
    tb, cb, tb2, cb2, tb3, cb3,
):
    lane = lanes_of()
    in_half = lane % 64
    outer = (in_half < 8) | ((in_half >= 40) & (in_half < 48))
    low_slot = lane % 16 < 8
    for t in range(5):
        for a in range(5):
            halos = []
            for n in range(2):
                right, left = from_right[t, a, n], from_left[t, a, n]
                halos.append((jnp.where(low_slot, right, left), jnp.where(low_slot, left, right)))
            for i in range(8):
                val = chips[t, a, i]
                for z in range(2):
                    here = jnp.where((in_half >= 8) & (in_half < 40), roll(val, 8 - 32 * z, 1), 0.0)
                    halo = roll(halos[i // 4][z], 40 - 8 * z - 16 * (i % 4), 1)
                    here = jnp.where(outer, halo, here)
                    nat[a, i, z, 8 * t : 8 * t + 8] = here
    for i in range(8):
        for y in range(5):
            rows = pl.ds(y, 8, stride=5)
            for z in range(2):
                young[i + 1, y, z] = 2.0 * nat[0, i, z, rows]
                free[i + 1, y, z] = nat[1, i, z, rows]
                for c in range(3):
                    res[c, i, y, z] = nat[2 + c, i, z, rows]
    wrap(young, 8)
    wrap(free, 8)

    inv1 = 1.0 / estimate_of(sums, 1)
    inv2 = 1.0 / estimate_of(sums, 2)
    start = 1.0 / centre_share
    later = turns()

    def begin(i, carry):
        total = added(low_sum(get_plane(young, i + 1)), low_sum(get_plane(young, i)))
        for y in range(5):
            for z in range(2):
                inverse = inverse_diagonal(total[y][z], free[i + 1, y, z], 1.0)
                dinv[i, y, z] = inverse
                for c in range(3):
                    d = (start * inv1) * inverse * res[c, i, y, z]
                    d_a[c, i + 1, y, z] = d
                    x[c, i, y, z] = d
        return carry

    lax.fori_loop(0, 8, begin, 0)
    for c in range(3):
        wrap(d_a, 8, c)
    steps = [(d_a, d_b) + later[0], (d_b, d_a) + later[1], (d_a, None, 0.0, 0.0)]
    smooth((tb, cb), 8, young, free, dinv, res, x, inv1, steps)

    for a in range(5):
        for k in range(4):
            nat2[a, k, 0:8] = jnp.zeros(REG, f32)
            nat2[a, k, 48:56] = jnp.zeros(REG, f32)
    for k in range(4):
        for y in range(5):
            rows = pl.ds(8 + y, 8, stride=5)
            both = [young[2 * k + 1, y, z] + young[2 * k + 2, y, z] for z in range(2)]
            nat2[0, k, rows] = both[0] + both[1]
            nat2[1, k, rows] = free[2 * k + 1, y, 0]
            for c in range(3):
                part = []
                for z in range(2):
                    below = res[c, 2 * k - 1, y, z] if k else roll(res[c, 7, y, z], 64, 1)
                    part.append(res[c, 2 * k, y, z] + 0.5 * (below + res[c, 2 * k + 1, y, z]))
                nat2[2 + c, k, rows] = part[0] + 0.5 * (part[1] + roll(part[1], 1, 1))
        for y in range(3):
            at = [pl.ds(8 + 2 * y + n, 8, stride=6) for n in (-1, 0, 1)]
            young2[k + 1, y, 0] = 0.25 * (nat2[0, k, at[1]] + nat2[0, k, at[2]])
            mask = nat2[1, k, at[1]]
            free2[k + 1, y, 0] = mask
            for c in range(3):
                val = nat2[2 + c, k, at[1]] + 0.5 * (nat2[2 + c, k, at[0]] + nat2[2 + c, k, at[2]])
                res2[c, k, y, 0] = val * mask
    wrap(young2, 4)
    wrap(free2, 4)
    for k in range(4):
        total = added(low_sum(get_plane(young2, k + 1)), low_sum(get_plane(young2, k)))
        for y in range(3):
            inverse = inverse_diagonal(total[y][0], free2[k + 1, y, 0], 1.0)
            dinv2[k, y, 0] = inverse
            for c in range(3):
                d = (start * inv2) * inverse * res2[c, k, y, 0]
                d2_a[c, k + 1, y, 0] = d
                x2[c, k, y, 0] = d
    for c in range(3):
        wrap(d2_a, 4, c)
    steps = [(d2_a, d2_b) + later[0], (d2_b, d2_a) + later[1]]
    smooth((tb2, cb2), 4, young2, free2, dinv2, res2, x2, inv2, steps)

    for i in range(8):
        for z in range(2):
            for y in range(5):
                rows = pl.ds(y, 8, stride=5)
                nat[0, i, z, rows] = dinv[i, y, z]
                for c in range(3):
                    nat[1 + c, i, z, rows] = res[c, i, y, z]
            for y in range(3):
                rows = pl.ds(8 + y, 8, stride=3)
                dinv3[i, y, z] = nat[0, i, z, rows]
                for c in range(3):
                    res3[c, i, y, z] = nat[1 + c, i, z, rows]
    for i in range(8):
        for z in range(2):
            for y in range(5):
                rows = pl.ds(y, 8, stride=5)
                nat[0, i, z, rows] = young[i + 1, y, z]
                nat[1, i, z, rows] = free[i + 1, y, z]
                for c in range(3):
                    nat[2 + c, i, z, rows] = x[c, i, y, z]
            for y in range(3):
                rows = pl.ds(8 + y, 8, stride=3)
                young3[i + 1, y, z] = nat[0, i, z, rows]
                free3[i + 1, y, z] = nat[1, i, z, rows]
                for c in range(3):
                    x3[c, i, y, z] = nat[2 + c, i, z, rows]
    wrap(young3, 8)
    wrap(free3, 8)
    d3_a, d3_b = d_a, d_b
    for c in range(3):
        for k in range(4):
            here = [x2[c, k, y, 0] for y in range(3)]
            if k < 3:
                nxt = [x2[c, k + 1, y, 0] for y in range(3)]
            else:
                nxt = [roll(x2[c, 0, y, 0], 64, 1) for y in range(3)]
            for n, val in enumerate((here, [0.5 * (p + q) for p, q in zip(here, nxt)])):
                above = val[1:] + [roll(val[0], -1, 0)]
                for y in range(3):
                    nat3[n, pl.ds(2 * y, 8, stride=6)] = val[y]
                    nat3[n, pl.ds(2 * y + 1, 8, stride=6)] = 0.5 * (val[y] + above[y])
                i = 2 * k + n
                for y in range(3):
                    even = nat3[n, pl.ds(8 + y, 8, stride=3)]
                    odd = 0.5 * (even + roll(even, -1, 1))
                    for z, e in enumerate((even, odd)):
                        e = e * free3[i + 1, y, z]
                        d3_b[c, i + 1, y, z] = e
                        x3[c, i, y, z] = x3[c, i, y, z] + e
        wrap(d3_b, 8, c)
    steps = [(d3_b, d3_a, 0.0, start), (d3_a, d3_b) + later[0], (d3_b, d3_a) + later[1]]
    smooth((tb3, cb3), 8, young3, free3, dinv3, res3, x3, inv1, steps)

    place = 2 * (lax.axis_index("gx") & 1)
    for k in range(6):
        plane = (place + (14 + k)) & 15
        i = plane & 7
        swap = plane > 7
        for c in range(3):
            for y in range(3):
                rows = pl.ds(24 * (3 * k + c) + y, 8, stride=3)
                for z, dst in enumerate((rows_e, rows_o)):
                    val = x3[c, i, y, z]
                    dst[rows] = jnp.where(swap, roll(val, 64, 1), val)
    place_e = matrix(lambda r, c: to_f((r < 48) & (c == (2 * r + 112) % 128)))
    place_o = matrix(lambda r, c: to_f((r < 48) & (c == (2 * r + 113) % 128)))
    out[...] = (dot(rows_e[...], place_e) + dot(rows_o[...], place_o)).reshape(6, 3, 24, 128)


def last_kernel(sums, stat, dinv, res_in, pre, x1, out, e0, res, d_a, d_b, rows, tb, cb):
    inv = 1.0 / estimate_of(sums, 0)
    start = 1.0 / centre_share
    later = turns()

    def raised(c, k):
        at = [x1[k, c, pl.ds(4 + n, 8, stride=2)] for n in range(3)]
        groups = [at[0], 0.5 * (at[0] + at[1]), at[1], 0.5 * (at[1] + at[2])]
        return [[v, 0.5 * (v + roll(v, -1, 1))] for v in groups]

    for c in range(3):
        here = raised(c, 0)
        for k in range(6):
            nxt = raised(c, k + 1) if k < 5 else None
            for y in range(4):
                for z in range(2):
                    e0[c, 2 * k, y, z] = here[y][z] * stat[1, 2 * k + 2, y, z]
                    if k < 5:
                        e0[c, 2 * k + 1, y, z] = 0.5 * (here[y][z] + nxt[y][z]) * stat[1, 2 * k + 3, y, z]
            here = nxt

    def loader(ref, shift):
        def load_w(i, y):
            mask = [stat[1, i, y, z] for z in range(2)]
            return [[ref[c, i - shift, y, z] * mask[z] for z in range(2)] for c in range(3)]

        return load_w

    def emit_e(i, y, g):
        for z in range(2):
            mask = stat[1, i, y, z]
            scaled = (start * inv) * dinv[i, y, z]
            for c in range(3):
                left = res_in[c, i - 4, y, z] - jnp.where(mask > 0.5, g[c][z], e0[c, i - 2, y, z])
                res[c, i - 4, y, z] = left
                d_a[c, i - 4, y, z] = scaled * left

    def emit_a(i, y, g):
        keep, gain = later[0]
        for z in range(2):
            mask = stat[1, i, y, z]
            scaled = (gain * inv) * dinv[i, y, z]
            for c in range(3):
                d = d_a[c, i - 4, y, z]
                left = res[c, i - 4, y, z] - jnp.where(mask > 0.5, g[c][z], d)
                res[c, i - 4, y, z] = left
                d_b[c, i - 4, y, z] = keep * d + scaled * left

    def emit_b(i, y, g):
        keep, gain = later[1]
        total = [[None, None] for _ in range(3)]
        for z in range(2):
            mask = stat[1, i, y, z]
            scaled = (gain * inv) * dinv[i, y, z]
            for c in range(3):
                d = d_b[c, i - 4, y, z]
                left = res[c, i - 4, y, z] - jnp.where(mask > 0.5, g[c][z], d)
                new = keep * d + scaled * left
                old = pre[c, i - 6, y, z] + e0[c, i - 2, y, z] + d_a[c, i - 4, y, z]
                total[c][z] = old + d + new
        for c in range(3):
            val = jnp.where(lanes_of() < 64, total[c][0], roll(total[c][1], 64, 1))
            rows[c, i - 6, pl.ds(y, 8, stride=4)] = val

    young = lambda i, y, z: stat[0, i, y, z]
    apply_planes((tb, cb), 4, 8, loader(e0, 2), young, emit_e)
    apply_planes((tb, cb), 5, 6, loader(d_a, 4), young, emit_a)
    apply_planes((tb, cb), 6, 4, loader(d_b, 4), young, emit_b)
    join = join_matrix()
    for c in range(3):
        for k in range(4):
            out[c, k] = dot(rows[c, k, 8:24], join)


def call(kernel, outs, scratch=(), smem=None, flops=0, limit=3, in_hbm=(), hbm_in=False, plain_out=False):
    def run(*args):
        where = pltpu.HBM if hbm_in else pltpu.VMEM
        specs = [pl.BlockSpec(memory_space=pltpu.SMEM if n == smem else where) for n in range(len(args))]
        args = [a if n == smem else pltpu.with_memory_space_constraint(a, where) for n, a in enumerate(args)]
        spaces = [pltpu.HBM if n in in_hbm else pltpu.VMEM for n in range(len(outs))]
        return pl.pallas_call(
            kernel,
            in_specs=specs,
            out_specs=[pl.BlockSpec(memory_space=space) for space in spaces],
            out_shape=[jax.ShapeDtypeStruct(s, f32) if plain_out else space(s, f32) for s, space in zip(outs, spaces)],
            scratch_shapes=[s if not isinstance(s, tuple) else pltpu.VMEM(s, f32) for s in scratch],
            compiler_params=pltpu.CompilerParams(vmem_limit_bytes=limit * 1024 * 1024),
            cost_estimate=pl.CostEstimate(flops=flops, bytes_accessed=1 << 20, transcendentals=0),
        )(*args)

    return run


def send(value, axis, shift):
    count = lax.axis_size(axis)
    return lax.ppermute(value, axis, [(i, (i + shift) % count) for i in range(count)])


def swap_core(value):
    return lax.ppermute(value, "gx", [(i, i ^ 1) for i in range(lax.axis_size("gx"))])


def local(density_level, support_mask, load_mask, load_vector):
    block = density_level.shape
    ints = [pltpu.VMEM(block, jnp.int32)] * 3
    low, high = call(
        prepare_kernel, [(5, 4, 8, 128)] * 2, ints + [(3,) + block, pltpu.SemaphoreType.DMA((4,))], hbm_in=True
    )(density_level, support_mask, load_mask, load_vector)
    up, down = send(high, "gy", 1), send(low, "gy", -1)
    own, first, last = call(join_y_kernel, [(5, 4, 32, 128), (5, 1, 32, 128), (5, 2, 32, 128)])(up, low, high, down)
    planes = [send(last, "gx", 2), send(own, "gx", 1), own, send(own, "gx", -1), send(first, "gx", -2)]
    first, last = call(pack_z_kernel, [(5, 32, 128)] * 2)(*planes)
    from_left, from_right = send(last, "gz", 1), send(first, "gz", -1)
    fine = (4, 2) + REG
    stat, load, dinv, w0, static, sums = call(
        first_kernel,
        [(2, NXE) + fine, (3, NXE) + fine, (NXE,) + fine, (3, 4) + fine, (5,) + REG, (8,) + REG],
        [(5, 2, 16, 128)] + work_buffers(4, 2),
        limit=8,
    )(*planes, from_left, from_right)
    w0, w1, w2, pack = call(
        second_kernel,
        [(3, NXE) + fine, (3, NXE) + fine, (3, 8) + fine, (14,) + REG],
        [(3, NXE) + fine, (3, NXE) + fine, (3, 8) + fine, (3, 3, 2, 16, 128)]
        + work_buffers(4, 2)
        + [pltpu.SemaphoreType.DMA((3,))],
        flops=1 << 26,
        limit=11,
        in_hbm=(0, 1, 2),
    )(stat, dinv, w0, load, static)
    sums = call(sum_kernel, [(32,) + REG])(lax.all_to_all(sums, "gy", 0, 0), pack)[0]
    tiles = [send(pack, "gy", 2), send(pack, "gy", 1), pack, send(pack, "gy", -1), send(pack, "gy", -2)]
    parts = lax.all_to_all(sums, ("gx", "gz"), 0, 0)
    mine, sums = call(combine_kernel, [(5, 5) + REG, REG])(parts, *tiles)
    res, pre = call(residual_kernel, [(3, 8) + fine, (3, 4) + fine], flops=1 << 22)(sums, load, dinv, w0, w1, w2)
    chips = [mine, send(mine, "gx", -2), send(mine, "gx", 4), send(mine, "gx", 2)]
    chips += [swap_core(val) for val in chips]
    chips, first, last = call(join_chips_kernel, [(5, 5, 8) + REG] + [(5, 5, 2) + REG] * 2)(*chips)
    from_left, from_right = send(last, "gz", 1), send(first, "gz", -1)
    five, three, one = (5, 2) + REG, (3, 2) + REG, (3, 1) + REG
    x1 = call(
        coarse_kernel,
        [(6, 3, 24, 128)],
        [(5, 8, 2, 40, 128), (10,) + five, (10,) + five, (8,) + five]
        + [(3, 8) + five, (3, 10) + five, (3, 10) + five, (3, 8) + five]
        + [(5, 4, 56, 128), (6,) + one, (6,) + one, (4,) + one]
        + [(3, 4) + one, (3, 6) + one, (3, 6) + one, (3, 4) + one]
        + [(2, 48, 128), (10,) + three, (10,) + three, (8,) + three]
        + [(3, 8) + three, (3, 8) + three, (432, 128), (432, 128)]
        + work_buffers(5, 2)
        + work_buffers(3, 1)
        + work_buffers(3, 2),
        limit=20,
    )(sums, chips, from_left, from_right)[0]
    return call(
        last_kernel,
        [(3, 4, 16, 128)],
        [(3, 12) + fine, (3, 8) + fine, (3, 8) + fine, (3, 8) + fine, (3, 4, 32, 128)] + work_buffers(4, 2),
        plain_out=True,
        limit=9,
    )(sums, stat, dinv, res, pre, x1)[0]


def solution(mesh):
    block = P("gx", "gy", "gz")
    return jax.shard_map(
        local,
        mesh=mesh,
        in_specs=(block, block, block, P(None, "gx", "gy", "gz")),
        out_specs=P(None, "gx", "gy", "gz"),
        check_vma=False,
    )
```
